32 devices in a mesh: seq: 8 (over z, core), mem: 4 (over y, x).
Axes of the slice: x: 2, y: 2, z: 4, core: 2. Of those that a mesh axis runs over, the one named last changes fastest.
Arguments:
- inputs: bfloat16 [2, 8, 4, 256, 1472], P(None, 'seq', 'mem'), may hold values from -6 to 6
- memory: bfloat16 [2, 8, 4, 1024, 1472], P(None, 'seq', None, 'mem'), may hold values from -6 to 6
- memory_lengths: int32 [2, 8, 4], P(None, 'seq'), may hold values from 1 to 1024, 2048 in all within a row
- keep_mask: int32 [2, 8, 4, 1024], P(None, 'seq', None, 'mem'), may hold values 0 or 1
- norm_self: bfloat16 [1472], replicated, may hold values from 0.099609375 to 1.8984375
- query_self: bfloat16 [1472, 384], P(None, 'seq'), may hold values from -0.0390625 to 0.0390625
- key_self: bfloat16 [1472, 384], P(None, 'seq'), may hold values from -0.15625 to 0.15625
- value_self: bfloat16 [1472, 384], P(None, 'seq'), may hold values from -0.15625 to 0.15625
- output_self: bfloat16 [384, 1472], P('seq'), may hold values from -1.25 to 1.25
- bias_table: bfloat16 [32, 6], replicated, may hold values from -4 to 4
- norm_cross: bfloat16 [1472], replicated, may hold values from 0.099609375 to 1.8984375
- query_cross: bfloat16 [1472, 384], P(None, 'seq'), may hold values from -0.0390625 to 0.0390625
- key_cross: bfloat16 [1472, 384], P(None, 'seq'), may hold values from -0.15625 to 0.15625
- value_cross: bfloat16 [1472, 384], P(None, 'seq'), may hold values from -0.15625 to 0.15625
- output_cross: bfloat16 [384, 1472], P('seq'), may hold values from -2.5 to 2.5
- norm_feed: bfloat16 [1472], replicated, may hold values from 0.099609375 to 1.8984375
- gate_feed: bfloat16 [1472, 3584], P(None, 'seq'), may hold values from -0.15625 to 0.15625
- linear_feed: bfloat16 [1472, 3584], P(None, 'seq'), may hold values from -0.15625 to 0.15625
- down_feed: bfloat16 [3584, 1472], P('seq'), may hold values from -0.09375 to 0.09375
- output_grad: bfloat16 [2, 8, 4, 256, 1472], P(None, 'seq', 'mem'), may hold values from -6 to 6
Outputs:
- result: float32 [2, 8, 4, 256, 1472], P(None, 'seq', 'mem')
- input_grad: float32 [2, 8, 4, 256, 1472], P(None, 'seq', 'mem')
- memory_grad: float32 [2, 8, 4, 1024, 1472], P(None, 'seq', None, 'mem')
- norm_self_grad: float32 [1472], replicated
- query_self_grad: float32 [1472, 384], P(None, 'seq')
- key_self_grad: float32 [1472, 384], P(None, 'seq')
- value_self_grad: float32 [1472, 384], P(None, 'seq')
- output_self_grad: float32 [384, 1472], P('seq')
- bias_table_grad: float32 [32, 6], replicated
- norm_cross_grad: float32 [1472], replicated
- query_cross_grad: float32 [1472, 384], P(None, 'seq')
- key_cross_grad: float32 [1472, 384], P(None, 'seq')
- value_cross_grad: float32 [1472, 384], P(None, 'seq')
- output_cross_grad: float32 [384, 1472], P('seq')
- norm_feed_grad: float32 [1472], replicated
- gate_feed_grad: float32 [1472, 3584], P(None, 'seq')
- linear_feed_grad: float32 [1472, 3584], P(None, 'seq')
- down_feed_grad: float32 [3584, 1472], P('seq')
The draws below stay inside these ranges and needn't reach their ends.
Inputs may be any that keep to these rules, and one draw needn't show every extreme that they name: `memory_lengths`: each encoder length of a group; in every group of 4 pairs the longest has exactly 1024 and their sum is 2048.
All inputs are finite; a program needn't handle non-finite values. No bound on the sum of `keep_mask` on one device may be relied on, other than what follows from the above.
Results may differ from the reference program's by a relative error of at most 0.03.
The reference program's roundings to bfloat16 on the way count: a program that leaves them out, or rounds other values in their place, can miss the bound.
Values may be sent and summed in bfloat16 or wider, within the bound.
No kernel may reach another device: no remote copies, remote signals or barrier semaphores. Data moves between devices by JAX's collectives and lax.ppermute only.
A program may use at most 320 MiB of HBM per device.

```python
import math
import jax
import jax.numpy as jnp
import numpy as np
from jax import lax

D = 1472
FF = 3584
H = 6
BUCKETS = 32
MICRO = 2
LT = 256
CAP = 1024
INNER = 384
GROUPS = 8
PAIRS = 4


def with_ends(values, own_key, least, top_value):
    index_at = [jax.random.randint(jax.random.fold_in(own_key, axis), (), 0, length) for axis, length in enumerate(values.shape)]
    main_axis = values.shape.index(max(values.shape))
    beside = index_at[:main_axis] + [(index_at[main_axis] + 1) % values.shape[main_axis]] + index_at[main_axis + 1:]
    return values.at[tuple(index_at)].set(least).at[tuple(beside)].set(top_value)


def block_levels(key, extent, shards, smallest, high):
    loudness = 1.0
    for position, shards_of in shards:
        heights = jax.random.uniform(jax.random.fold_in(jax.random.fold_in(key, 6), position), (shards_of,), jnp.float32, smallest / len(shards), high / len(shards))
        loudness = loudness * jnp.repeat(jnp.exp(heights), extent[position] // shards_of).reshape((-1,) + (1,) * (len(extent) - 1 - position))
    return loudness


def profile(amount, total, limit, slope):
    loads = [(1 << 20) // math.isqrt(grade ** slope) + 1 for grade in range(2, amount + 1)]
    spare, counts = total - limit - (amount - 1), [1] * (amount - 1)
    while spare > 0:
        free = [i for i in range(amount - 1) if counts[i] < limit]
        mass, left = sum([loads[i] for i in free]), spare
        for i in free:
            addition = min(limit - counts[i], max(1, left * loads[i] // mass), spare)
            counts[i] = counts[i] + addition
            spare = spare - addition
    return np.array([limit] + counts)


def ragged(stream_key, number_of, total, most, slope):
    if number_of == 2:
        one = jax.random.randint(stream_key, (), max(1, total - most), min(most, total - 1) + 1)
        return jnp.stack([one, total - one])
    sizes = jnp.asarray(profile(number_of, total, most, slope), jnp.int32)
    couples = (number_of - 1) // 2
    giver, sink = sizes[1:1 + 2 * couples:2], sizes[2:2 + 2 * couples:2]
    slack = jnp.minimum(giver - 1, most - sink)
    moved = jax.random.randint(jax.random.fold_in(stream_key, 1), (couples,), 0, 1 << 20) % (slack + 1)
    sizes = sizes.at[1:1 + 2 * couples:2].set(giver - moved).at[2:2 + 2 * couples:2].set(sink + moved)
    return sizes[jax.random.permutation(jax.random.fold_in(stream_key, 2), number_of)]


def normal_values(rng, dims, spread, limit, split=(), kind=jnp.bfloat16):
    array = spread * jax.random.normal(rng, dims, jnp.float32)
    if split:
        array = array * block_levels(rng, dims, split, -0.22, 0.18)
    return jnp.clip(array, -limit, limit).astype(kind)


def setup_inputs(seed: int = 0) -> dict:
    keys = jax.random.split(jax.random.key(seed), 21)
    return {
        "inputs": normal_values(keys[0], (MICRO, GROUPS, PAIRS, LT, D), 1.0, 6.0, ((1, 8), (2, 4))),
        "memory": normal_values(keys[1], (MICRO, GROUPS, PAIRS, CAP, D), 1.0, 6.0, ((1, 8), (3, 4))),
        "memory_lengths": jax.vmap(lambda own: ragged(own, PAIRS, PAIRS * CAP // 2, CAP, 2))(jax.random.split(keys[2], MICRO * GROUPS)).reshape((MICRO, GROUPS, PAIRS)).astype(jnp.int32),
        "keep_mask": with_ends((jax.random.randint(keys[3], (MICRO, GROUPS, PAIRS, CAP), 0, 4) < 3).astype(jnp.int32), jax.random.fold_in(keys[3], 1), 0, 1),
        "norm_self": jnp.clip(1.0 + 0.18 * jax.random.normal(keys[4], (D,), jnp.float32), 0.099609375, 1.8984375).astype(jnp.bfloat16),
        "query_self": normal_values(keys[5], (D, INNER), (16 * D) ** -0.5, 0.0390625, ((1, 8),)),
        "key_self": normal_values(keys[6], (D, INNER), D ** -0.5, 0.15625, ((1, 8),)),
        "value_self": normal_values(keys[7], (D, INNER), D ** -0.5, 0.15625, ((1, 8),)),
        "output_self": normal_values(keys[8], (INNER, D), (max(INNER // 16, 1)) ** -0.5, 1.25, ((0, 8),)),
        "bias_table": normal_values(keys[9], (BUCKETS, H), 1.0, 4.0),
        "norm_cross": jnp.clip(1.0 + 0.18 * jax.random.normal(keys[10], (D,), jnp.float32), 0.099609375, 1.8984375).astype(jnp.bfloat16),
        "query_cross": normal_values(keys[11], (D, INNER), (16 * D) ** -0.5, 0.0390625, ((1, 8),)),
        "key_cross": normal_values(keys[12], (D, INNER), D ** -0.5, 0.15625, ((1, 8),)),
        "value_cross": normal_values(keys[13], (D, INNER), D ** -0.5, 0.15625, ((1, 8),)),
        "output_cross": normal_values(keys[14], (INNER, D), (max(INNER // 64, 1)) ** -0.5, 2.5, ((0, 8),)),
        "norm_feed": jnp.clip(1.0 + 0.18 * jax.random.normal(keys[15], (D,), jnp.float32), 0.099609375, 1.8984375).astype(jnp.bfloat16),
        "gate_feed": normal_values(keys[16], (D, FF), D ** -0.5, 0.15625, ((1, 8),)),
        "linear_feed": normal_values(keys[17], (D, FF), D ** -0.5, 0.15625, ((1, 8),)),
        "down_feed": normal_values(keys[18], (FF, D), FF ** -0.5, 0.09375, ((0, 8),)),
        "output_grad": normal_values(keys[19], (MICRO, GROUPS, PAIRS, LT, D), 1.0, 6.0, ((1, 8), (2, 4))),
    }


norm_eps = 1e-06
masked_score = -1e+30
highest = lax.Precision.HIGHEST

@jax.custom_vjp
def low(v):
    return lax.optimization_barrier(v.astype(jnp.bfloat16)).astype(jnp.float32)

@jax.custom_vjp
def low_back(v):
    return v

def low_keep(v):
    return (low(v), None)

def low_pass(kept, grad):
    return (grad,)

def back_keep(v):
    return (v, None)

def back_low(kept, grad):
    return (low(grad),)
low.defvjp(low_keep, low_pass)
low_back.defvjp(back_keep, back_low)

def rounded_both(value):
    return low(low_back(value))

def bucket_edges():
    return [math.ceil(16 * 8 ** ((number - 16) / 16)) for number in range(17, 32)]

def position_buckets(length):
    row_index = jnp.arange(length, dtype=jnp.int32)
    offset = jnp.maximum(row_index[:, None] - row_index[None, :], 0)
    bucket = jnp.minimum(offset, 16)
    for threshold in bucket_edges():
        bucket = bucket + (offset >= threshold).astype(jnp.int32)
    return bucket

def rms_norm(value, gain):
    scale = lax.rsqrt(lax.optimization_barrier(jnp.mean(value * value, axis=-1, keepdims=True)) + norm_eps)
    return value * scale * gain

def product(left, right):
    return jnp.matmul(left, right, precision=highest)

def block_forward(params, tokens, source, lengths, keep):
    norm_self, query_self, key_self, value_self, output_self, bias_table, norm_cross, query_cross, key_cross, value_cross, output_cross, norm_feed, gate_feed, linear_feed, down_feed = params
    pair_count = tokens.shape[0]
    length = tokens.shape[1]
    slot_count = source.shape[1]
    head_count = bias_table.shape[1]
    normed = low(rms_norm(tokens, norm_self))
    query_low = rounded_both(product(normed, query_self)).reshape(pair_count, length, head_count, -1)
    keys_low = rounded_both(product(normed, key_self)).reshape(pair_count, length, head_count, -1)
    values_low = rounded_both(product(normed, value_self)).reshape(pair_count, length, head_count, -1)
    onehot = (position_buckets(length)[:, :, None] == jnp.arange(bias_table.shape[0], dtype=jnp.int32)[None, None, :]).astype(jnp.float32)
    position_bias = jnp.einsum('ijb,bh->hij', onehot, bias_table, precision=highest)
    row_index = jnp.arange(length, dtype=jnp.int32)
    causal = row_index[:, None] >= row_index[None, :]
    scores = jnp.einsum('pihd,pjhd->phij', query_low, keys_low, precision=highest) + position_bias[None]
    scores = low_back(jnp.where(causal[None, None], scores, masked_score))
    attend = low(jax.nn.softmax(scores, axis=-1))
    mixed = rounded_both(jnp.einsum('phij,pjhd->pihd', attend, values_low, precision=highest)).reshape(pair_count, length, -1)
    first_sum = tokens + low_back(product(mixed, output_self))
    normed_cross = low(rms_norm(first_sum, norm_cross))
    cross_query = rounded_both(product(normed_cross, query_cross)).reshape(pair_count, length, head_count, -1)
    cross_keys = rounded_both(product(source, key_cross)).reshape(pair_count, slot_count, head_count, -1)
    cross_values = rounded_both(product(source, value_cross)).reshape(pair_count, slot_count, head_count, -1)
    spots = jnp.arange(slot_count, dtype=jnp.int32)
    valid = (spots[None, :] < lengths[:, None]) & ((keep == 1) | (spots[None, :] == 0))
    cross_scores = jnp.einsum('pihd,pjhd->phij', cross_query, cross_keys, precision=highest)
    cross_scores = low_back(jnp.where(valid[:, None, None, :], cross_scores, masked_score))
    cross_attend = low(jax.nn.softmax(cross_scores, axis=-1))
    cross_mixed = rounded_both(jnp.einsum('phij,pjhd->pihd', cross_attend, cross_values, precision=highest)).reshape(pair_count, length, -1)
    second_sum = first_sum + low_back(product(cross_mixed, output_cross))
    normed_feed = low(rms_norm(second_sum, norm_feed))
    gate_act = low_back(product(normed_feed, gate_feed))
    linear = low_back(product(normed_feed, linear_feed))
    hidden = low(jax.nn.gelu(gate_act, approximate=True) * linear)
    return second_sum + low_back(product(hidden, down_feed))

def reference(inputs, memory, memory_lengths, keep_mask, norm_self, query_self, key_self, value_self, output_self, bias_table, norm_cross, query_cross, key_cross, value_cross, output_cross, norm_feed, gate_feed, linear_feed, down_feed, output_grad):
    params = (norm_self.astype(jnp.float32), query_self.astype(jnp.float32), key_self.astype(jnp.float32), value_self.astype(jnp.float32), output_self.astype(jnp.float32), bias_table.astype(jnp.float32), norm_cross.astype(jnp.float32), query_cross.astype(jnp.float32), key_cross.astype(jnp.float32), value_cross.astype(jnp.float32), output_cross.astype(jnp.float32), norm_feed.astype(jnp.float32), gate_feed.astype(jnp.float32), linear_feed.astype(jnp.float32), down_feed.astype(jnp.float32))
    block_count = MICRO * GROUPS
    tokens = inputs.astype(jnp.float32).reshape(block_count, PAIRS, LT, D)
    source = memory.astype(jnp.float32).reshape(block_count, PAIRS, CAP, D)
    lengths = memory_lengths.reshape(block_count, PAIRS)
    keeps = keep_mask.reshape(block_count, PAIRS, CAP)
    step_block = jax.checkpoint(block_forward)

    def forward(weights, token_blocks, source_blocks):

        def one_block(pieces):
            return step_block(weights, pieces[0], pieces[1], pieces[2], pieces[3])
        return lax.map(one_block, (token_blocks, source_blocks, lengths, keeps))
    result, pullback = jax.vjp(forward, params, tokens, source)
    weight_grads, token_grads, source_grads = pullback(output_grad.astype(jnp.float32).reshape(result.shape))
    return (result.reshape(MICRO, GROUPS, PAIRS, LT, D), token_grads.reshape(MICRO, GROUPS, PAIRS, LT, D), source_grads.reshape(MICRO, GROUPS, PAIRS, CAP, D), weight_grads[0], weight_grads[1], weight_grads[2], weight_grads[3], weight_grads[4], weight_grads[5], weight_grads[6], weight_grads[7], weight_grads[8], weight_grads[9], weight_grads[10], weight_grads[11], weight_grads[12], weight_grads[13], weight_grads[14])
```

```python
import functools
import math

import jax
import jax.numpy as jnp
from jax import lax
from jax.experimental import pallas as pl
from jax.experimental.pallas import tpu as pltpu
from jax.sharding import PartitionSpec as P

norm_eps = 1e-06
masked_score = -1e30
bf16 = jnp.bfloat16
f32 = jnp.float32


def bucket_edges():
    return [math.ceil(16 * 8 ** ((number - 16) / 16)) for number in range(17, 32)]


def position_buckets(length):
    row_index = jnp.arange(length, dtype=jnp.int32)
    offset = jnp.maximum(row_index[:, None] - row_index[None, :], 0)
    bucket = jnp.minimum(offset, 16)
    for threshold in bucket_edges():
        bucket = bucket + (offset >= threshold).astype(jnp.int32)
    return bucket


def matmul(left, right):
    return jnp.dot(left, right, preferred_element_type=f32)


def contract_rows(left, right):
    return lax.dot_general(left, right, (((0,), (0,)), ((), ())), preferred_element_type=f32)


def contract_cols(left, right):
    return lax.dot_general(left, right, (((1,), (1,)), ((), ())), preferred_element_type=f32)


def add_low(left, right):
    return (left.astype(f32) + right.astype(f32)).astype(bf16)


def to_core(value):
    count = lax.axis_size("seq")
    return lax.ppermute(value, "seq", [(i, i ^ 1) for i in range(count)])


def to_next(value):
    count = lax.axis_size("seq")
    return lax.ppermute(value, "seq", [(i, (i + 2) % count) for i in range(count)])


def to_mem(value, mask):
    count = lax.axis_size("mem")
    return lax.ppermute(value, "mem", [(i, i ^ mask) for i in range(count)])


def mem_bits():
    return [1 << b for b in range((lax.axis_size("mem") - 1).bit_length())]


def to_step(value, step):
    count = lax.axis_size("seq")
    return lax.ppermute(value, "seq", [(i, (i + 2 * step) % count) for i in range(count)])


def to_seq(value, mask):
    count = lax.axis_size("seq")
    return lax.ppermute(value, "seq", [(i, i ^ mask) for i in range(count)])


def after(value, *others):
    return lax.optimization_barrier((value, *others))[0]


def ring_gather(value):
    pieces = [value]
    for _ in range(lax.axis_size("seq") // 2 - 1):
        pieces.append(to_next(pieces[-1]))
    return pieces


def ring_sum(pieces):
    total = pieces[1]
    for piece in pieces[2:]:
        total = add_low(to_next(total), piece)
    return add_low(to_next(total), pieces[0])


def spread_gather(value, bits):
    held, order = value[None], [0]
    for bit in bits:
        held = jnp.concatenate([held, to_mem(held, bit)], axis=0)
        order = order + [k | bit for k in order]
    return [held[order.index(k)] for k in range(len(order))]


def fold(held, bits):
    order = list(range(held.shape[0]))
    for bit in bits:
        keep = [i for i, k in enumerate(order) if not k & bit]
        send = [order.index(order[i] | bit) for i in keep]
        moved = to_mem(jnp.stack([held[i] for i in send]), bit)
        held = jnp.stack([add_low(held[i], moved[n]) for n, i in enumerate(keep)])
        order = [order[i] for i in keep]
    return held[0]


def sum_low(pieces):
    total = pieces[0].astype(f32)
    for piece in pieces[1:]:
        total = total + piece.astype(f32)
    return total.astype(bf16)


def direct_fold(pieces):
    return sum_low([to_mem(p, k) if k else p for k, p in enumerate(pieces)])


def natural(pieces, mem_index):
    stacked = jnp.stack(pieces)
    return jnp.stack(
        [
            lax.dynamic_index_in_dim(stacked, mem_index ^ k, 0, keepdims=False)
            for k in range(len(pieces))
        ]
    )


def back_to_mem(value, mem_index):
    pieces = [to_mem(value, k) if k else value for k in range(lax.axis_size("mem"))]
    return natural(pieces, mem_index).astype(f32)


def assemble_kernel(spot, own, other, out):
    chips = own.shape[0]
    core, chip = spot[0], spot[1]
    for j in range(chips):
        at = lax.rem(chip - j + chips, chips) * 2
        out[0, at + core] = own[j, 0]
        out[0, at + 1 - core] = other[j, 0]


def assemble(spot, own, other):
    chips, mems, share, width = own.shape
    block = pl.BlockSpec((chips, 1, share, width), lambda q, spot: (0, spot[2 + q], 0, 0))
    return pl.pallas_call(
        assemble_kernel,
        grid_spec=pltpu.PrefetchScalarGridSpec(
            num_scalar_prefetch=1,
            grid=(mems,),
            in_specs=[block, block],
            out_specs=pl.BlockSpec((1, 2 * chips, share, width), lambda q, spot: (q, 0, 0, 0)),
        ),
        out_shape=jax.ShapeDtypeStruct((mems, 2 * chips, share, width), bf16),
        compiler_params=params(32),
        name="assemble",
    )(spot, own, other)

def params(limit_mb=56):
    return pltpu.CompilerParams(vmem_limit_bytes=limit_mb * 1024 * 1024)


def row_norm(value):
    return lax.rsqrt(jnp.mean(value * value, axis=-1, keepdims=True) + norm_eps)


def norm_back_rows(value, gain, upstream):
    scale = row_norm(value)
    weighted = upstream * gain
    mean_dot = jnp.mean(weighted * value, axis=-1, keepdims=True)
    gain_grad = jnp.sum(upstream * value * scale, axis=0, keepdims=True)
    return weighted * scale - value * (scale * scale * scale * mean_dot), gain_grad


def lane_head(length, depth):
    return lax.broadcasted_iota(jnp.int32, (length, 128), 1) // depth


def self_fwd_kernel(depth, length, tok, g1, qw, kw, vw, ow, bias, g2, cw, normed_o, q_o, k_o, v_o, mixed_o, first_o, nc_o, cq_o):
    x = tok[...].astype(f32)
    normed = (x * row_norm(x) * g1[...]).astype(bf16)
    normed_o[...] = normed
    q_o[...] = contract_cols(normed, qw[...]).astype(bf16)
    k_o[...] = contract_cols(normed, kw[...]).astype(bf16)
    v_o[...] = contract_cols(normed, vw[...]).astype(bf16)
    inner = qw.shape[0]
    groups, share = inner // 128, 128 // depth
    lanes = lane_head(length, depth)

    def body(step, carry):
        micro, group = step // groups, step % groups
        rows = pl.ds(pl.multiple_of(micro * length, length), length)
        cols = pl.ds(pl.multiple_of(group * 128, 128), 128)
        q, k, v = q_o[rows, cols], k_o[rows, cols], v_o[rows, cols]
        out = jnp.zeros((length, 128), f32)
        for a in range(share):
            s = contract_cols(jnp.where(lanes == a, q, 0), k) + bias[group * share + a]
            e = jnp.exp(s - jnp.max(s, axis=-1, keepdims=True))
            p = (e / jnp.sum(e, axis=-1, keepdims=True)).astype(bf16)
            out = jnp.where(lanes == a, matmul(p, v), out)
        mixed_o[rows, cols] = out.astype(bf16)
        return carry

    lax.fori_loop(0, x.shape[0] // length * groups, body, 0)
    first = tok[...].astype(f32) + matmul(mixed_o[...], ow[...])
    first_o[...] = first
    nc = (first * row_norm(first) * g2[...]).astype(bf16)
    nc_o[...] = nc
    cq_o[...] = contract_cols(nc, cw[...]).astype(bf16)


def self_fwd(depth, length, tok, g1, qw, kw, vw, ow, bias, g2, cw):
    rows, width = tok.shape
    inner = qw.shape[0]
    low, slim = jax.ShapeDtypeStruct((rows, width), bf16), jax.ShapeDtypeStruct((rows, inner), bf16)
    return pl.pallas_call(
        functools.partial(self_fwd_kernel, depth, length),
        out_shape=(low, slim, slim, slim, slim, jax.ShapeDtypeStruct((rows, width), f32), low, slim),
        compiler_params=params(),
        name="self_fwd",
    )(tok, g1, qw, kw, vw, ow, bias, g2, cw)


def cross_fwd_kernel(depth, length, parts, cq, mask, ow, first, g3, *refs):
    kvs, (mixed_o, second_o, nf_o) = refs[:parts], refs[parts:]
    inner = ow.shape[0]
    groups, share = inner // 128, 128 // depth
    lanes = lane_head(length, depth)

    def body(step, carry):
        micro, group = step // groups, step % groups
        rows = pl.ds(pl.multiple_of(micro * length, length), length)
        cols = pl.ds(pl.multiple_of(group * 128, 128), 128)
        vcols = pl.ds(pl.multiple_of(inner + group * 128, 128), 128)
        q = cq[rows, cols]
        k = jnp.concatenate([kv[micro, :, cols] for kv in kvs], axis=0)
        v = jnp.concatenate([kv[micro, :, vcols] for kv in kvs], axis=0)
        out = jnp.zeros((length, 128), f32)
        for a in range(share):
            s = contract_cols(jnp.where(lanes == a, q, 0), k)
            s = jnp.where(mask[micro] > 0, s, masked_score)
            e = jnp.exp(s - jnp.max(s, axis=-1, keepdims=True))
            p = (e / jnp.sum(e, axis=-1, keepdims=True)).astype(bf16)
            out = jnp.where(lanes == a, matmul(p, v), out)
        mixed_o[rows, cols] = out.astype(bf16)
        return carry

    lax.fori_loop(0, cq.shape[0] // length * groups, body, 0)
    second = first[...] + matmul(mixed_o[...], ow[...])
    second_o[...] = second
    nf_o[...] = (second * row_norm(second) * g3[...]).astype(bf16)


def cross_fwd(depth, length, cq, mask, ow, first, g3, kvs):
    rows, width = first.shape
    return pl.pallas_call(
        functools.partial(cross_fwd_kernel, depth, length, len(kvs)),
        out_shape=(
            jax.ShapeDtypeStruct(cq.shape, bf16),
            jax.ShapeDtypeStruct((rows, width), f32),
            jax.ShapeDtypeStruct((rows, width), bf16),
        ),
        compiler_params=params(),
        name="cross_fwd",
    )(cq, mask, ow, first, g3, *kvs)


def cross_bwd_kernel(depth, length, parts, og, nf_own, nf_more, second, g3, mixed, cq, mask, ow, first, g2, nc, qw, *refs):
    kvs = refs[:parts]
    kvg = refs[parts : 2 * parts]
    g3_o, dow_o, dqw_o, firstg_o, g2_o, mixg, dq = refs[2 * parts :]
    inner = ow.shape[0]
    slots = kvs[0].shape[1]
    groups, share = inner // 128, 128 // depth
    lanes = lane_head(length, depth)
    part, gain = norm_back_rows(second[...], g3[...], nf_own[...] + nf_more[...].astype(f32))
    g3_o[...] = gain
    second_grad = og[...].astype(f32) + part
    firstg_o[...] = second_grad
    low = second_grad.astype(bf16)
    dow_o[...] = contract_rows(mixed[...], low).astype(bf16)
    mixg[...] = contract_cols(low, ow[...]).astype(bf16)

    def body(step, carry):
        micro, group = step // groups, step % groups
        rows = pl.ds(pl.multiple_of(micro * length, length), length)
        cols = pl.ds(pl.multiple_of(group * 128, 128), 128)
        vcols = pl.ds(pl.multiple_of(inner + group * 128, 128), 128)
        q, o = cq[rows, cols], mixg[rows, cols]
        k = jnp.concatenate([kv[micro, :, cols] for kv in kvs], axis=0)
        v = jnp.concatenate([kv[micro, :, vcols] for kv in kvs], axis=0)
        q_grad = jnp.zeros((length, 128), f32)
        k_grad = jnp.zeros((parts * slots, 128), f32)
        v_grad = jnp.zeros((parts * slots, 128), f32)
        for a in range(share):
            qa, oa = jnp.where(lanes == a, q, 0), jnp.where(lanes == a, o, 0)
            s = contract_cols(qa, k)
            s = jnp.where(mask[micro] > 0, s, masked_score)
            e = jnp.exp(s - jnp.max(s, axis=-1, keepdims=True))
            p = e / jnp.sum(e, axis=-1, keepdims=True)
            v_grad += contract_rows(p.astype(bf16), oa)
            dp = contract_cols(oa, v)
            ds = (p * (dp - jnp.sum(p * dp, axis=-1, keepdims=True))).astype(bf16)
            q_grad = jnp.where(lanes == a, matmul(ds, k), q_grad)
            k_grad += contract_rows(ds, qa)
        dq[rows, cols] = q_grad.astype(bf16)
        for t in range(parts):
            kvg[t][micro, :, cols] = k_grad[t * slots : (t + 1) * slots].astype(bf16)
            kvg[t][micro, :, vcols] = v_grad[t * slots : (t + 1) * slots].astype(bf16)
        return carry

    lax.fori_loop(0, cq.shape[0] // length * groups, body, 0)
    dqw_o[...] = contract_rows(dq[...], nc[...]).astype(bf16)
    part, gain = norm_back_rows(first[...], g2[...], matmul(dq[...], qw[...]))
    g2_o[...] = gain
    firstg_o[...] = firstg_o[...] + part


def cross_bwd(depth, length, og, nf_own, nf_more, second, g3, mixed, cq, mask, ow, first, g2, nc, qw, kvs):
    rows, width = first.shape
    gain = jax.ShapeDtypeStruct((1, width), f32)
    weight = jax.ShapeDtypeStruct(ow.shape, bf16)
    out = pl.pallas_call(
        functools.partial(cross_bwd_kernel, depth, length, len(kvs)),
        out_shape=(
            *[jax.ShapeDtypeStruct(kv.shape, bf16) for kv in kvs],
            gain,
            weight,
            weight,
            jax.ShapeDtypeStruct((rows, width), f32),
            gain,
        ),
        scratch_shapes=[pltpu.VMEM(cq.shape, bf16), pltpu.VMEM(cq.shape, bf16)],
        compiler_params=params(),
        name="cross_bwd",
    )(og, nf_own, nf_more, second, g3, mixed, cq, mask, ow, first, g2, nc, qw, *kvs)
    return out[: len(kvs)], out[len(kvs) :]


def self_bwd_kernel(depth, length, first_grad, mixed, q, k, v, bias, ow, qw, kw, vw, normed, tok, g1, dow_o, dqw_o, dkw_o, dvw_o, ing_o, g1_o, ds_o, mixg, dq, dk, dv):
    inner = ow.shape[0]
    groups, share = inner // 128, 128 // depth
    lanes = lane_head(length, depth)
    low = first_grad[...].astype(bf16)
    dow_o[...] = contract_rows(mixed[...], low).astype(bf16)
    mixg[...] = contract_cols(low, ow[...]).astype(bf16)

    def body(group, carry):
        cols = pl.ds(pl.multiple_of(group * 128, 128), 128)
        total = [jnp.zeros((length, length), f32) for _ in range(share)]
        for micro in range(tok.shape[0] // length):
            rows = slice(micro * length, (micro + 1) * length)
            qs, ks, vs, o = q[rows, cols], k[rows, cols], v[rows, cols], mixg[rows, cols]
            q_grad = jnp.zeros((length, 128), f32)
            k_grad = jnp.zeros((length, 128), f32)
            v_grad = jnp.zeros((length, 128), f32)
            for a in range(share):
                qa, oa = jnp.where(lanes == a, qs, 0), jnp.where(lanes == a, o, 0)
                s = contract_cols(qa, ks) + bias[group * share + a]
                e = jnp.exp(s - jnp.max(s, axis=-1, keepdims=True))
                p = e / jnp.sum(e, axis=-1, keepdims=True)
                v_grad += contract_rows(p.astype(bf16), oa)
                dp = contract_cols(oa, vs)
                ds = (p * (dp - jnp.sum(p * dp, axis=-1, keepdims=True))).astype(bf16)
                total[a] = total[a] + ds.astype(f32)
                q_grad = jnp.where(lanes == a, matmul(ds, ks), q_grad)
                k_grad += contract_rows(ds, qa)
            dq[rows, cols] = q_grad.astype(bf16)
            dk[rows, cols] = k_grad.astype(bf16)
            dv[rows, cols] = v_grad.astype(bf16)
        for a in range(share):
            ds_o[group * share + a] = total[a]
        return carry

    lax.fori_loop(0, groups, body, 0)
    dqw_o[...] = contract_rows(dq[...], normed[...]).astype(bf16)
    dkw_o[...] = contract_rows(dk[...], normed[...]).astype(bf16)
    dvw_o[...] = contract_rows(dv[...], normed[...]).astype(bf16)
    up = matmul(dq[...], qw[...]) + matmul(dk[...], kw[...]) + matmul(dv[...], vw[...])
    part, gain = norm_back_rows(tok[...].astype(f32), g1[...], up)
    g1_o[...] = gain
    ing_o[...] = first_grad[...] + part


def self_bwd(depth, length, first_grad, mixed, q, k, v, bias, ow, qw, kw, vw, normed, tok, g1):
    rows, width = tok.shape
    weight = jax.ShapeDtypeStruct(ow.shape, bf16)
    return pl.pallas_call(
        functools.partial(self_bwd_kernel, depth, length),
        out_shape=(
            weight,
            weight,
            weight,
            weight,
            jax.ShapeDtypeStruct((rows, width), f32),
            jax.ShapeDtypeStruct((1, width), f32),
            jax.ShapeDtypeStruct(bias.shape, f32),
        ),
        scratch_shapes=[pltpu.VMEM(q.shape, bf16)] * 4,
        compiler_params=params(),
        name="self_bwd",
    )(first_grad, mixed, q, k, v, bias, ow, qw, kw, vw, normed, tok, g1)


def kv_fwd_kernel(place, source, kw, vw, out):
    inner = kw.shape[0]
    rows = source[0, 0]
    out[0, 0, :, :inner] = contract_cols(rows, kw[...]).astype(bf16)
    out[0, 0, :, inner:] = contract_cols(rows, vw[...]).astype(bf16)


def kv_fwd(place, memory, kw, vw):
    micros, pairs, slots, width = memory.shape
    inner = kw.shape[0]
    whole = pl.BlockSpec((inner, width), lambda s, m, place: (0, 0))
    return pl.pallas_call(
        kv_fwd_kernel,
        grid_spec=pltpu.PrefetchScalarGridSpec(
            num_scalar_prefetch=1,
            grid=(pairs, micros),
            in_specs=[
                pl.BlockSpec((1, 1, slots, width), lambda s, m, place: (m, place[s], 0, 0)),
                whole,
                whole,
            ],
            out_specs=pl.BlockSpec((1, 1, slots, 2 * inner), lambda s, m, place: (s, m, 0, 0)),
        ),
        out_shape=jax.ShapeDtypeStruct((pairs, micros, slots, 2 * inner), bf16),
        compiler_params=params(32),
        name="kv_fwd",
    )(place, memory, kw, vw)


def kv_bwd_kernel(place, source, kw, vw, kvg, out, dkw_o, dvw_o, acc):
    inner = kw.shape[0]
    step = pl.program_id(0) * pl.num_programs(1) + pl.program_id(1)
    grads = kvg[0, 0]

    @pl.when(step == 0)
    def clear():
        acc[...] = jnp.zeros_like(acc)

    out[0, 0] = matmul(grads[:, :inner], kw[...]) + matmul(grads[:, inner:], vw[...])
    acc[...] += contract_rows(grads, source[0, 0])

    @pl.when(step == pl.num_programs(0) * pl.num_programs(1) - 1)
    def write():
        dkw_o[...] = acc[:inner].astype(bf16)
        dvw_o[...] = acc[inner:].astype(bf16)


def kv_bwd(place, memory, kw, vw, kvg):
    micros, pairs, slots, width = memory.shape
    inner = kw.shape[0]
    whole = pl.BlockSpec((inner, width), lambda s, m, place: (0, 0))
    weight = jax.ShapeDtypeStruct((inner, width), bf16)
    block = pl.BlockSpec((1, 1, slots, width), lambda s, m, place: (m, place[s], 0, 0))
    return pl.pallas_call(
        kv_bwd_kernel,
        grid_spec=pltpu.PrefetchScalarGridSpec(
            num_scalar_prefetch=1,
            grid=(pairs, micros),
            in_specs=[
                block,
                whole,
                whole,
                pl.BlockSpec((1, 1, slots, 2 * inner), lambda s, m, place: (s, m, 0, 0)),
            ],
            out_specs=(block, whole, whole),
            scratch_shapes=[pltpu.VMEM((2 * inner, width), f32)],
        ),
        out_shape=(jax.ShapeDtypeStruct(memory.shape, f32), weight, weight),
        compiler_params=params(48),
        name="kv_bwd",
    )(place, memory, kw, vw, kvg)


gelu_c = math.sqrt(2 / math.pi)


def feed_kernel(nf_a, nf_b, og_a, og_b, gw, lw, dw, dgw_o, dlw_o, ddw_o, res_o, res_b, nfg_o, nfg_b, nf, og, res_t, nfg_t, sems):
    step = pl.program_id(0)
    rows = nf_a.shape[0]

    @pl.when(step == 0)
    def load():
        copies = [
            pltpu.make_async_copy(src, dst.at[pl.ds(at, rows)], sems.at[i])
            for i, (src, dst, at) in enumerate([(nf_a, nf, 0), (nf_b, nf, rows), (og_a, og, 0), (og_b, og, rows)])
        ]
        for copy in copies:
            copy.start()
        for copy in copies:
            copy.wait()

    x, up = nf[...], og[...]
    g = contract_cols(x, gw[...])
    lin = contract_cols(x, lw[...])
    hg = contract_cols(up, dw[...])
    t = jnp.tanh(gelu_c * (g + 0.044715 * (g * g * g)))
    act = 0.5 * g * (1.0 + t)
    slope = 0.5 * (1.0 + t) + 0.5 * g * (1.0 - t * t) * (gelu_c * (1.0 + 3 * 0.044715 * (g * g)))
    hidden = (act * lin).astype(bf16)
    gl = (hg * lin * slope).astype(bf16)
    ll = (hg * act).astype(bf16)
    ddw_o[...] = contract_rows(hidden, up).astype(bf16)
    dgw_o[...] = contract_rows(gl, x).astype(bf16)
    dlw_o[...] = contract_rows(ll, x).astype(bf16)
    res = matmul(hidden, dw[...])
    nfg = matmul(gl, gw[...]) + matmul(ll, lw[...])

    @pl.when(step == 0)
    def first():
        res_o[...] = res[:rows]
        res_t[...] = res[rows:]
        nfg_o[...] = nfg[:rows]
        nfg_t[...] = nfg[rows:]

    @pl.when(step > 0)
    def later():
        res_o[...] += res[:rows]
        res_t[...] += res[rows:]
        nfg_o[...] += nfg[:rows]
        nfg_t[...] += nfg[rows:]

    @pl.when(step == pl.num_programs(0) - 1)
    def last():
        res_b[...] = res_t[...].astype(bf16)
        nfg_b[...] = nfg_t[...].astype(bf16)


def feed_layer(nf_a, nf_b, og_a, og_b, gw, lw, dw, block):
    rows, width = nf_a.shape
    hidden = gw.shape[0]
    any_spec = pl.BlockSpec(memory_space=pl.ANY)
    tile = pl.BlockSpec((block, width), lambda i: (i, 0))
    whole = pl.BlockSpec((rows, width), lambda i: (0, 0))
    weight = jax.ShapeDtypeStruct((hidden, width), bf16)
    wide, low = jax.ShapeDtypeStruct((rows, width), f32), jax.ShapeDtypeStruct((rows, width), bf16)
    return pl.pallas_call(
        feed_kernel,
        grid=(hidden // block,),
        in_specs=[any_spec] * 4 + [tile] * 3,
        out_specs=(tile, tile, tile, whole, whole, whole, whole),
        out_shape=(weight, weight, weight, wide, low, wide, low),
        scratch_shapes=[
            pltpu.VMEM((2 * rows, width), bf16),
            pltpu.VMEM((2 * rows, width), bf16),
            pltpu.VMEM((rows, width), f32),
            pltpu.VMEM((rows, width), f32),
            pltpu.SemaphoreType.DMA((4,)),
        ],
        compiler_params=params(60),
        name="feed",
    )(nf_a, nf_b, og_a, og_b, gw, lw, dw)


def per_device(
    inputs,
    memory,
    memory_lengths,
    keep_mask,
    norm_self,
    query_self,
    key_self,
    value_self,
    output_self,
    bias_table,
    norm_cross,
    query_cross,
    key_cross,
    value_cross,
    output_cross,
    norm_feed,
    gate_feed,
    linear_feed,
    down_feed,
    output_grad,
):
    micros = inputs.shape[0]
    length = inputs.shape[3]
    width = inputs.shape[4]
    pairs = memory.shape[2]
    slots = memory.shape[3]
    heads = bias_table.shape[1]
    buckets = bias_table.shape[0]
    seqs = lax.axis_size("seq")
    mems = lax.axis_size("mem")
    chips = seqs // 2
    slim = query_self.shape[1]
    inner = slim * seqs
    depth = inner // heads
    feed = gate_feed.shape[1]
    part = feed // mems
    rows = micros * length
    seq_index = lax.axis_index("seq")
    core = seq_index % 2
    chip = seq_index // 2
    mem_index = lax.axis_index("mem")
    gain_self = norm_self.astype(f32)
    gain_cross = norm_cross.astype(f32)
    gain_feed = norm_feed.astype(f32)


    bits = mem_bits()
    spot = jnp.stack([core, chip] + [mem_index ^ q for q in range(mems)]).astype(jnp.int32)

    def quarters(shard):
        shard = shard.reshape(mems, shard.shape[0] // mems, width)
        return jnp.stack(
            [lax.dynamic_index_in_dim(shard, mem_index ^ k, 0, keepdims=False) for k in range(mems)]
        )

    first_pack = quarters(jnp.concatenate([key_cross.T, value_cross.T, query_self.T, key_self.T], axis=0))
    second_pack = jnp.concatenate([value_self.T, output_self, query_cross.T, output_cross], axis=0)
    ring = ring_gather(first_pack[0])
    others = jnp.stack(ring[1:])
    spread = jnp.stack([to_mem(others, k) if k else others for k in range(mems)], axis=1)
    held = jnp.concatenate([first_pack[None], spread], axis=0)
    first_mats = assemble(spot, held, to_core(held))
    first_mats = (
        first_mats.reshape(4, mems // 4, seqs, -1, width).transpose(0, 2, 1, 3, 4).reshape(4, inner, width)
    )
    second_mats = lax.all_gather(second_pack, "seq", axis=0).reshape(seqs, 4, slim, width)
    kc_full, vc_full, qs_full, ks_full = [first_mats[i] for i in range(4)]
    vs_full, os_full, qc_full, oc_full = [second_mats[:, i].reshape(inner, width) for i in range(4)]

    gate_own, linear_own, down_own = quarters(gate_feed.T), quarters(linear_feed.T), quarters(down_feed)
    start = after(jnp.stack([gate_own[0], linear_own[0]]), ring[-1])
    both_ring = jnp.stack(ring_gather(start)[1:])
    gate_spread = spread_gather(both_ring[:, 0], bits)
    linear_spread = spread_gather(both_ring[:, 1], bits[::-1])
    down_ring = ring_gather(after(down_own, both_ring))
    gate_full = jnp.stack([jnp.concatenate([gate_own[k][None], gate_spread[k]]) for k in range(mems)])
    linear_full = jnp.stack([jnp.concatenate([linear_own[k][None], linear_spread[k]]) for k in range(mems)])
    down_full = jnp.stack(down_ring, axis=1)
    hidden_all = mems * chips * part
    gate_full = gate_full.reshape(hidden_all, width)
    linear_full = linear_full.reshape(hidden_all, width)
    down_full = down_full.reshape(hidden_all, width)

    onehot = (
        position_buckets(length).reshape(length * length, 1)
        == jnp.arange(buckets, dtype=jnp.int32)[None, :]
    ).astype(bf16)
    position_bias = (
        jnp.dot(onehot, bias_table, preferred_element_type=f32)
        .reshape(length, length, heads)
        .transpose(2, 0, 1)
    )
    row_index = jnp.arange(length, dtype=jnp.int32)
    causal = row_index[:, None] >= row_index[None, :]
    position_bias = jnp.where(causal[None], position_bias, masked_score)
    tokens = inputs.reshape(rows, width)
    og_low = output_grad.reshape(rows, width)
    og_other = to_core(og_low)
    source = memory.reshape(micros, pairs, slots, width)
    gain_self, gain_cross, gain_feed = [g.reshape(1, width) for g in (gain_self, gain_cross, gain_feed)]
    keep_all = lax.all_gather(keep_mask[:, 0], "mem", axis=0)
    keep_own = lax.dynamic_index_in_dim(keep_all, mem_index, 2, keepdims=False)
    keep_own = jnp.stack(
        [lax.dynamic_index_in_dim(keep_own, mem_index ^ s, 0, keepdims=False) for s in range(mems)], 1
    )
    spots = jnp.stack(
        [(mem_index ^ s) * slots + jnp.arange(slots, dtype=jnp.int32) for s in range(mems)], 0
    )
    len_own = lax.dynamic_index_in_dim(memory_lengths[:, 0], mem_index, 1, keepdims=False)
    valid = (spots[None] < len_own[:, None, None]) & ((keep_own == 1) | (spots[None] == 0))
    valid = valid.reshape(micros, 1, mems * slots).astype(f32)
    place = spot[2:]

    kv_local = kv_fwd(place, source, kc_full, vc_full)
    kvs = [to_mem(kv_local[s], s) if s else kv_local[s] for s in range(mems)]
    normed, q, k, v, mixed, first_sum, normed_cross, cq = self_fwd(
        depth, length, tokens, gain_self, qs_full, ks_full, vs_full, os_full, position_bias, gain_cross, qc_full
    )
    cmixed, second_sum, normed_feed = cross_fwd(depth, length, cq, valid, oc_full, first_sum, gain_feed, kvs)
    nf_other = to_core(normed_feed)
    block = 256 if hidden_all % 256 == 0 else part
    grad_gate, grad_linear, grad_down, res_own, res_send, nfg_own, nfg_send = feed_layer(
        normed_feed, nf_other, og_low, og_other, gate_full, linear_full, down_full, block
    )
    nfg_more = to_core(nfg_send)
    result = second_sum + res_own + to_core(res_send).astype(f32)

    split = (mems, chips, part, width)
    gate_sum = fold(grad_gate.reshape(split), bits[::-1])
    linear_sum = fold(grad_linear.reshape(split), bits)
    both_sum = ring_sum([jnp.stack([gate_sum[j], linear_sum[j]]) for j in range(chips)])
    grad_down = grad_down.reshape(split)
    down_sum = ring_sum([grad_down[:, j] for j in range(chips)])
    down_sum = direct_fold([down_sum[s] for s in range(mems)])
    feed_out = back_to_mem(jnp.concatenate([both_sum, down_sum[None]]), mem_index)
    gate_out, linear_out, down_out = [feed_out[:, i].reshape(feed, width) for i in range(3)]

    kvg, (grad_gain_feed, grad_co, grad_cq, first_grad, grad_gain_cross) = cross_bwd(
        depth, length, og_low, nfg_own, nfg_more, second_sum, gain_feed, cmixed, cq, valid, oc_full,
        first_sum, gain_cross, normed_cross, qc_full, kvs,
    )
    kvg = jnp.stack([to_mem(kvg[s], s) if s else kvg[s] for s in range(mems)])
    memory_grad, grad_kc, grad_vc = kv_bwd(place, source, kc_full, vc_full, kvg)
    grad_os, grad_qs, grad_ks, grad_vs, input_grad, grad_gain_self, score_sum = self_bwd(
        depth, length, first_grad, mixed, q, k, v, position_bias, os_full, qs_full, ks_full, vs_full,
        normed, tokens, gain_self,
    )

    cross_stack = jnp.stack([g.reshape(seqs, slim, width) for g in (grad_kc, grad_vc, grad_cq, grad_co)], axis=1)
    cross_sum = lax.psum_scatter(cross_stack.reshape(seqs, 4 * slim, width), "seq", scatter_dimension=0)
    cross_sum = direct_fold([cross_sum] * mems).astype(f32).reshape(4, slim, width)

    self_stack = jnp.stack(
        [g.reshape(chips, 2, slim, width) for g in (grad_qs, grad_ks, grad_vs, grad_os)], axis=2
    )
    kept = lax.dynamic_index_in_dim(self_stack, core, 1, keepdims=False)
    sent = lax.dynamic_index_in_dim(self_stack, 1 - core, 1, keepdims=False)
    total = add_low(kept, to_core(sent)).reshape(chips, mems, 4 * slim // mems, width)
    total = direct_fold(
        [lax.dynamic_index_in_dim(total, mem_index ^ s, 1, keepdims=False) for s in range(mems)]
    )
    pieces = [
        lax.dynamic_index_in_dim(total, (chip + j) % chips, 0, keepdims=False) for j in range(chips)
    ]
    total = sum_low([to_step(p, j) if j else p for j, p in enumerate(pieces)])
    self_sum = back_to_mem(total, mem_index).reshape(4, slim, width)

    grad_table = lax.dot_general(
        onehot.astype(f32),
        score_sum.reshape(heads, length * length),
        (((0,), (1,)), ((), ())),
        preferred_element_type=f32,
    )
    table_row = jnp.pad(grad_table.reshape(1, buckets * heads), ((0, 0), (0, width - buckets * heads)))
    small = jnp.concatenate([grad_gain_self, grad_gain_cross, grad_gain_feed, table_row], axis=0)
    for bit in bits:
        small = small + to_mem(small, bit)
    for bit in [1 << b for b in range((seqs - 1).bit_length())]:
        small = small + to_seq(small, bit)
    return (
        result.reshape(inputs.shape),
        input_grad.reshape(inputs.shape),
        memory_grad.reshape(memory.shape),
        small[0],
        self_sum[0].T,
        self_sum[1].T,
        self_sum[2].T,
        self_sum[3],
        small[3, : buckets * heads].reshape(buckets, heads),
        small[1],
        cross_sum[2].T,
        cross_sum[0].T,
        cross_sum[1].T,
        cross_sum[3],
        small[2],
        gate_out.T,
        linear_out.T,
        down_out,
    )


def solution(mesh):
    tokens_at = P(None, "seq", "mem", None, None)
    memory_at = P(None, "seq", None, "mem", None)
    columns, row_cut = P(None, "seq"), P("seq", None)
    return jax.shard_map(
        per_device,
        mesh=mesh,
        in_specs=(
            tokens_at,
            memory_at,
            P(None, "seq", None),
            P(None, "seq", None, "mem"),
            P(),
            columns,
            columns,
            columns,
            row_cut,
            P(),
            P(),
            columns,
            columns,
            columns,
            row_cut,
            P(),
            columns,
            columns,
            row_cut,
            tokens_at,
        ),
        out_specs=(
            tokens_at,
            tokens_at,
            memory_at,
            P(),
            columns,
            columns,
            columns,
            row_cut,
            P(),
            P(),
            columns,
            columns,
            columns,
            row_cut,
            P(),
            columns,
            columns,
            row_cut,
        ),
        check_vma=False,
    )
```

```python
import functools
import math

import jax
import jax.numpy as jnp
from jax import lax
from jax.experimental import pallas as pl
from jax.experimental.pallas import tpu as pltpu
from jax.sharding import PartitionSpec as P

norm_eps = 1e-06
masked_score = -1e30
bf16 = jnp.bfloat16
f32 = jnp.float32


def bucket_edges():
    return [math.ceil(16 * 8 ** ((number - 16) / 16)) for number in range(17, 32)]


def position_buckets(length):
    row_index = jnp.arange(length, dtype=jnp.int32)
    offset = jnp.maximum(row_index[:, None] - row_index[None, :], 0)
    bucket = jnp.minimum(offset, 16)
    for threshold in bucket_edges():
        bucket = bucket + (offset >= threshold).astype(jnp.int32)
    return bucket


def matmul(left, right):
    return jnp.dot(left, right, preferred_element_type=f32)


def contract_rows(left, right):
    return lax.dot_general(left, right, (((0,), (0,)), ((), ())), preferred_element_type=f32)


def contract_cols(left, right):
    return lax.dot_general(left, right, (((1,), (1,)), ((), ())), preferred_element_type=f32)


def add_low(left, right):
    return (left.astype(f32) + right.astype(f32)).astype(bf16)


def to_core(value):
    count = lax.axis_size("seq")
    return lax.ppermute(value, "seq", [(i, i ^ 1) for i in range(count)])


def rows_to_core(value):
    return to_core(value.reshape(-1, 64, value.shape[-1])).reshape(value.shape)


def to_next(value):
    count = lax.axis_size("seq")
    return lax.ppermute(value, "seq", [(i, (i + 2) % count) for i in range(count)])


def to_mem(value, mask):
    count = lax.axis_size("mem")
    return lax.ppermute(value, "mem", [(i, i ^ mask) for i in range(count)])


def mem_bits():
    return [1 << b for b in range((lax.axis_size("mem") - 1).bit_length())]


def to_step(value, step):
    count = lax.axis_size("seq")
    return lax.ppermute(value, "seq", [(i, (i + 2 * step) % count) for i in range(count)])


def to_seq(value, mask):
    count = lax.axis_size("seq")
    return lax.ppermute(value, "seq", [(i, i ^ mask) for i in range(count)])


def after(value, *others):
    return lax.optimization_barrier((value, *others))[0]


def ring_gather(value):
    pieces = [value]
    for _ in range(lax.axis_size("seq") // 2 - 1):
        pieces.append(to_next(pieces[-1]))
    return pieces


def ring_sum(pieces):
    total = pieces[1]
    for piece in pieces[2:]:
        total = add_low(to_next(total), piece)
    return add_low(to_next(total), pieces[0])


def spread_gather(value, bits):
    held, order = value[None], [0]
    for bit in bits:
        held = jnp.concatenate([held, to_mem(held, bit)], axis=0)
        order = order + [k | bit for k in order]
    return [held[order.index(k)] for k in range(len(order))]


def fold(held, bits):
    order = list(range(held.shape[0]))
    for bit in bits:
        keep = [i for i, k in enumerate(order) if not k & bit]
        send = [order.index(order[i] | bit) for i in keep]
        moved = to_mem(jnp.stack([held[i] for i in send]), bit)
        held = jnp.stack([add_low(held[i], moved[n]) for n, i in enumerate(keep)])
        order = [order[i] for i in keep]
    return held[0]


def sum_low(pieces):
    total = pieces[0].astype(f32)
    for piece in pieces[1:]:
        total = total + piece.astype(f32)
    return total.astype(bf16)


def direct_fold(pieces):
    return sum_low([to_mem(p, k) if k else p for k, p in enumerate(pieces)])


def natural(pieces, mem_index):
    stacked = jnp.stack(pieces)
    return jnp.stack(
        [
            lax.dynamic_index_in_dim(stacked, mem_index ^ k, 0, keepdims=False)
            for k in range(len(pieces))
        ]
    )


def back_to_mem(value, mem_index):
    pieces = [to_mem(value, k) if k else value for k in range(lax.axis_size("mem"))]
    return natural(pieces, mem_index).astype(f32)


def assemble_kernel(spot, own, other, out):
    chips = own.shape[0]
    core, chip = spot[0], spot[1]
    for j in range(chips):
        at = lax.rem(chip - j + chips, chips) * 2
        out[0, at + core] = own[j, 0]
        out[0, at + 1 - core] = other[j, 0]


def assemble(spot, own, other):
    chips, mems, share, width = own.shape
    block = pl.BlockSpec((chips, 1, share, width), lambda q, spot: (0, spot[2 + q], 0, 0))
    return pl.pallas_call(
        assemble_kernel,
        grid_spec=pltpu.PrefetchScalarGridSpec(
            num_scalar_prefetch=1,
            grid=(mems,),
            in_specs=[block, block],
            out_specs=pl.BlockSpec((1, 2 * chips, share, width), lambda q, spot: (q, 0, 0, 0)),
        ),
        out_shape=jax.ShapeDtypeStruct((mems, 2 * chips, share, width), bf16),
        compiler_params=params(32),
        cost_estimate=cost(3),
        name="assemble",
    )(spot, own, other)

def params(limit_mb=56):
    return pltpu.CompilerParams(vmem_limit_bytes=limit_mb * 1024 * 1024)


def cost(micro_seconds):
    return pl.CostEstimate(
        flops=micro_seconds * 10**9, bytes_accessed=micro_seconds * 3 * 10**6, transcendentals=0
    )


def row_norm(value):
    return lax.rsqrt(jnp.mean(value * value, axis=-1, keepdims=True) + norm_eps)


def norm_back_rows(value, gain, upstream):
    scale = row_norm(value)
    weighted = upstream * gain
    mean_dot = jnp.mean(weighted * value, axis=-1, keepdims=True)
    gain_grad = jnp.sum(upstream * value * scale, axis=0, keepdims=True)
    return weighted * scale - value * (scale * scale * scale * mean_dot), gain_grad


def lane_head(length, depth):
    return lax.broadcasted_iota(jnp.int32, (length, 128), 1) // depth


def self_fwd_kernel(depth, length, tok, g1, qw, kw, vw, ow, bias, g2, cw, normed_o, q_o, k_o, v_o, mixed_o, first_o, nc_o, cq_o):
    x = tok[...].astype(f32)
    normed = (x * row_norm(x) * g1[...]).astype(bf16)
    normed_o[...] = normed
    q_o[...] = contract_cols(normed, qw[...]).astype(bf16)
    k_o[...] = contract_cols(normed, kw[...]).astype(bf16)
    v_o[...] = contract_cols(normed, vw[...]).astype(bf16)
    inner = qw.shape[0]
    groups, share = inner // 128, 128 // depth
    lanes = lane_head(length, depth)

    def body(step, carry):
        micro, group = step // groups, step % groups
        rows = pl.ds(pl.multiple_of(micro * length, length), length)
        cols = pl.ds(pl.multiple_of(group * 128, 128), 128)
        q, k, v = q_o[rows, cols], k_o[rows, cols], v_o[rows, cols]
        out = jnp.zeros((length, 128), f32)
        for a in range(share):
            s = contract_cols(jnp.where(lanes == a, q, 0), k) + bias[group * share + a]
            e = jnp.exp(s - jnp.max(s, axis=-1, keepdims=True))
            p = (e / jnp.sum(e, axis=-1, keepdims=True)).astype(bf16)
            out = jnp.where(lanes == a, matmul(p, v), out)
        mixed_o[rows, cols] = out.astype(bf16)
        return carry

    lax.fori_loop(0, x.shape[0] // length * groups, body, 0)
    first = tok[...].astype(f32) + matmul(mixed_o[...], ow[...])
    first_o[...] = first
    nc = (first * row_norm(first) * g2[...]).astype(bf16)
    nc_o[...] = nc
    cq_o[...] = contract_cols(nc, cw[...]).astype(bf16)


def self_fwd(depth, length, tok, g1, qw, kw, vw, ow, bias, g2, cw):
    rows, width = tok.shape
    inner = qw.shape[0]
    low, slim = jax.ShapeDtypeStruct((rows, width), bf16), jax.ShapeDtypeStruct((rows, inner), bf16)
    return pl.pallas_call(
        functools.partial(self_fwd_kernel, depth, length),
        out_shape=(low, slim, slim, slim, slim, jax.ShapeDtypeStruct((rows, width), f32), low, slim),
        compiler_params=params(),
        cost_estimate=cost(16),
        name="self_fwd",
    )(tok, g1, qw, kw, vw, ow, bias, g2, cw)


def cross_fwd_kernel(depth, length, parts, cq, mask, ow, first, g3, *refs):
    kvs, (mixed_o, second_o, nf_o) = refs[:parts], refs[parts:]
    inner = ow.shape[0]
    groups, share = inner // 128, 128 // depth
    lanes = lane_head(length, depth)

    def body(step, carry):
        micro, group = step // groups, step % groups
        rows = pl.ds(pl.multiple_of(micro * length, length), length)
        cols = pl.ds(pl.multiple_of(group * 128, 128), 128)
        vcols = pl.ds(pl.multiple_of(inner + group * 128, 128), 128)
        q = cq[rows, cols]
        k = jnp.concatenate([kv[micro, :, cols] for kv in kvs], axis=0)
        v = jnp.concatenate([kv[micro, :, vcols] for kv in kvs], axis=0)
        out = jnp.zeros((length, 128), f32)
        for a in range(share):
            s = contract_cols(jnp.where(lanes == a, q, 0), k)
            s = jnp.where(mask[micro] > 0, s, masked_score)
            e = jnp.exp(s - jnp.max(s, axis=-1, keepdims=True))
            p = (e / jnp.sum(e, axis=-1, keepdims=True)).astype(bf16)
            out = jnp.where(lanes == a, matmul(p, v), out)
        mixed_o[rows, cols] = out.astype(bf16)
        return carry

    lax.fori_loop(0, cq.shape[0] // length * groups, body, 0)
    second = first[...] + matmul(mixed_o[...], ow[...])
    second_o[...] = second
    nf_o[...] = (second * row_norm(second) * g3[...]).astype(bf16)


def cross_fwd(depth, length, cq, mask, ow, first, g3, kvs):
    rows, width = first.shape
    return pl.pallas_call(
        functools.partial(cross_fwd_kernel, depth, length, len(kvs)),
        out_shape=(
            jax.ShapeDtypeStruct(cq.shape, bf16),
            jax.ShapeDtypeStruct((rows, width), f32),
            jax.ShapeDtypeStruct((rows, width), bf16),
        ),
        compiler_params=params(),
        cost_estimate=cost(15),
        name="cross_fwd",
    )(cq, mask, ow, first, g3, *kvs)


def cross_bwd_kernel(depth, length, parts, og, nf_own, nf_more, second, g3, mixed, cq, mask, ow, first, g2, nc, qw, *refs):
    kvs = refs[:parts]
    kvg = refs[parts : 2 * parts]
    g3_o, dow_o, dqw_o, firstg_o, g2_o, mixg, dq = refs[2 * parts :]
    inner = ow.shape[0]
    slots = kvs[0].shape[1]
    groups, share = inner // 128, 128 // depth
    lanes = lane_head(length, depth)
    part, gain = norm_back_rows(second[...], g3[...], nf_own[...] + nf_more[...].astype(f32))
    g3_o[...] = gain
    second_grad = og[...].astype(f32) + part
    firstg_o[...] = second_grad
    low = second_grad.astype(bf16)
    dow_o[...] = contract_rows(mixed[...], low).astype(bf16)
    mixg[...] = contract_cols(low, ow[...]).astype(bf16)

    def body(step, carry):
        micro, group = step // groups, step % groups
        rows = pl.ds(pl.multiple_of(micro * length, length), length)
        cols = pl.ds(pl.multiple_of(group * 128, 128), 128)
        vcols = pl.ds(pl.multiple_of(inner + group * 128, 128), 128)
        q, o = cq[rows, cols], mixg[rows, cols]
        k = jnp.concatenate([kv[micro, :, cols] for kv in kvs], axis=0)
        v = jnp.concatenate([kv[micro, :, vcols] for kv in kvs], axis=0)
        q_grad = jnp.zeros((length, 128), f32)
        k_grad = jnp.zeros((parts * slots, 128), f32)
        v_grad = jnp.zeros((parts * slots, 128), f32)
        for a in range(share):
            qa, oa = jnp.where(lanes == a, q, 0), jnp.where(lanes == a, o, 0)
            s = contract_cols(qa, k)
            s = jnp.where(mask[micro] > 0, s, masked_score)
            e = jnp.exp(s - jnp.max(s, axis=-1, keepdims=True))
            p = e / jnp.sum(e, axis=-1, keepdims=True)
            v_grad += contract_rows(p.astype(bf16), oa)
            dp = contract_cols(oa, v)
            ds = (p * (dp - jnp.sum(p * dp, axis=-1, keepdims=True))).astype(bf16)
            q_grad = jnp.where(lanes == a, matmul(ds, k), q_grad)
            k_grad += contract_rows(ds, qa)
        dq[rows, cols] = q_grad.astype(bf16)
        for t in range(parts):
            kvg[t][micro, :, cols] = k_grad[t * slots : (t + 1) * slots].astype(bf16)
            kvg[t][micro, :, vcols] = v_grad[t * slots : (t + 1) * slots].astype(bf16)
        return carry

    lax.fori_loop(0, cq.shape[0] // length * groups, body, 0)
    dqw_o[...] = contract_rows(dq[...], nc[...]).astype(bf16)
    part, gain = norm_back_rows(first[...], g2[...], matmul(dq[...], qw[...]))
    g2_o[...] = gain
    firstg_o[...] = firstg_o[...] + part


def cross_bwd(depth, length, og, nf_own, nf_more, second, g3, mixed, cq, mask, ow, first, g2, nc, qw, kvs):
    rows, width = first.shape
    gain = jax.ShapeDtypeStruct((1, width), f32)
    weight = jax.ShapeDtypeStruct(ow.shape, bf16)
    out = pl.pallas_call(
        functools.partial(cross_bwd_kernel, depth, length, len(kvs)),
        out_shape=(
            *[jax.ShapeDtypeStruct(kv.shape, bf16) for kv in kvs],
            gain,
            weight,
            weight,
            jax.ShapeDtypeStruct((rows, width), f32),
            gain,
        ),
        scratch_shapes=[pltpu.VMEM(cq.shape, bf16), pltpu.VMEM(cq.shape, bf16)],
        compiler_params=params(),
        cost_estimate=cost(31),
        name="cross_bwd",
    )(og, nf_own, nf_more, second, g3, mixed, cq, mask, ow, first, g2, nc, qw, *kvs)
    return out[: len(kvs)], out[len(kvs) :]


def self_bwd_kernel(depth, length, first_grad, mixed, q, k, v, bias, ow, qw, kw, vw, normed, tok, g1, dow_o, dqw_o, dkw_o, dvw_o, ing_o, g1_o, ds_o, mixg, dq, dk, dv):
    inner = ow.shape[0]
    groups, share = inner // 128, 128 // depth
    lanes = lane_head(length, depth)
    low = first_grad[...].astype(bf16)
    dow_o[...] = contract_rows(mixed[...], low).astype(bf16)
    mixg[...] = contract_cols(low, ow[...]).astype(bf16)

    def body(group, carry):
        cols = pl.ds(pl.multiple_of(group * 128, 128), 128)
        total = [jnp.zeros((length, length), f32) for _ in range(share)]
        for micro in range(tok.shape[0] // length):
            rows = slice(micro * length, (micro + 1) * length)
            qs, ks, vs, o = q[rows, cols], k[rows, cols], v[rows, cols], mixg[rows, cols]
            q_grad = jnp.zeros((length, 128), f32)
            k_grad = jnp.zeros((length, 128), f32)
            v_grad = jnp.zeros((length, 128), f32)
            for a in range(share):
                qa, oa = jnp.where(lanes == a, qs, 0), jnp.where(lanes == a, o, 0)
                s = contract_cols(qa, ks) + bias[group * share + a]
                e = jnp.exp(s - jnp.max(s, axis=-1, keepdims=True))
                p = e / jnp.sum(e, axis=-1, keepdims=True)
                v_grad += contract_rows(p.astype(bf16), oa)
                dp = contract_cols(oa, vs)
                ds = (p * (dp - jnp.sum(p * dp, axis=-1, keepdims=True))).astype(bf16)
                total[a] = total[a] + ds.astype(f32)
                q_grad = jnp.where(lanes == a, matmul(ds, ks), q_grad)
                k_grad += contract_rows(ds, qa)
            dq[rows, cols] = q_grad.astype(bf16)
            dk[rows, cols] = k_grad.astype(bf16)
            dv[rows, cols] = v_grad.astype(bf16)
        for a in range(share):
            ds_o[group * share + a] = total[a]
        return carry

    lax.fori_loop(0, groups, body, 0)
    dqw_o[...] = contract_rows(dq[...], normed[...]).astype(bf16)
    dkw_o[...] = contract_rows(dk[...], normed[...]).astype(bf16)
    dvw_o[...] = contract_rows(dv[...], normed[...]).astype(bf16)
    up = matmul(dq[...], qw[...]) + matmul(dk[...], kw[...]) + matmul(dv[...], vw[...])
    part, gain = norm_back_rows(tok[...].astype(f32), g1[...], up)
    g1_o[...] = gain
    ing_o[...] = first_grad[...] + part


def self_bwd(depth, length, first_grad, mixed, q, k, v, bias, ow, qw, kw, vw, normed, tok, g1):
    rows, width = tok.shape
    weight = jax.ShapeDtypeStruct(ow.shape, bf16)
    return pl.pallas_call(
        functools.partial(self_bwd_kernel, depth, length),
        out_shape=(
            weight,
            weight,
            weight,
            weight,
            jax.ShapeDtypeStruct((rows, width), f32),
            jax.ShapeDtypeStruct((1, width), f32),
            jax.ShapeDtypeStruct(bias.shape, f32),
        ),
        scratch_shapes=[pltpu.VMEM(q.shape, bf16)] * 4,
        compiler_params=params(),
        cost_estimate=cost(21),
        name="self_bwd",
    )(first_grad, mixed, q, k, v, bias, ow, qw, kw, vw, normed, tok, g1)


def kv_fwd_kernel(place, source, kw, vw, out):
    inner = kw.shape[0]
    rows = source[0, 0]
    for n, w in enumerate((kw, vw)):
        out[0, 0, :, n * inner : (n + 1) * inner] = lax.dot_general(
            rows, w[...], (((0,), (1,)), ((), ())), preferred_element_type=f32
        ).astype(bf16)


def kv_fwd(place, memory, kw, vw):
    micros, pairs, width, slots = memory.shape
    inner = kw.shape[0]
    whole = pl.BlockSpec((inner, width), lambda s, m, place: (0, 0))
    return pl.pallas_call(
        kv_fwd_kernel,
        grid_spec=pltpu.PrefetchScalarGridSpec(
            num_scalar_prefetch=1,
            grid=(pairs, micros),
            in_specs=[
                pl.BlockSpec((1, 1, width, slots), lambda s, m, place: (m, place[s], 0, 0)),
                whole,
                whole,
            ],
            out_specs=pl.BlockSpec((1, 1, slots, 2 * inner), lambda s, m, place: (s, m, 0, 0)),
        ),
        out_shape=jax.ShapeDtypeStruct((pairs, micros, slots, 2 * inner), bf16),
        compiler_params=params(32),
        cost_estimate=cost(9),
        name="kv_fwd",
    )(place, memory, kw, vw)


def kv_bwd_kernel(place, source, kw, vw, kvg, out, dkw_o, dvw_o, acc):
    inner = kw.shape[0]
    step = pl.program_id(0) * pl.num_programs(1) + pl.program_id(1)
    grads = kvg[0, 0]

    @pl.when(step == 0)
    def clear():
        acc[...] = jnp.zeros_like(acc)

    out[0, 0] = lax.dot_general(
        kw[...], grads[:, :inner], (((0,), (1,)), ((), ())), preferred_element_type=f32
    ) + lax.dot_general(
        vw[...], grads[:, inner:], (((0,), (1,)), ((), ())), preferred_element_type=f32
    )
    acc[...] += lax.dot_general(
        grads, source[0, 0], (((0,), (1,)), ((), ())), preferred_element_type=f32
    )

    @pl.when(step == pl.num_programs(0) * pl.num_programs(1) - 1)
    def write():
        dkw_o[...] = acc[:inner].astype(bf16)
        dvw_o[...] = acc[inner:].astype(bf16)


def kv_bwd(place, memory, kw, vw, kvg):
    micros, pairs, width, slots = memory.shape
    inner = kw.shape[0]
    whole = pl.BlockSpec((inner, width), lambda s, m, place: (0, 0))
    weight = jax.ShapeDtypeStruct((inner, width), bf16)
    block = pl.BlockSpec((1, 1, width, slots), lambda s, m, place: (m, place[s], 0, 0))
    return pl.pallas_call(
        kv_bwd_kernel,
        grid_spec=pltpu.PrefetchScalarGridSpec(
            num_scalar_prefetch=1,
            grid=(pairs, micros),
            in_specs=[
                block,
                whole,
                whole,
                pl.BlockSpec((1, 1, slots, 2 * inner), lambda s, m, place: (s, m, 0, 0)),
            ],
            out_specs=(block, whole, whole),
            scratch_shapes=[pltpu.VMEM((2 * inner, width), f32)],
        ),
        out_shape=(jax.ShapeDtypeStruct(memory.shape, f32), weight, weight),
        compiler_params=params(48),
        cost_estimate=cost(17),
        name="kv_bwd",
    )(place, memory, kw, vw, kvg)


gelu_c = math.sqrt(2 / math.pi)


def plan(steps):
    arrays, out = [], []
    for buffers in steps:
        out.append([])
        for n, sources in enumerate(buffers):
            at = 0
            for array, index, rows in sources:
                found = [i for i, known in enumerate(arrays) if known is array]
                if not found:
                    arrays.append(array)
                out[-1].append((found[0] if found else len(arrays) - 1, index, n, at, rows))
                at += rows
    return arrays, out


def fetch(places, refs, hold, sems, step, slot):
    copies = []
    for i, (which, index, n, at, rows) in enumerate(places[step]):
        src = refs[which].at[index] if index else refs[which]
        copies.append(pltpu.make_async_copy(src, hold.at[slot, n, pl.ds(at, rows)], sems.at[slot, i]))
    return copies


def run_fetch(places, refs, hold, sems):
    step = pl.program_id(0)
    for i in range(len(places)):

        @pl.when(step == i)
        def move(i=i):
            if i == 0:
                for copy in fetch(places, refs, hold, sems, 0, 0):
                    copy.start()
            if i + 1 < len(places):
                for copy in fetch(places, refs, hold, sems, i + 1, (i + 1) % 2):
                    copy.start()
            for copy in fetch(places, refs, hold, sems, i, i % 2):
                copy.wait()


def feed_grad_kernel(places, count, *refs):
    nf_a, nf_b, og_a, og_b = refs[:4]
    weights = refs[4 : 4 + count]
    dgw_o, dlw_o, ddw_o, hid_o, gl_o, ll_o, nf, og, hold, sems, whole_sems = refs[4 + count :]
    rows = nf_a.shape[0]
    step = pl.program_id(0)

    def loads():
        return [
            pltpu.make_async_copy(src, dst.at[pl.ds(at, rows)], whole_sems.at[i])
            for i, (src, dst, at) in enumerate([(nf_a, nf, 0), (nf_b, nf, rows), (og_a, og, 0), (og_b, og, rows)])
        ]

    @pl.when(step == 0)
    def load():
        for copy in loads():
            copy.start()

    run_fetch(places, weights, hold, sems)

    @pl.when(step == 0)
    def loaded():
        for copy in loads():
            copy.wait()

    slot = lax.rem(step, 2)
    x, up = nf[...], og[...]
    g = contract_cols(x, hold[slot, 0])
    lin = contract_cols(x, hold[slot, 1])
    hg = contract_cols(up, hold[slot, 2])
    t = jnp.tanh(gelu_c * (g + 0.044715 * (g * g * g)))
    act = 0.5 * g * (1.0 + t)
    slope = 0.5 * (1.0 + t) + 0.5 * g * (1.0 - t * t) * (gelu_c * (1.0 + 3 * 0.044715 * (g * g)))
    hidden = (act * lin).astype(bf16)
    gl = (hg * lin * slope).astype(bf16)
    ll = (hg * act).astype(bf16)
    hid_o[0] = hidden
    gl_o[0] = gl
    ll_o[0] = ll
    dgw_o[0] = contract_rows(gl, x).astype(bf16)
    dlw_o[0] = contract_rows(ll, x).astype(bf16)
    ddw_o[0] = contract_rows(hidden, up).astype(bf16)


def feed_grad(nf_a, nf_b, og_a, og_b, steps, block):
    rows, width = nf_a.shape
    weights, places = plan(steps)
    n = len(steps)
    any_spec = pl.BlockSpec(memory_space=pl.ANY)
    tile = pl.BlockSpec((1, block, width), lambda i: (i, 0, 0))
    column = pl.BlockSpec((1, 2 * rows, block), lambda i: (i, 0, 0))
    weight = jax.ShapeDtypeStruct((n, block, width), bf16)
    act = jax.ShapeDtypeStruct((n, 2 * rows, block), bf16)
    return pl.pallas_call(
        functools.partial(feed_grad_kernel, places, len(weights)),
        grid=(n,),
        in_specs=[any_spec] * (4 + len(weights)),
        out_specs=(tile, tile, tile, column, column, column),
        out_shape=(weight, weight, weight, act, act, act),
        scratch_shapes=[
            pltpu.VMEM((2 * rows, width), bf16),
            pltpu.VMEM((2 * rows, width), bf16),
            pltpu.VMEM((2, 3, block, width), bf16),
            pltpu.SemaphoreType.DMA((2, max(len(p) for p in places))),
            pltpu.SemaphoreType.DMA((4,)),
        ],
        compiler_params=params(60),
        cost_estimate=cost(13 * n),
        name="feed_grad",
    )(nf_a, nf_b, og_a, og_b, *weights)


def feed_out_kernel(places, act_places, count, act_count, *refs):
    weights, acts = refs[:count], refs[count : count + act_count]
    nfg_o, nfg_b, res_o, res_b, res_t, nfg_t, hold, acts_hold, sems, act_sems = refs[count + act_count :]
    step = pl.program_id(0)
    rows = nfg_o.shape[0]
    run_fetch(places, weights, hold, sems)
    run_fetch(act_places, acts, acts_hold, act_sems)
    slot = lax.rem(step, 2)
    nfg = matmul(acts_hold[slot, 0], hold[slot, 0]) + matmul(acts_hold[slot, 1], hold[slot, 1])
    res = matmul(acts_hold[slot, 2], hold[slot, 2])

    @pl.when(step == 0)
    def first():
        res_o[...] = res[:rows]
        res_t[...] = res[rows:]
        nfg_o[...] = nfg[:rows]
        nfg_t[...] = nfg[rows:]

    @pl.when(step > 0)
    def later():
        res_o[...] += res[:rows]
        res_t[...] += res[rows:]
        nfg_o[...] += nfg[:rows]
        nfg_t[...] += nfg[rows:]

    @pl.when(step == pl.num_programs(0) - 1)
    def last():
        res_b[...] = res_t[...].astype(bf16)
        nfg_b[...] = nfg_t[...].astype(bf16)


def feed_out(rows, width, steps, act_steps, block):
    weights, places = plan(steps)
    acts, act_places = plan(act_steps)
    whole = pl.BlockSpec((rows, width), lambda i: (0, 0))
    wide, low = jax.ShapeDtypeStruct((rows, width), f32), jax.ShapeDtypeStruct((rows, width), bf16)
    return pl.pallas_call(
        functools.partial(feed_out_kernel, places, act_places, len(weights), len(acts)),
        grid=(len(steps),),
        in_specs=[pl.BlockSpec(memory_space=pl.ANY)] * (len(weights) + len(acts)),
        out_specs=(whole, whole, whole, whole),
        out_shape=(wide, low, wide, low),
        scratch_shapes=[
            pltpu.VMEM((rows, width), f32),
            pltpu.VMEM((rows, width), f32),
            pltpu.VMEM((2, 3, block, width), bf16),
            pltpu.VMEM((2, 3, 2 * rows, block), bf16),
            pltpu.SemaphoreType.DMA((2, max(len(p) for p in places))),
            pltpu.SemaphoreType.DMA((2, max(len(p) for p in act_places))),
        ],
        compiler_params=params(60),
        cost_estimate=cost(30),
        name="feed_out",
    )(*weights, *acts)


def tree_sum(values):
    while len(values) > 1:
        values = [left + right for left, right in zip(values[::2], values[1::2])]
    return values[0]


def tie(*values):
    return lax.optimization_barrier(values)


def fold_parts(held, order, bit):
    keep = [i for i, k in enumerate(order) if not k & bit]
    send = [order.index(order[i] | bit) for i in keep]
    return [jnp.stack([held[:, i] for i in at], axis=1) for at in (keep, send)]


def fold_step(held, order, bit):
    kept, sent = fold_parts(held, order, bit)
    return kept, to_mem(sent, bit), [k for k in order if not k & bit]


def per_device(
    inputs,
    memory,
    memory_lengths,
    keep_mask,
    norm_self,
    query_self,
    key_self,
    value_self,
    output_self,
    bias_table,
    norm_cross,
    query_cross,
    key_cross,
    value_cross,
    output_cross,
    norm_feed,
    gate_feed,
    linear_feed,
    down_feed,
    output_grad,
):
    micros = inputs.shape[0]
    length = inputs.shape[3]
    width = inputs.shape[4]
    pairs = memory.shape[2]
    slots = memory.shape[3]
    heads = bias_table.shape[1]
    buckets = bias_table.shape[0]
    seqs = lax.axis_size("seq")
    mems = lax.axis_size("mem")
    chips = seqs // 2
    slim = query_self.shape[1]
    inner = slim * seqs
    depth = inner // heads
    feed = gate_feed.shape[1]
    part = feed // mems
    rows = micros * length
    seq_index = lax.axis_index("seq")
    core = seq_index % 2
    chip = seq_index // 2
    mem_index = lax.axis_index("mem")
    gain_self = norm_self.astype(f32)
    gain_cross = norm_cross.astype(f32)
    gain_feed = norm_feed.astype(f32)


    bits = mem_bits()
    spot = jnp.stack([core, chip] + [mem_index ^ q for q in range(mems)]).astype(jnp.int32)

    def quarters(shard):
        shard = shard.reshape(mems, shard.shape[0] // mems, width)
        return jnp.stack(
            [lax.dynamic_index_in_dim(shard, mem_index ^ k, 0, keepdims=False) for k in range(mems)]
        )

    last = chips - 1
    early = list(range(1, last))

    def matrices(held, other):
        full = assemble(spot, held, other)
        full = full.reshape(4, mems // 4, seqs, -1, width).transpose(0, 2, 1, 3, 4)
        return full.reshape(4, inner, width)

    def hold_plane(pack, moved):
        return jnp.concatenate([pack[None], jnp.stack(moved, axis=1)], axis=0)

    first_pack = quarters(jnp.concatenate([key_cross.T, value_cross.T, query_self.T, key_self.T], axis=0))
    second_pack = quarters(
        jnp.concatenate([value_self.T, output_self, query_cross.T, output_cross], axis=0)
    )
    gate_own, linear_own, down_own = quarters(gate_feed.T), quarters(linear_feed.T), quarters(down_feed)
    both = [jnp.stack([gate_own[0], linear_own[0]])]
    down = [down_own]

    onehot = (
        position_buckets(length).reshape(length * length, 1)
        == jnp.arange(buckets, dtype=jnp.int32)[None, :]
    ).astype(bf16)
    position_bias = (
        jnp.dot(onehot, bias_table, preferred_element_type=f32)
        .reshape(length, length, heads)
        .transpose(2, 0, 1)
    )
    row_index = jnp.arange(length, dtype=jnp.int32)
    causal = row_index[:, None] >= row_index[None, :]
    position_bias = jnp.where(causal[None], position_bias, masked_score)
    tokens = inputs.reshape(rows, width)
    og_low = output_grad.reshape(rows, width)
    gain_self, gain_cross, gain_feed = [g.reshape(1, width) for g in (gain_self, gain_cross, gain_feed)]
    spots = jnp.stack(
        [(mem_index ^ s) * slots + jnp.arange(slots, dtype=jnp.int32) for s in range(mems)], 0
    )
    len_own = lax.dynamic_index_in_dim(memory_lengths[:, 0], mem_index, 1, keepdims=False)
    place = spot[2:]
    source = memory.reshape(micros, pairs, slots, width).swapaxes(2, 3)
    both_packs = jnp.stack([first_pack[0], second_pack[0]])
    moved = [to_step(both_packs, j) for j in range(1, chips)]
    og_other = rows_to_core(og_low)
    keep_all = lax.all_gather(keep_mask[:, 0], "mem", axis=0)
    moved, both[0], og_other, keep_all = tie(moved, both[0], og_other, keep_all)
    keep_own = lax.dynamic_index_in_dim(keep_all, mem_index, 2, keepdims=False)
    keep_own = jnp.stack(
        [lax.dynamic_index_in_dim(keep_own, mem_index ^ s, 0, keepdims=False) for s in range(mems)], 1
    )
    valid = (spots[None] < len_own[:, None, None]) & ((keep_own == 1) | (spots[None] == 0))
    valid = valid.reshape(micros, 1, mems * slots).astype(f32)


    first_parts, second_parts = [jnp.stack([piece[i] for piece in moved])[None] for i in range(2)]
    first_order, second_order = [0], [0]
    for first_bit, second_bit in zip(bits, bits[::-1]):
        first_more, second_more = to_mem(first_parts, first_bit), to_mem(second_parts, second_bit)
        first_order = first_order + [k | first_bit for k in first_order]
        second_order = second_order + [k | second_bit for k in second_order]
        if len(both) < last:
            both.append(to_next(both[-1]))
        first_more, second_more, both[-1] = tie(first_more, second_more, both[-1])
        first_parts = jnp.concatenate([first_parts, first_more])
        second_parts = jnp.concatenate([second_parts, second_more])
    while len(both) < last:
        both.append(to_next(both[-1]))

    def hold_parts(pack, parts, order):
        spread = jnp.stack([parts[order.index(k)] for k in range(mems)], axis=1)
        return jnp.concatenate([pack[None], spread], axis=0)

    first_held = hold_parts(first_pack, first_parts, first_order)
    first_more = to_core(first_held)
    gate_early = jnp.stack([both[j][0] for j in early])[None]
    linear_early = jnp.stack([both[j][1] for j in early])[None]
    gate_a1 = to_mem(gate_early, bits[0])
    linear_a1 = to_mem(linear_early, bits[-1])
    both.append(to_next(both[-1]))
    second_held = hold_parts(second_pack, second_parts, second_order)
    first_more, gate_a1, linear_a1, both[last], second_held = tie(
        first_more, gate_a1, linear_a1, both[last], second_held
    )

    second_more = to_core(second_held)
    gate_late, linear_late = both[last][:1], both[last][1:]
    gate_late_a1 = to_mem(gate_late, bits[0])
    linear_late_a1 = to_mem(linear_late, bits[-1])
    first_mats = matrices(first_held, first_more)
    kc_full, vc_full, qs_full, ks_full = [first_mats[i] for i in range(4)]
    kv_local = kv_fwd(place, source, kc_full, vc_full)
    gate_early = jnp.concatenate([gate_early, gate_a1])
    linear_early = jnp.concatenate([linear_early, linear_a1])
    kv_local, second_more, gate_late_a1, linear_late_a1, down[0], gate_early, linear_early = tie(
        kv_local, second_more, gate_late_a1, linear_late_a1, down[0], gate_early, linear_early
    )

    kvs = [to_mem(kv_local[s], s) if s else kv_local[s] for s in range(mems)]
    down.append(to_next(down[0]))
    second_mats = matrices(second_held, second_more)
    vs_full, os_full, qc_full, oc_full = [second_mats[i] for i in range(4)]
    normed, q, k, v, mixed, first_sum, normed_cross, cq = self_fwd(
        depth, length, tokens, gain_self, qs_full, ks_full, vs_full, os_full, position_bias, gain_cross, qc_full
    )
    kvs, down[1], cq, gate_early, linear_early = tie(kvs, down[1], cq, gate_early, linear_early)

    def spread_rest(held, order, over):
        parts = [held]
        for bit in over:
            parts.append(to_mem(jnp.concatenate(parts) if len(parts) > 1 else parts[0], bit))
            order = order + [k | bit for k in order]
        return parts, order

    gate_parts, gate_order = spread_rest(gate_early, [0, bits[0]], bits[1:])
    linear_parts, linear_order = spread_rest(linear_early, [0, bits[-1]], bits[::-1][1:])
    gate_late = jnp.concatenate([gate_late, gate_late_a1])
    linear_late = jnp.concatenate([linear_late, linear_late_a1])
    for _ in early[1:]:
        down.append(to_next(down[-1]))
    cmixed, second_sum, normed_feed = cross_fwd(depth, length, cq, valid, oc_full, first_sum, gain_feed, kvs)
    gate_parts, linear_parts, gate_late, linear_late, down[1:], normed_feed = tie(
        gate_parts, linear_parts, gate_late, linear_late, down[1:], normed_feed
    )

    def sources(parts, order, n):
        places = {}
        at = 0
        for piece in parts:
            for i in range(piece.shape[0]):
                places[order[at]] = (piece, (i, n) if piece.ndim == 4 else (i,), part)
                at += 1
        return [places[k] for k in range(mems)]

    def whole_source(array, listed):
        if part % 16 == 0:
            return listed
        pieces = []
        for piece, index, _ in listed:
            for i in index:
                piece = piece[i]
            pieces.append(piece)
        return [(jnp.concatenate(pieces), (), feed)]

    own_steps = [[(g.reshape(feed, width), (), feed)] for g in (gate_own, linear_own, down_own)]
    early_steps = [
        [
            whole_source(None, sources(gate_parts, gate_order, n)),
            whole_source(None, sources(linear_parts, linear_order, n)),
            [(down[j].reshape(feed, width), (), feed)],
        ]
        for n, j in enumerate(early)
    ]
    nf_other = rows_to_core(normed_feed)
    gate_late_parts, gate_order = spread_rest(gate_late, [0, bits[0]], bits[1:])
    linear_late_parts, linear_order = spread_rest(linear_late, [0, bits[-1]], bits[::-1][1:])
    down.append(to_next(down[-1]))
    grads_a = feed_grad(normed_feed, nf_other, og_low, og_other, early_steps + [own_steps], feed)
    grads_a, gate_late_parts, linear_late_parts, down[last], nf_more = tie(
        grads_a, gate_late_parts, linear_late_parts, down[last], nf_other
    )

    gate_x = grads_a[0].reshape(last, mems, part, width)
    linear_x = grads_a[1].reshape(last, mems, part, width)
    natural_order = list(range(mems))
    gate_kept, gate_moved, gate_ord = fold_step(gate_x, natural_order, bits[-1])
    linear_kept, linear_moved, linear_ord = fold_step(linear_x, natural_order, bits[0])
    down_total = to_next(grads_a[2][0])
    late_steps = [
        [
            whole_source(None, sources(gate_late_parts, gate_order, 0)),
            whole_source(None, sources(linear_late_parts, linear_order, 0)),
            [(down[last].reshape(feed, width), (), feed)],
        ]
    ]
    grads_b = feed_grad(normed_feed, nf_more, og_low, og_other, late_steps, feed)
    act_steps = [
        [[(grads[i], (n,), 2 * rows)] for i in (4, 5, 3)]
        for grads, count in ((grads_a, last), (grads_b, 1))
        for n in range(count)
    ]
    nfg_own, nfg_send, res_own, res_send = feed_out(
        rows, width, early_steps + [own_steps] + late_steps, act_steps, feed
    )
    gate_moved, linear_moved, down_total, nfg_send, dg_b, dl_b = tie(
        gate_moved, linear_moved, down_total, nfg_send, grads_b[0], grads_b[1]
    )

    def two_folds(fresh, order, bit, older, older_order, older_bit):
        kept, sent = fold_parts(fresh, order, bit)
        older_kept, older_sent = fold_parts(older, older_order, older_bit)
        moved = to_mem(jnp.concatenate([sent.reshape(-1, part, width), older_sent.reshape(-1, part, width)]), bit)
        count = sent.shape[0] * sent.shape[1]
        return kept, moved[:count].reshape(sent.shape), older_kept, moved[count:].reshape(older_sent.shape)

    def fold_to_last(held, order, over):
        for bit in over[:-1]:
            kept, moved, order = fold_step(held, order, bit)
            held = add_low(kept, moved)
        return held, order

    gate_y, gate_yo = fold_to_last(add_low(gate_kept, gate_moved), gate_ord, bits[::-1][1:])
    linear_y, linear_yo = fold_to_last(add_low(linear_kept, linear_moved), linear_ord, bits[1:])
    nfg_more = rows_to_core(nfg_send)
    gate_b, gate_bm, linear_yk, linear_ym = two_folds(
        dg_b.reshape(1, mems, part, width), natural_order, bits[-1], linear_y, linear_yo, bits[-1]
    )
    linear_b, linear_bm, gate_yk, gate_ym = two_folds(
        dl_b.reshape(1, mems, part, width), natural_order, bits[0], gate_y, gate_yo, bits[0]
    )
    for j in early[1:]:
        down_total = to_next(add_low(down_total, grads_a[2][j - 1]))
    kvg, (grad_gain_feed, grad_co, grad_cq, first_grad, grad_gain_cross) = cross_bwd(
        depth, length, og_low, nfg_own, nfg_more, second_sum, gain_feed, cmixed, cq, valid, oc_full,
        first_sum, gain_cross, normed_cross, qc_full, kvs,
    )
    gate_bm, linear_bm, gate_ym, linear_ym, down_total, kvg, grad_gain_cross, res_send = tie(
        gate_bm, linear_bm, gate_ym, linear_ym, down_total, kvg, grad_gain_cross, res_send
    )

    kvg = [to_mem(kvg[s], s) if s else kvg[s] for s in range(mems)]
    gate_y, linear_y = add_low(gate_yk, gate_ym)[:, 0], add_low(linear_yk, linear_ym)[:, 0]
    down_total = add_low(down_total, grads_b[2][0]).reshape(mems, part, width)
    ring = to_next(jnp.concatenate([down_total, gate_y[:1], linear_y[:1]]))
    res_more = rows_to_core(res_send)
    grad_os, grad_qs, grad_ks, grad_vs, input_grad, grad_gain_self, score_sum = self_bwd(
        depth, length, first_grad, mixed, q, k, v, position_bias, os_full, qs_full, ks_full, vs_full,
        normed, tokens, gain_self,
    )
    kvg, ring, grad_qs, res_more, gate_bm, linear_bm = tie(kvg, ring, grad_qs, res_more, gate_bm, linear_bm)

    self_stack = jnp.stack(
        [g.reshape(chips, 2, slim, width) for g in (grad_qs, grad_ks, grad_vs, grad_os)], axis=2
    )
    kept = lax.dynamic_index_in_dim(self_stack, core, 1, keepdims=False)
    sent = to_core(lax.dynamic_index_in_dim(self_stack, 1 - core, 1, keepdims=False))
    down_total, both_total = ring[:mems], ring[mems:]
    for j in early[1:]:
        both_total = to_next(add_low(both_total, jnp.stack([gate_y[j - 1], linear_y[j - 1]])))
    gate_b, gate_bo = fold_to_last(add_low(gate_b, gate_bm), gate_ord, bits[::-1][1:])
    linear_b, linear_bo = fold_to_last(add_low(linear_b, linear_bm), linear_ord, bits[1:])
    gate_bk, gate_bm, _ = fold_step(gate_b, gate_bo, bits[0])
    linear_bk, linear_bm, _ = fold_step(linear_b, linear_bo, bits[-1])
    memory_grad, grad_kc, grad_vc = kv_bwd(place, source, kc_full, vc_full, jnp.stack(kvg))
    sent, both_total, gate_bm, linear_bm, grad_kc = tie(sent, both_total, gate_bm, linear_bm, grad_kc)

    grad_table = lax.dot_general(
        onehot.astype(f32),
        score_sum.reshape(heads, length * length),
        (((0,), (1,)), ((), ())),
        preferred_element_type=f32,
    )
    table_row = jnp.pad(grad_table.reshape(1, buckets * heads), ((0, 0), (0, width - buckets * heads)))
    small = jnp.concatenate([grad_gain_self, grad_gain_cross, grad_gain_feed, table_row], axis=0)

    def to_rows(value):
        high = value.astype(bf16)
        rest = (value - high.astype(f32)).astype(bf16)
        return jnp.concatenate([high, rest, jnp.zeros((16 - 2 * value.shape[0], width), bf16)])

    def from_rows(value, count):
        return value[:count].astype(f32) + value[count : 2 * count].astype(f32)

    cross_stack = jnp.stack(
        [g.reshape(seqs, slim, width) for g in (grad_kc, grad_vc, grad_cq, grad_co)], axis=1
    ).reshape(seqs, 4 * slim, width)
    cross_sum = lax.psum_scatter(cross_stack, "seq", scatter_dimension=0)
    total = add_low(kept, sent).reshape(chips, mems, 4 * slim // mems, width)
    share = 4 * slim // mems
    down_mine = add_low(down_total, grads_a[2][last - 1].reshape(mems, part, width))
    columns = []
    for s in range(mems):
        column = lax.dynamic_index_in_dim(total, mem_index ^ s, 1, keepdims=False).reshape(-1, width)
        columns.append(jnp.concatenate([column, down_mine[s], to_rows(small)]))
    columns = [to_mem(p, s) if s else p for s, p in enumerate(columns)]
    gate_b, linear_b = add_low(gate_bk, gate_bm)[0, 0], add_low(linear_bk, linear_bm)[0, 0]
    both_total = to_next(add_low(both_total, jnp.stack([gate_b, linear_b])))
    columns, both_total = tie(columns, both_total)

    down_sum = sum_low([p[chips * share : chips * share + part] for p in columns])
    small = tree_sum([from_rows(p[chips * share + part :], 4) for p in columns])
    total = sum_low([p[: chips * share] for p in columns]).reshape(chips, share, width)
    pieces = [
        jnp.concatenate(
            [lax.dynamic_index_in_dim(total, (chip + j) % chips, 0, keepdims=False), to_rows(small)]
        )
        for j in range(chips)
    ]
    pieces = [to_step(p, j) if j else p for j, p in enumerate(pieces)]
    both_sum = add_low(both_total, jnp.stack([gate_y[last - 1], linear_y[last - 1]]))
    gate_g = [both_sum[:1], to_mem(both_sum[:1], bits[0])]
    linear_g = [both_sum[1:], to_mem(both_sum[1:], bits[-1])]
    pieces, gate_g, linear_g, cross_sum = tie(pieces, gate_g, linear_g, cross_sum)

    self_mine = sum_low([p[:share] for p in pieces])
    small = jnp.stack([from_rows(p[share:], 4) for p in pieces])
    small = tree_sum(
        [lax.dynamic_index_in_dim(small, (chip - z) % chips, 0, keepdims=False) for z in range(chips)]
    )
    gate_g, gate_order = spread_rest(jnp.concatenate(gate_g), [0, bits[0]], bits[1:])
    linear_g, linear_order = spread_rest(jnp.concatenate(linear_g), [0, bits[-1]], bits[::-1][1:])
    cross_parts = [to_mem(p, s) if s else p for s, p in enumerate(quarters(cross_sum))]
    gate_g, linear_g, cross_parts, small, self_mine = tie(gate_g, linear_g, cross_parts, small, self_mine)

    mine = jnp.concatenate([self_mine, sum_low(cross_parts), down_sum])
    mine_g = [mine] + [to_mem(mine, k) for k in range(1, mems)]
    small = small + to_core(small)

    def settle(parts, order):
        flat = jnp.concatenate(parts)
        pieces = [flat[order.index(k)] for k in range(mems)]
        return natural(pieces, mem_index).astype(f32)

    gate_out = settle(gate_g, gate_order).reshape(feed, width)
    linear_out = settle(linear_g, linear_order).reshape(feed, width)
    mine_g, gate_out, linear_out = tie(mine_g, gate_out, linear_out)
    result = second_sum + res_own + res_more.astype(f32)

    def settled(start, rows_of):
        return natural([p[start : start + rows_of] for p in mine_g], mem_index).astype(f32)

    self_sum = settled(0, share).reshape(4, slim, width)
    cross_sum = settled(share, share).reshape(4, slim, width)
    down_out = settled(2 * share, part).reshape(feed, width)
    return (
        result.reshape(inputs.shape),
        input_grad.reshape(inputs.shape),
        memory_grad.swapaxes(2, 3).reshape(memory.shape),
        small[0],
        self_sum[0].T,
        self_sum[1].T,
        self_sum[2].T,
        self_sum[3],
        small[3, : buckets * heads].reshape(buckets, heads),
        small[1],
        cross_sum[2].T,
        cross_sum[0].T,
        cross_sum[1].T,
        cross_sum[3],
        small[2],
        gate_out.T,
        linear_out.T,
        down_out,
    )


def solution(mesh):
    tokens_at = P(None, "seq", "mem", None, None)
    memory_at = P(None, "seq", None, "mem", None)
    columns, row_cut = P(None, "seq"), P("seq", None)
    return jax.shard_map(
        per_device,
        mesh=mesh,
        in_specs=(
            tokens_at,
            memory_at,
            P(None, "seq", None),
            P(None, "seq", None, "mem"),
            P(),
            columns,
            columns,
            columns,
            row_cut,
            P(),
            P(),
            columns,
            columns,
            columns,
            row_cut,
            P(),
            columns,
            columns,
            row_cut,
            tokens_at,
        ),
        out_specs=(
            tokens_at,
            tokens_at,
            memory_at,
            P(),
            columns,
            columns,
            columns,
            row_cut,
            P(),
            P(),
            columns,
            columns,
            columns,
            row_cut,
            P(),
            columns,
            columns,
            row_cut,
        ),
        check_vma=False,
    )
```

```python
import functools
import math

import jax
import jax.numpy as jnp
from jax import lax
from jax.experimental import pallas as pl
from jax.experimental.pallas import tpu as pltpu
from jax.sharding import PartitionSpec as P

norm_eps = 1e-06
masked_score = -1e30
bf16 = jnp.bfloat16
f32 = jnp.float32


def bucket_edges():
    return [math.ceil(16 * 8 ** ((number - 16) / 16)) for number in range(17, 32)]


def position_buckets(length):
    row_index = jnp.arange(length, dtype=jnp.int32)
    offset = jnp.maximum(row_index[:, None] - row_index[None, :], 0)
    bucket = jnp.minimum(offset, 16)
    for threshold in bucket_edges():
        bucket = bucket + (offset >= threshold).astype(jnp.int32)
    return bucket


def matmul(left, right):
    return jnp.dot(left, right, preferred_element_type=f32)


def contract_rows(left, right):
    return lax.dot_general(left, right, (((0,), (0,)), ((), ())), preferred_element_type=f32)


def contract_cols(left, right):
    return lax.dot_general(left, right, (((1,), (1,)), ((), ())), preferred_element_type=f32)


def add_low(left, right):
    return (left.astype(f32) + right.astype(f32)).astype(bf16)


def to_core(value):
    count = lax.axis_size("seq")
    return lax.ppermute(value, "seq", [(i, i ^ 1) for i in range(count)])


def rows_to_core(value):
    return to_core(value.reshape(-1, 64, value.shape[-1])).reshape(value.shape)


def to_next(value):
    count = lax.axis_size("seq")
    return lax.ppermute(value, "seq", [(i, (i + 2) % count) for i in range(count)])


def to_mem(value, mask):
    count = lax.axis_size("mem")
    return lax.ppermute(value, "mem", [(i, i ^ mask) for i in range(count)])


def mem_bits():
    return [1 << b for b in range((lax.axis_size("mem") - 1).bit_length())]


def to_step(value, step):
    count = lax.axis_size("seq")
    return lax.ppermute(value, "seq", [(i, (i + 2 * step) % count) for i in range(count)])


def to_seq(value, mask):
    count = lax.axis_size("seq")
    return lax.ppermute(value, "seq", [(i, i ^ mask) for i in range(count)])


def after(value, *others):
    return lax.optimization_barrier((value, *others))[0]


def ring_gather(value):
    pieces = [value]
    for _ in range(lax.axis_size("seq") // 2 - 1):
        pieces.append(to_next(pieces[-1]))
    return pieces


def ring_sum(pieces):
    total = pieces[1]
    for piece in pieces[2:]:
        total = add_low(to_next(total), piece)
    return add_low(to_next(total), pieces[0])


def spread_gather(value, bits):
    held, order = value[None], [0]
    for bit in bits:
        held = jnp.concatenate([held, to_mem(held, bit)], axis=0)
        order = order + [k | bit for k in order]
    return [held[order.index(k)] for k in range(len(order))]


def fold(held, bits):
    order = list(range(held.shape[0]))
    for bit in bits:
        keep = [i for i, k in enumerate(order) if not k & bit]
        send = [order.index(order[i] | bit) for i in keep]
        moved = to_mem(jnp.stack([held[i] for i in send]), bit)
        held = jnp.stack([add_low(held[i], moved[n]) for n, i in enumerate(keep)])
        order = [order[i] for i in keep]
    return held[0]


def sum_low(pieces):
    total = pieces[0].astype(f32)
    for piece in pieces[1:]:
        total = total + piece.astype(f32)
    return total.astype(bf16)


def direct_fold(pieces):
    return sum_low([to_mem(p, k) if k else p for k, p in enumerate(pieces)])


def natural(pieces, mem_index):
    stacked = jnp.stack(pieces)
    return jnp.stack(
        [
            lax.dynamic_index_in_dim(stacked, mem_index ^ k, 0, keepdims=False)
            for k in range(len(pieces))
        ]
    )


def back_to_mem(value, mem_index):
    pieces = [to_mem(value, k) if k else value for k in range(lax.axis_size("mem"))]
    return natural(pieces, mem_index).astype(f32)


def assemble_kernel(spot, own, other, *outs):
    chips = own.shape[0]
    core, chip = spot[0], spot[1]
    for q, out in enumerate(outs):
        for j in range(chips):
            at = lax.rem(chip - j + chips, chips) * 2
            out[at + core] = own[j, spot[2 + q]]
            out[at + 1 - core] = other[j, spot[2 + q]]


def assemble(spot, own, other):
    chips, mems, share, width = own.shape
    vmem = pl.BlockSpec(memory_space=pltpu.VMEM)
    return pl.pallas_call(
        assemble_kernel,
        in_specs=[pl.BlockSpec(memory_space=pltpu.SMEM), vmem, vmem],
        out_shape=[jax.ShapeDtypeStruct((2 * chips, share, width), bf16)] * mems,
        compiler_params=params(26),
        cost_estimate=cost(3),
        name="assemble",
    )(spot, own, other)


def params(limit_mb=56):
    return pltpu.CompilerParams(vmem_limit_bytes=limit_mb * 1024 * 1024)


def cost(micro_seconds):
    return pl.CostEstimate(
        flops=micro_seconds * 10**9, bytes_accessed=micro_seconds * 3 * 10**6, transcendentals=0
    )


def row_norm(value):
    return lax.rsqrt(jnp.mean(value * value, axis=-1, keepdims=True) + norm_eps)


def norm_back_rows(value, gain, upstream):
    scale = row_norm(value)
    weighted = upstream * gain
    mean_dot = jnp.mean(weighted * value, axis=-1, keepdims=True)
    gain_grad = jnp.sum(upstream * value * scale, axis=0, keepdims=True)
    return weighted * scale - value * (scale * scale * scale * mean_dot), gain_grad


def lane_head(length, depth):
    return lax.broadcasted_iota(jnp.int32, (length, 128), 1) // depth


def self_fwd_kernel(depth, length, tok, g1, qw, kw, vw, ow, bias, g2, cw, tok_o, normed_o, q_o, k_o, v_o, mixed_o, first_o, nc_o, cq_o):
    for m in range(tok.shape[0]):
        tok_o[m * length : (m + 1) * length] = tok[m].astype(f32).T.astype(bf16)
    x = tok_o[...].astype(f32)
    normed = (x * row_norm(x) * g1[...]).astype(bf16)
    normed_o[...] = normed
    q_o[...] = contract_cols(normed, qw[...]).astype(bf16)
    k_o[...] = contract_cols(normed, kw[...]).astype(bf16)
    v_o[...] = contract_cols(normed, vw[...]).astype(bf16)
    inner = qw.shape[0]
    groups, share = inner // 128, 128 // depth
    lanes = lane_head(length, depth)

    def body(step, carry):
        micro, group = step // groups, step % groups
        rows = pl.ds(pl.multiple_of(micro * length, length), length)
        cols = pl.ds(pl.multiple_of(group * 128, 128), 128)
        q, k, v = q_o[rows, cols], k_o[rows, cols], v_o[rows, cols]
        out = jnp.zeros((length, 128), f32)
        for a in range(share):
            s = contract_cols(jnp.where(lanes == a, q, 0), k) + bias[group * share + a]
            e = jnp.exp(s - jnp.max(s, axis=-1, keepdims=True))
            p = (e / jnp.sum(e, axis=-1, keepdims=True)).astype(bf16)
            out = jnp.where(lanes == a, matmul(p, v), out)
        mixed_o[rows, cols] = out.astype(bf16)
        return carry

    lax.fori_loop(0, x.shape[0] // length * groups, body, 0)
    first = tok_o[...].astype(f32) + matmul(mixed_o[...], ow[...])
    first_o[...] = first
    nc = (first * row_norm(first) * g2[...]).astype(bf16)
    nc_o[...] = nc
    cq_o[...] = contract_cols(nc, cw[...]).astype(bf16)


def self_fwd(depth, length, tok, g1, qw, kw, vw, ow, bias, g2, cw):
    rows, width = tok.shape[0] * tok.shape[2], tok.shape[1]
    inner = qw.shape[0]
    low, slim = jax.ShapeDtypeStruct((rows, width), bf16), jax.ShapeDtypeStruct((rows, inner), bf16)
    return pl.pallas_call(
        functools.partial(self_fwd_kernel, depth, length),
        out_shape=(low, low, slim, slim, slim, slim, jax.ShapeDtypeStruct((rows, width), f32), low, slim),
        compiler_params=params(40),
        cost_estimate=cost(16),
        name="self_fwd",
    )(tok, g1, qw, kw, vw, ow, bias, g2, cw)


def cross_fwd_kernel(depth, length, parts, cq, mask, ow, first, g3, *refs):
    kvs, (mixed_o, second_o, nf_o) = refs[:parts], refs[parts:]
    inner = ow.shape[0]
    groups, share = inner // 128, 128 // depth
    lanes = lane_head(length, depth)

    def body(step, carry):
        micro, group = step // groups, step % groups
        rows = pl.ds(pl.multiple_of(micro * length, length), length)
        cols = pl.ds(pl.multiple_of(group * 128, 128), 128)
        vcols = pl.ds(pl.multiple_of(inner + group * 128, 128), 128)
        q = cq[rows, cols]
        k = jnp.concatenate([kv[micro, :, cols] for kv in kvs], axis=0)
        v = jnp.concatenate([kv[micro, :, vcols] for kv in kvs], axis=0)
        out = jnp.zeros((length, 128), f32)
        for a in range(share):
            s = contract_cols(jnp.where(lanes == a, q, 0), k)
            s = jnp.where(mask[micro] > 0, s, masked_score)
            e = jnp.exp(s - jnp.max(s, axis=-1, keepdims=True))
            p = (e / jnp.sum(e, axis=-1, keepdims=True)).astype(bf16)
            out = jnp.where(lanes == a, matmul(p, v), out)
        mixed_o[rows, cols] = out.astype(bf16)
        return carry

    lax.fori_loop(0, cq.shape[0] // length * groups, body, 0)
    second = first[...] + matmul(mixed_o[...], ow[...])
    second_o[...] = second
    nf_o[...] = (second * row_norm(second) * g3[...]).astype(bf16)


def cross_fwd(depth, length, cq, mask, ow, first, g3, kvs):
    rows, width = first.shape
    return pl.pallas_call(
        functools.partial(cross_fwd_kernel, depth, length, len(kvs)),
        out_shape=(
            jax.ShapeDtypeStruct(cq.shape, bf16),
            jax.ShapeDtypeStruct((rows, width), f32),
            jax.ShapeDtypeStruct((rows, width), bf16),
        ),
        compiler_params=params(36),
        cost_estimate=cost(15),
        name="cross_fwd",
    )(cq, mask, ow, first, g3, *kvs)


def cross_bwd_kernel(depth, length, parts, og, nf_own, nf_more, second, g3, mixed, cq, mask, ow, first, g2, nc, qw, *refs):
    kvs = refs[:parts]
    kvg = refs[parts : 2 * parts]
    g3_o, dow_o, dqw_o, firstg_o, g2_o, mixg, dq = refs[2 * parts :]
    inner = ow.shape[0]
    slots = kvs[0].shape[1]
    groups, share = inner // 128, 128 // depth
    lanes = lane_head(length, depth)
    part, gain = norm_back_rows(second[...], g3[...], nf_own[...] + nf_more[...].astype(f32))
    g3_o[...] = gain
    second_grad = og[...].astype(f32) + part
    firstg_o[...] = second_grad
    low = second_grad.astype(bf16)
    dow_o[...] = contract_rows(mixed[...], low).astype(bf16)
    mixg[...] = contract_cols(low, ow[...]).astype(bf16)

    def body(step, carry):
        micro, group = step // groups, step % groups
        rows = pl.ds(pl.multiple_of(micro * length, length), length)
        cols = pl.ds(pl.multiple_of(group * 128, 128), 128)
        vcols = pl.ds(pl.multiple_of(inner + group * 128, 128), 128)
        q, o = cq[rows, cols], mixg[rows, cols]
        k = jnp.concatenate([kv[micro, :, cols] for kv in kvs], axis=0)
        v = jnp.concatenate([kv[micro, :, vcols] for kv in kvs], axis=0)
        q_grad = jnp.zeros((length, 128), f32)
        k_grad = jnp.zeros((parts * slots, 128), f32)
        v_grad = jnp.zeros((parts * slots, 128), f32)
        for a in range(share):
            qa, oa = jnp.where(lanes == a, q, 0), jnp.where(lanes == a, o, 0)
            s = contract_cols(qa, k)
            s = jnp.where(mask[micro] > 0, s, masked_score)
            e = jnp.exp(s - jnp.max(s, axis=-1, keepdims=True))
            p = e / jnp.sum(e, axis=-1, keepdims=True)
            v_grad += contract_rows(p.astype(bf16), oa)
            dp = contract_cols(oa, v)
            ds = (p * (dp - jnp.sum(p * dp, axis=-1, keepdims=True))).astype(bf16)
            q_grad = jnp.where(lanes == a, matmul(ds, k), q_grad)
            k_grad += contract_rows(ds, qa)
        dq[rows, cols] = q_grad.astype(bf16)
        for t in range(parts):
            kvg[t][micro, :, cols] = k_grad[t * slots : (t + 1) * slots].astype(bf16)
            kvg[t][micro, :, vcols] = v_grad[t * slots : (t + 1) * slots].astype(bf16)
        return carry

    lax.fori_loop(0, cq.shape[0] // length * groups, body, 0)
    dqw_o[...] = contract_rows(dq[...], nc[...]).astype(bf16)
    part, gain = norm_back_rows(first[...], g2[...], matmul(dq[...], qw[...]))
    g2_o[...] = gain
    firstg_o[...] = firstg_o[...] + part


def cross_bwd(depth, length, og, nf_own, nf_more, second, g3, mixed, cq, mask, ow, first, g2, nc, qw, kvs):
    rows, width = first.shape
    gain = jax.ShapeDtypeStruct((1, width), f32)
    weight = jax.ShapeDtypeStruct(ow.shape, bf16)
    out = pl.pallas_call(
        functools.partial(cross_bwd_kernel, depth, length, len(kvs)),
        out_shape=(
            *[jax.ShapeDtypeStruct(kv.shape, bf16) for kv in kvs],
            gain,
            weight,
            weight,
            jax.ShapeDtypeStruct((rows, width), f32),
            gain,
        ),
        scratch_shapes=[pltpu.VMEM(cq.shape, bf16), pltpu.VMEM(cq.shape, bf16)],
        compiler_params=params(50),
        cost_estimate=cost(31),
        name="cross_bwd",
    )(og, nf_own, nf_more, second, g3, mixed, cq, mask, ow, first, g2, nc, qw, *kvs)
    return out[: len(kvs)], out[len(kvs) :]


def self_bwd_kernel(depth, length, first_grad, mixed, q, k, v, bias, ow, qw, kw, vw, normed, tok, g1, dow_o, dqw_o, dkw_o, dvw_o, ing_o, g1_o, ds_o, mixg, dq, dk, dv):
    inner = ow.shape[0]
    groups, share = inner // 128, 128 // depth
    lanes = lane_head(length, depth)
    low = first_grad[...].astype(bf16)
    dow_o[...] = contract_rows(mixed[...], low).astype(bf16)
    mixg[...] = contract_cols(low, ow[...]).astype(bf16)

    def body(group, carry):
        cols = pl.ds(pl.multiple_of(group * 128, 128), 128)
        total = [jnp.zeros((length, length), f32) for _ in range(share)]
        for micro in range(tok.shape[0] // length):
            rows = slice(micro * length, (micro + 1) * length)
            qs, ks, vs, o = q[rows, cols], k[rows, cols], v[rows, cols], mixg[rows, cols]
            q_grad = jnp.zeros((length, 128), f32)
            k_grad = jnp.zeros((length, 128), f32)
            v_grad = jnp.zeros((length, 128), f32)
            for a in range(share):
                qa, oa = jnp.where(lanes == a, qs, 0), jnp.where(lanes == a, o, 0)
                s = contract_cols(qa, ks) + bias[group * share + a]
                e = jnp.exp(s - jnp.max(s, axis=-1, keepdims=True))
                p = e / jnp.sum(e, axis=-1, keepdims=True)
                v_grad += contract_rows(p.astype(bf16), oa)
                dp = contract_cols(oa, vs)
                ds = (p * (dp - jnp.sum(p * dp, axis=-1, keepdims=True))).astype(bf16)
                total[a] = total[a] + ds.astype(f32)
                q_grad = jnp.where(lanes == a, matmul(ds, ks), q_grad)
                k_grad += contract_rows(ds, qa)
            dq[rows, cols] = q_grad.astype(bf16)
            dk[rows, cols] = k_grad.astype(bf16)
            dv[rows, cols] = v_grad.astype(bf16)
        for a in range(share):
            ds_o[group * share + a] = total[a]
        return carry

    lax.fori_loop(0, groups, body, 0)
    dqw_o[...] = contract_rows(dq[...], normed[...]).astype(bf16)
    dkw_o[...] = contract_rows(dk[...], normed[...]).astype(bf16)
    dvw_o[...] = contract_rows(dv[...], normed[...]).astype(bf16)
    up = matmul(dq[...], qw[...]) + matmul(dk[...], kw[...]) + matmul(dv[...], vw[...])
    part, gain = norm_back_rows(tok[...].astype(f32), g1[...], up)
    g1_o[...] = gain
    ing_o[...] = first_grad[...] + part


def self_bwd(depth, length, first_grad, mixed, q, k, v, bias, ow, qw, kw, vw, normed, tok, g1):
    rows, width = tok.shape
    weight = jax.ShapeDtypeStruct(ow.shape, bf16)
    return pl.pallas_call(
        functools.partial(self_bwd_kernel, depth, length),
        out_shape=(
            weight,
            weight,
            weight,
            weight,
            jax.ShapeDtypeStruct((rows, width), f32),
            jax.ShapeDtypeStruct((1, width), f32),
            jax.ShapeDtypeStruct(bias.shape, f32),
        ),
        scratch_shapes=[pltpu.VMEM(q.shape, bf16)] * 4,
        compiler_params=params(42),
        cost_estimate=cost(21),
        name="self_bwd",
    )(first_grad, mixed, q, k, v, bias, ow, qw, kw, vw, normed, tok, g1)


def kv_fwd_kernel(place, source, kw, vw, *outs):
    rows = source[0, 0]
    both = [
        lax.dot_general(rows, w[...], (((0,), (1,)), ((), ())), preferred_element_type=f32).astype(bf16)
        for w in (kw, vw)
    ]
    for s, out in enumerate(outs):

        @pl.when(pl.program_id(0) == s)
        def write(out=out):
            out[0] = jnp.concatenate(both, axis=1)


def kv_fwd(place, memory, kw, vw):
    micros, pairs, width, slots = memory.shape
    inner = kw.shape[0]
    whole = pl.BlockSpec((inner, width), lambda s, m, place: (0, 0))
    return pl.pallas_call(
        kv_fwd_kernel,
        grid_spec=pltpu.PrefetchScalarGridSpec(
            num_scalar_prefetch=1,
            grid=(pairs, micros),
            in_specs=[
                pl.BlockSpec((1, 1, width, slots), lambda s, m, place: (m, place[s], 0, 0)),
                whole,
                whole,
            ],
            out_specs=[
                pl.BlockSpec(
                    (1, slots, 2 * inner),
                    lambda s, m, place, t=t: (jnp.where(s < t, 0, jnp.where(s == t, m, micros - 1)), 0, 0),
                )
                for t in range(pairs)
            ],
        ),
        out_shape=[jax.ShapeDtypeStruct((micros, slots, 2 * inner), bf16)] * pairs,
        compiler_params=params(20),
        cost_estimate=cost(9),
        name="kv_fwd",
    )(place, memory, kw, vw)


def kv_weights_kernel(place, source, *refs):
    kvgs, (dkw_o, dvw_o, acc) = refs[:-3], refs[-3:]
    inner = dkw_o.shape[0]
    pair = pl.program_id(0)
    step = pair * pl.num_programs(1) + pl.program_id(1)

    @pl.when(step == 0)
    def clear():
        acc[...] = jnp.zeros_like(acc)

    grads = kvgs[0][0]
    for t in range(1, len(kvgs)):
        grads = jnp.where(pair == t, kvgs[t][0], grads)
    acc[...] += lax.dot_general(
        grads, source[0, 0], (((0,), (1,)), ((), ())), preferred_element_type=f32
    )

    @pl.when(step == pl.num_programs(0) * pl.num_programs(1) - 1)
    def write():
        dkw_o[...] = acc[:inner].astype(bf16)
        dvw_o[...] = acc[inner:].astype(bf16)


def kv_memory_kernel(place, kw, vw, *refs):
    kvgs, out = refs[:-1], refs[-1]
    inner = kw.shape[0]
    pair = pl.program_id(0)
    grads = kvgs[0][0]
    for t in range(1, len(kvgs)):
        grads = jnp.where(pair == t, kvgs[t][0], grads)
    out[0, 0] = lax.dot_general(
        kw[...], grads[:, :inner], (((0,), (1,)), ((), ())), preferred_element_type=f32
    ) + lax.dot_general(
        vw[...], grads[:, inner:], (((0,), (1,)), ((), ())), preferred_element_type=f32
    )


def kv_specs(pairs, micros, slots, inner, width):
    whole = pl.BlockSpec((inner, width), lambda s, m, place: (0, 0))
    block = pl.BlockSpec((1, 1, width, slots), lambda s, m, place: (m, place[s], 0, 0))
    pieces = [
        pl.BlockSpec(
            (1, slots, 2 * inner),
            lambda s, m, place, t=t: (jnp.where(s < t, 0, jnp.where(s == t, m, micros - 1)), 0, 0),
        )
        for t in range(pairs)
    ]
    return whole, block, pieces


def kv_weights(place, memory, kvgs, inner):
    micros, pairs, width, slots = memory.shape
    whole, block, pieces = kv_specs(pairs, micros, slots, inner, width)
    weight = jax.ShapeDtypeStruct((inner, width), bf16)
    return pl.pallas_call(
        kv_weights_kernel,
        grid_spec=pltpu.PrefetchScalarGridSpec(
            num_scalar_prefetch=1,
            grid=(pairs, micros),
            in_specs=[block, *pieces],
            out_specs=(whole, whole),
            scratch_shapes=[pltpu.VMEM((2 * inner, width), f32)],
        ),
        out_shape=(weight, weight),
        compiler_params=params(24),
        cost_estimate=cost(9),
        name="kv_weights",
    )(place, memory, *kvgs)


def kv_memory(place, shape, kw, vw, kvgs):
    micros, pairs, width, slots = shape
    inner = kw.shape[0]
    whole, block, pieces = kv_specs(pairs, micros, slots, inner, width)
    return pl.pallas_call(
        kv_memory_kernel,
        grid_spec=pltpu.PrefetchScalarGridSpec(
            num_scalar_prefetch=1,
            grid=(pairs, micros),
            in_specs=[whole, whole, *pieces],
            out_specs=block,
        ),
        out_shape=jax.ShapeDtypeStruct(shape, f32),
        compiler_params=params(20),
        cost_estimate=cost(10),
        name="kv_memory",
    )(place, kw, vw, *kvgs)


gelu_c = math.sqrt(2 / math.pi)


def plan(steps):
    arrays, out = [], []
    for buffers in steps:
        out.append([])
        for n, sources in enumerate(buffers):
            at = 0
            for array, index, rows in sources:
                found = [i for i, known in enumerate(arrays) if known is array]
                if not found:
                    arrays.append(array)
                out[-1].append((found[0] if found else len(arrays) - 1, index, n, at, rows))
                at += rows
    return arrays, out


def fetch(places, refs, hold, sems, step, slot):
    copies = []
    for i, (which, index, n, at, rows) in enumerate(places[step]):
        src = refs[which].at[index] if index else refs[which]
        copies.append(pltpu.make_async_copy(src, hold.at[slot, n, pl.ds(at, rows)], sems.at[slot, i]))
    return copies


def run_fetch(places, refs, hold, sems):
    step = pl.program_id(0)
    for i in range(len(places)):

        @pl.when(step == i)
        def move(i=i):
            if i == 0:
                for copy in fetch(places, refs, hold, sems, 0, 0):
                    copy.start()
            if i + 1 < len(places):
                for copy in fetch(places, refs, hold, sems, i + 1, (i + 1) % 2):
                    copy.start()
            for copy in fetch(places, refs, hold, sems, i, i % 2):
                copy.wait()


def feed_grad_kernel(places, count, mems, *refs):
    nf_a, nf_b, og_a, og_b = refs[:4]
    weights = refs[4 : 4 + count]
    split = 2 if mems else 1
    dgw_o, dlw_o = refs[4 + count : 4 + count + split], refs[4 + count + split : 4 + count + 2 * split]
    steps = len(places)
    ddw_o = refs[4 + count + 2 * split : 4 + count + 2 * split + steps]
    hid_o, gl_o, ll_o, nf, og, hold, sems, whole_sems = refs[4 + count + 2 * split + steps :]
    rows = nf_a.shape[0]
    step = pl.program_id(0)

    def loads():
        return [
            pltpu.make_async_copy(src, dst.at[pl.ds(at, rows)], whole_sems.at[i])
            for i, (src, dst, at) in enumerate([(nf_a, nf, 0), (nf_b, nf, rows), (og_a, og, 0), (og_b, og, rows)])
        ]

    @pl.when(step == 0)
    def load():
        for copy in loads():
            copy.start()

    run_fetch(places, weights, hold, sems)

    @pl.when(step == 0)
    def loaded():
        for copy in loads():
            copy.wait()

    slot = lax.rem(step, 2)
    x, up = nf[...], og[...]
    g = contract_cols(x, hold[slot, 0])
    lin = contract_cols(x, hold[slot, 1])
    hg = contract_cols(up, hold[slot, 2])
    t = jnp.tanh(gelu_c * (g + 0.044715 * (g * g * g)))
    act = 0.5 * g * (1.0 + t)
    slope = 0.5 * (1.0 + t) + 0.5 * g * (1.0 - t * t) * (gelu_c * (1.0 + 3 * 0.044715 * (g * g)))
    hidden = (act * lin).astype(bf16)
    gl = (hg * lin * slope).astype(bf16)
    ll = (hg * act).astype(bf16)
    hid_o[0] = hidden
    gl_o[0] = gl
    ll_o[0] = ll
    for outs, upstream, bit in ((dgw_o, gl, mems // 2), (dlw_o, ll, 1)):
        grad = contract_rows(upstream, x).astype(bf16)
        if not mems:
            outs[0][0] = grad
            continue
        part = grad.shape[0] // mems
        for k in range(mems):
            at = [i for i in range(mems) if (i & bit) == (k & bit)].index(k)
            outs[1 if k & bit else 0][0, at] = grad[k * part : (k + 1) * part]
    down_grad = contract_rows(hidden, up).astype(bf16)

    for i, out in enumerate(ddw_o):

        @pl.when(step == i)
        def write(out=out):
            out[...] = down_grad


def feed_grad(nf_a, nf_b, og_a, og_b, steps, block, mems):
    rows, width = nf_a.shape
    weights, places = plan(steps)
    n = len(steps)
    any_spec = pl.BlockSpec(memory_space=pl.ANY)
    tile = pl.BlockSpec((1, block, width), lambda i: (i, 0, 0))
    column = pl.BlockSpec((1, 2 * rows, block), lambda i: (i, 0, 0))
    weight = jax.ShapeDtypeStruct((n, block, width), bf16)
    act = jax.ShapeDtypeStruct((n, 2 * rows, block), bf16)
    half_tile, half = tile, weight
    if mems:
        half_tile = pl.BlockSpec((1, mems // 2, block // mems, width), lambda i: (i, 0, 0, 0))
        half = jax.ShapeDtypeStruct((n, mems // 2, block // mems, width), bf16)
    count = 4 if mems else 2
    return pl.pallas_call(
        functools.partial(feed_grad_kernel, places, len(weights), mems),
        grid=(n,),
        in_specs=[any_spec] * (4 + len(weights)),
        out_specs=(
            *[half_tile] * count,
            *[pl.BlockSpec((block, width), lambda i: (0, 0))] * n,
            column,
            column,
            column,
        ),
        out_shape=(
            *[half] * count,
            *[jax.ShapeDtypeStruct((block, width), bf16)] * n,
            act,
            act,
            act,
        ),
        scratch_shapes=[
            pltpu.VMEM((2 * rows, width), bf16),
            pltpu.VMEM((2 * rows, width), bf16),
            pltpu.VMEM((2, 3, block, width), bf16),
            pltpu.SemaphoreType.DMA((2, max(len(p) for p in places))),
            pltpu.SemaphoreType.DMA((4,)),
        ],
        compiler_params=params(54),
        cost_estimate=cost(13 * n),
        name="feed_grad",
    )(nf_a, nf_b, og_a, og_b, *weights)


def feed_out_kernel(places, act_places, count, act_count, *refs):
    weights, acts = refs[:count], refs[count : count + act_count]
    nfg_o, nfg_b, res_o, res_b, res_t, nfg_t, hold, acts_hold, sems, act_sems = refs[count + act_count :]
    step = pl.program_id(0)
    rows = nfg_o.shape[0]
    run_fetch(places, weights, hold, sems)
    run_fetch(act_places, acts, acts_hold, act_sems)
    slot = lax.rem(step, 2)
    nfg = matmul(acts_hold[slot, 0], hold[slot, 0]) + matmul(acts_hold[slot, 1], hold[slot, 1])
    res = matmul(acts_hold[slot, 2], hold[slot, 2])

    @pl.when(step == 0)
    def first():
        res_o[...] = res[:rows]
        res_t[...] = res[rows:]
        nfg_o[...] = nfg[:rows]
        nfg_t[...] = nfg[rows:]

    @pl.when(step > 0)
    def later():
        res_o[...] += res[:rows]
        res_t[...] += res[rows:]
        nfg_o[...] += nfg[:rows]
        nfg_t[...] += nfg[rows:]

    @pl.when(step == pl.num_programs(0) - 1)
    def last():
        res_b[...] = res_t[...].astype(bf16)
        nfg_b[...] = nfg_t[...].astype(bf16)


def feed_out(rows, width, steps, act_steps, block):
    weights, places = plan(steps)
    acts, act_places = plan(act_steps)
    whole = pl.BlockSpec((rows, width), lambda i: (0, 0))
    wide, low = jax.ShapeDtypeStruct((rows, width), f32), jax.ShapeDtypeStruct((rows, width), bf16)
    return pl.pallas_call(
        functools.partial(feed_out_kernel, places, act_places, len(weights), len(acts)),
        grid=(len(steps),),
        in_specs=[pl.BlockSpec(memory_space=pl.ANY)] * (len(weights) + len(acts)),
        out_specs=(whole, whole, whole, whole),
        out_shape=(wide, low, wide, low),
        scratch_shapes=[
            pltpu.VMEM((rows, width), f32),
            pltpu.VMEM((rows, width), f32),
            pltpu.VMEM((2, 3, block, width), bf16),
            pltpu.VMEM((2, 3, 2 * rows, block), bf16),
            pltpu.SemaphoreType.DMA((2, max(len(p) for p in places))),
            pltpu.SemaphoreType.DMA((2, max(len(p) for p in act_places))),
        ],
        compiler_params=params(54),
        cost_estimate=cost(30),
        name="feed_out",
    )(*weights, *acts)


def joined(value):
    return jnp.concatenate(value) if isinstance(value, list) else value


def fuse(fn, *arrays, limit=0):
    shapes = jax.eval_shape(lambda *a: [joined(o) for o in fn(*a)], *arrays)
    if any(a.shape[-2] % 16 for a in (*arrays, *shapes)):
        return [joined(o) for o in fn(*arrays)]

    limit = limit or 6 + sum(math.prod(a.shape) for a in (*arrays, *shapes)) * 4 // 2**20

    def kernel(*refs):
        for out, value in zip(refs[len(arrays) :], fn(*[ref[...] for ref in refs[: len(arrays)]])):
            at = 0
            for piece in value if isinstance(value, list) else [value]:
                out[at : at + piece.shape[0]] = piece
                at += piece.shape[0]

    return pl.pallas_call(
        kernel, out_shape=shapes, compiler_params=params(limit), cost_estimate=cost(3), name="fuse"
    )(*arrays)


def core_split_kernel(spot, *refs):
    grads, (kept, sent) = refs[:-2], refs[-2:]
    core = spot[0]
    for i, grad in enumerate(grads):
        for z in range(grad.shape[0]):
            kept[z, i] = grad[z, core]
            sent[z, i] = grad[z, 1 - core]


def core_split(spot, grads):
    chips, _, slim, width = grads[0].shape
    shape = jax.ShapeDtypeStruct((chips, len(grads), slim, width), bf16)
    return pl.pallas_call(
        core_split_kernel,
        in_specs=[pl.BlockSpec(memory_space=pltpu.SMEM)] + [pl.BlockSpec(memory_space=pltpu.VMEM)] * len(grads),
        out_shape=(shape, shape),
        compiler_params=params(60),
        cost_estimate=cost(4),
        name="core_split",
    )(spot, *grads)


def columns_kernel(spot, kept, moved, *outs):
    chips = kept.shape[0]
    for k, out in enumerate(outs):
        for z in range(chips):
            out[z] = add_low(kept[z, spot[2 + k]], moved[z, spot[2 + k]])


def columns_of(spot, kept, moved, mems):
    chips, count, slim, width = kept.shape
    if count != mems:
        total = add_low(kept, moved).reshape(chips, mems, -1, width)
        return [lax.dynamic_index_in_dim(total, spot[2 + k], 1, keepdims=False) for k in range(mems)]
    vmem = pl.BlockSpec(memory_space=pltpu.VMEM)
    return pl.pallas_call(
        columns_kernel,
        in_specs=[pl.BlockSpec(memory_space=pltpu.SMEM), vmem, vmem],
        out_shape=[jax.ShapeDtypeStruct((chips, slim, width), bf16)] * mems,
        compiler_params=params(18),
        cost_estimate=cost(4),
        name="columns",
    )(spot, kept, moved)


def tree_sum(values):
    while len(values) > 1:
        values = [left + right for left, right in zip(values[::2], values[1::2])]
    return values[0]


def tie(*values):
    return lax.optimization_barrier(values)


def fold_parts(held, order, bit):
    keep = [i for i, k in enumerate(order) if not k & bit]
    send = [order.index(order[i] | bit) for i in keep]
    return [jnp.stack([held[:, i] for i in at], axis=1) for at in (keep, send)]


def fold_step(held, order, bit):
    kept, sent = fold_parts(held, order, bit)
    return kept, to_mem(sent, bit), [k for k in order if not k & bit]


def per_device(
    inputs,
    memory,
    memory_lengths,
    keep_mask,
    norm_self,
    query_self,
    key_self,
    value_self,
    output_self,
    bias_table,
    norm_cross,
    query_cross,
    key_cross,
    value_cross,
    output_cross,
    norm_feed,
    gate_feed,
    linear_feed,
    down_feed,
    output_grad,
):
    micros = inputs.shape[0]
    length = inputs.shape[3]
    width = inputs.shape[4]
    pairs = memory.shape[2]
    slots = memory.shape[3]
    heads = bias_table.shape[1]
    buckets = bias_table.shape[0]
    seqs = lax.axis_size("seq")
    mems = lax.axis_size("mem")
    chips = seqs // 2
    slim = query_self.shape[1]
    inner = slim * seqs
    depth = inner // heads
    feed = gate_feed.shape[1]
    part = feed // mems
    rows = micros * length
    seq_index = lax.axis_index("seq")
    core = seq_index % 2
    chip = seq_index // 2
    mem_index = lax.axis_index("mem")
    gain_self = norm_self.astype(f32)
    gain_cross = norm_cross.astype(f32)
    gain_feed = norm_feed.astype(f32)


    bits = mem_bits()
    spot = jnp.stack([core, chip] + [mem_index ^ q for q in range(mems)]).astype(jnp.int32)

    def quarters(shard):
        shard = shard.reshape(mems, shard.shape[0] // mems, width)
        return jnp.stack(
            [lax.dynamic_index_in_dim(shard, mem_index ^ k, 0, keepdims=False) for k in range(mems)]
        )

    last = chips - 1
    early = list(range(1, last))

    def matrices(held, other):
        full = assemble(spot, held, other)
        if mems == 4:
            return [full[i].reshape(inner, width) for i in range(4)]
        full = jnp.stack(full).reshape(4, mems // 4, seqs, -1, width).transpose(0, 2, 1, 3, 4)
        return list(full.reshape(4, inner, width))

    def hold_plane(pack, moved):
        return jnp.concatenate([pack[None], jnp.stack(moved, axis=1)], axis=0)

    first_pack = quarters(jnp.concatenate([key_cross.T, value_cross.T, query_self.T, key_self.T], axis=0))
    second_pack = quarters(
        jnp.concatenate([value_self.T, output_self, query_cross.T, output_cross], axis=0)
    )
    gate_own, linear_own, down_own = quarters(gate_feed.T), quarters(linear_feed.T), quarters(down_feed)
    both = [jnp.stack([gate_own[0], linear_own[0]])]
    down = [down_own]

    onehot = (
        position_buckets(length).reshape(length * length, 1)
        == jnp.arange(buckets, dtype=jnp.int32)[None, :]
    ).astype(bf16)
    position_bias = (
        jnp.dot(onehot, bias_table, preferred_element_type=f32)
        .reshape(length, length, heads)
        .transpose(2, 0, 1)
    )
    row_index = jnp.arange(length, dtype=jnp.int32)
    causal = row_index[:, None] >= row_index[None, :]
    position_bias = jnp.where(causal[None], position_bias, masked_score)
    og_low = output_grad.reshape(rows, width)
    gain_self, gain_cross, gain_feed = [g.reshape(1, width) for g in (gain_self, gain_cross, gain_feed)]
    spots = jnp.stack(
        [(mem_index ^ s) * slots + jnp.arange(slots, dtype=jnp.int32) for s in range(mems)], 0
    )
    len_own = lax.dynamic_index_in_dim(memory_lengths[:, 0], mem_index, 1, keepdims=False)
    place = spot[2:]
    source = memory.reshape(micros, pairs, slots, width).swapaxes(2, 3)
    both_packs = jnp.stack([first_pack[0], second_pack[0]])
    moved = [to_step(both_packs, j) for j in range(1, chips)]
    og_other = rows_to_core(og_low)
    keep_all = lax.all_gather(keep_mask[:, 0], "mem", axis=0)
    moved, both[0], og_other, keep_all = tie(moved, both[0], og_other, keep_all)
    keep_own = lax.dynamic_index_in_dim(keep_all, mem_index, 2, keepdims=False)
    keep_own = jnp.stack(
        [lax.dynamic_index_in_dim(keep_own, mem_index ^ s, 0, keepdims=False) for s in range(mems)], 1
    )
    valid = (spots[None] < len_own[:, None, None]) & ((keep_own == 1) | (spots[None] == 0))
    valid = valid.reshape(micros, 1, mems * slots).astype(f32)


    first_parts, second_parts = fuse(
        lambda *m: [[p[:1] for p in m], [p[1:] for p in m]], *moved
    )
    first_parts, second_parts = first_parts[None], second_parts[None]
    first_order, second_order = [0], [0]
    for first_bit, second_bit in zip(bits, bits[::-1]):
        first_more, second_more = to_mem(first_parts, first_bit), to_mem(second_parts, second_bit)
        first_order = first_order + [k | first_bit for k in first_order]
        second_order = second_order + [k | second_bit for k in second_order]
        if len(both) < last:
            both.append(to_next(both[-1]))
        first_more, second_more, both[-1] = tie(first_more, second_more, both[-1])
        first_parts = jnp.concatenate([first_parts, first_more])
        second_parts = jnp.concatenate([second_parts, second_more])
    while len(both) < last:
        both.append(to_next(both[-1]))

    def hold_parts(pack, parts, order):
        spread = jnp.stack([parts[order.index(k)] for k in range(mems)], axis=1)
        return jnp.concatenate([pack[None], spread], axis=0)

    first_held = hold_parts(first_pack, first_parts, first_order)
    first_more = to_core(first_held)
    gate_early = jnp.stack([both[j][0] for j in early])[None]
    linear_early = jnp.stack([both[j][1] for j in early])[None]
    gate_a1 = to_mem(gate_early, bits[0])
    linear_a1 = to_mem(linear_early, bits[-1])
    both.append(to_next(both[-1]))
    second_held = hold_parts(second_pack, second_parts, second_order)
    first_more, gate_a1, linear_a1, both[last], second_held = tie(
        first_more, gate_a1, linear_a1, both[last], second_held
    )

    second_more = to_core(second_held)
    gate_late, linear_late = both[last][:1], both[last][1:]
    gate_late_a1 = to_mem(gate_late, bits[0])
    linear_late_a1 = to_mem(linear_late, bits[-1])
    first_mats = matrices(first_held, first_more)
    kc_full, vc_full, qs_full, ks_full = first_mats
    kv_local = kv_fwd(place, source, kc_full, vc_full)
    gate_early = jnp.concatenate([gate_early, gate_a1])
    linear_early = jnp.concatenate([linear_early, linear_a1])
    kv_local, second_more, gate_late_a1, linear_late_a1, down[0], gate_early, linear_early = tie(
        kv_local, second_more, gate_late_a1, linear_late_a1, down[0], gate_early, linear_early
    )

    kvs = [to_mem(kv_local[s], s) if s else kv_local[s] for s in range(mems)]
    down.append(to_next(down[0]))
    second_mats = matrices(second_held, second_more)
    vs_full, os_full, qc_full, oc_full = second_mats
    tokens, normed, q, k, v, mixed, first_sum, normed_cross, cq = self_fwd(
        depth, length, inputs.reshape(micros, length, width).swapaxes(1, 2), gain_self, qs_full, ks_full, vs_full, os_full, position_bias, gain_cross, qc_full
    )
    kvs, down[1], cq, gate_early, linear_early = tie(kvs, down[1], cq, gate_early, linear_early)

    def spread_rest(held, order, over):
        parts = [held]
        for bit in over:
            parts.append(to_mem(jnp.concatenate(parts) if len(parts) > 1 else parts[0], bit))
            order = order + [k | bit for k in order]
        return parts, order

    gate_parts, gate_order = spread_rest(gate_early, [0, bits[0]], bits[1:])
    linear_parts, linear_order = spread_rest(linear_early, [0, bits[-1]], bits[::-1][1:])
    gate_late = jnp.concatenate([gate_late, gate_late_a1])
    linear_late = jnp.concatenate([linear_late, linear_late_a1])
    for _ in early[1:]:
        down.append(to_next(down[-1]))
    cmixed, second_sum, normed_feed = cross_fwd(depth, length, cq, valid, oc_full, first_sum, gain_feed, kvs)
    gate_parts, linear_parts, gate_late, linear_late, down[1:], normed_feed = tie(
        gate_parts, linear_parts, gate_late, linear_late, down[1:], normed_feed
    )

    def sources(parts, order, n):
        places = {}
        at = 0
        for piece in parts:
            for i in range(piece.shape[0]):
                places[order[at]] = (piece, (i, n) if piece.ndim == 4 else (i,), part)
                at += 1
        return [places[k] for k in range(mems)]

    def whole_source(array, listed):
        if part % 16 == 0:
            return listed
        pieces = []
        for piece, index, _ in listed:
            for i in index:
                piece = piece[i]
            pieces.append(piece)
        return [(jnp.concatenate(pieces), (), feed)]

    own_steps = [[(g.reshape(feed, width), (), feed)] for g in (gate_own, linear_own, down_own)]
    early_steps = [
        [
            whole_source(None, sources(gate_parts, gate_order, n)),
            whole_source(None, sources(linear_parts, linear_order, n)),
            [(down[j].reshape(feed, width), (), feed)],
        ]
        for n, j in enumerate(early)
    ]
    nf_other = rows_to_core(normed_feed)
    gate_late_parts, gate_order = spread_rest(gate_late, [0, bits[0]], bits[1:])
    linear_late_parts, linear_order = spread_rest(linear_late, [0, bits[-1]], bits[::-1][1:])
    down.append(to_next(down[-1]))
    whole_bits = mems if mems == 4 and part % 16 == 0 else 0
    grads_a = feed_grad(normed_feed, nf_other, og_low, og_other, early_steps + [own_steps], feed, whole_bits)
    grads_a, gate_late_parts, linear_late_parts, down[last], nf_more = tie(
        grads_a, gate_late_parts, linear_late_parts, down[last], nf_other
    )

    natural_order = list(range(mems))
    gate_ord = [k for k in natural_order if not k & bits[-1]]
    linear_ord = [k for k in natural_order if not k & bits[0]]

    def halves(grads):
        if whole_bits:
            return (grads[0:2], grads[2:4], grads[4:-3], *grads[-3:])
        shape = (-1, mems, part, width)
        return (
            fold_parts(grads[0].reshape(shape), natural_order, bits[-1]),
            fold_parts(grads[1].reshape(shape), natural_order, bits[0]),
            grads[2:-3],
            *grads[-3:],
        )

    (gate_keep, gate_send), (linear_keep, linear_send), grad_down_a, *acts_a = halves(grads_a)
    down_total = to_next(grad_down_a[0])
    gate_moved = to_mem(gate_send, bits[-1])
    linear_moved = to_mem(linear_send, bits[0])
    late_steps = [
        [
            whole_source(None, sources(gate_late_parts, gate_order, 0)),
            whole_source(None, sources(linear_late_parts, linear_order, 0)),
            [(down[last].reshape(feed, width), (), feed)],
        ]
    ]
    grads_b = feed_grad(normed_feed, nf_more, og_low, og_other, late_steps, feed, whole_bits)
    (gate_b, gate_bs), (linear_b, linear_bs), (grad_down_b,), *acts_b = halves(grads_b)
    act_steps = [
        [[(acts[i], (n,), 2 * rows)] for i in (1, 2, 0)]
        for acts, count in ((acts_a, last), (acts_b, 1))
        for n in range(count)
    ]
    nfg_own, nfg_send, res_own, res_send = feed_out(
        rows, width, early_steps + [own_steps] + late_steps, act_steps, feed
    )
    gate_moved, linear_moved, down_total, nfg_send, gate_bs, linear_bs = tie(
        gate_moved, linear_moved, down_total, nfg_send, gate_bs, linear_bs
    )

    def fold_to_last(held, order, over):
        for bit in over[:-1]:
            kept, moved, order = fold_step(held, order, bit)
            held = add_low(kept, moved)
        return held

    down_next = down_total
    for j in early[1:]:
        down_next = to_next(add_low(down_next, grad_down_a[j - 1]))
    nfg_more = rows_to_core(nfg_send)
    half = mems // 2
    if len(bits) == 2:
        both_y = fuse(
            lambda gk, gm, lk, lm: [
                add_low(gk[:, 0], gm[:, 0]),
                add_low(gk[:, 1], gm[:, 1]),
                add_low(lk[:, 0], lm[:, 0]),
                add_low(lk[:, 1], lm[:, 1]),
            ],
            gate_keep, gate_moved, linear_keep, linear_moved,
        )
    else:
        gate_y = fold_to_last(add_low(gate_keep, gate_moved), gate_ord, bits[::-1][1:])
        linear_y = fold_to_last(add_low(linear_keep, linear_moved), linear_ord, bits[1:])
        both_y = [gate_y[:, 0], gate_y[:, 1], linear_y[:, 0], linear_y[:, 1]]
    message_y, message_x = fuse(
        lambda gs, ly, ls, gy: [[gs[0], ly], [ls[0], gy]], gate_bs, both_y[3], linear_bs, both_y[1]
    )
    message_y, message_x = to_mem(message_y, bits[-1]), to_mem(message_x, bits[0])
    kvg, (grad_gain_feed, grad_co, grad_cq, first_grad, grad_gain_cross) = cross_bwd(
        depth, length, og_low, nfg_own, nfg_more, second_sum, gain_feed, cmixed, cq, valid, oc_full,
        first_sum, gain_cross, normed_cross, qc_full, kvs,
    )
    message_y, message_x, down_next, kvg, grad_gain_cross, res_send = tie(
        message_y, message_x, down_next, kvg, grad_gain_cross, res_send
    )

    kvg = [to_mem(kvg[s], s) if s else kvg[s] for s in range(mems)]
    shards = (mems, part, width)
    own = last - 1
    gate_y, linear_y, both_own, ring = fuse(
        lambda g, x, l, y, d, b: [
            add_low(g[:own], x[half:-1]),
            add_low(l[:own], y[half:-1]),
            [add_low(g[own:], x[-1:]), add_low(l[own:], y[-1:])],
            [add_low(d, b), add_low(g[:1], x[half : half + 1]), add_low(l[:1], y[half : half + 1])],
        ],
        both_y[0], message_x, both_y[2], message_y, down_next.reshape(shards), grad_down_b.reshape(shards),
    )
    ring = to_next(ring)
    res_more = rows_to_core(res_send)
    grad_os, grad_qs, grad_ks, grad_vs, input_grad, grad_gain_self, score_sum = self_bwd(
        depth, length, first_grad, mixed, q, k, v, position_bias, os_full, qs_full, ks_full, vs_full,
        normed, tokens, gain_self,
    )
    kvg, ring, grad_qs, res_more = tie(kvg, ring, grad_qs, res_more)

    kept, sent = core_split(
        spot, [g.reshape(chips, 2, slim, width) for g in (grad_qs, grad_ks, grad_vs, grad_os)]
    )
    sent = to_core(sent)
    for j in early[1:-1]:
        ring_both = to_next(add_low(ring[mems:], jnp.stack([gate_y[j - 1], linear_y[j - 1]])))
        ring = jnp.concatenate([ring[:mems], ring_both])
    gate_b, linear_b = gate_b[0], linear_b[0]
    gate_bm, linear_bm = message_y, message_x
    if len(bits) > 2:
        gate_bm, linear_bm = message_y[:half], message_x[:half]
        gate_b = fold_to_last(add_low(gate_b, gate_bm)[None], gate_ord, bits[::-1][1:])[0]
        linear_b = fold_to_last(add_low(linear_b, linear_bm)[None], linear_ord, bits[1:])[0]
        gate_bm, linear_bm = jnp.zeros_like(gate_b), jnp.zeros_like(linear_b)
    at = early[-1] - 1
    parts = fuse(
        lambda r, g, l, gb, gm, lb, lm, d: [
            [add_low(r[mems : mems + 1], g[at : at + 1]), add_low(r[mems + 1 :], l[at : at + 1])],
            add_low(gb[:1], gm[:1]),
            add_low(lb[:1], lm[:1]),
            [add_low(gb[1:2], gm[1:2]), add_low(r[1:2], d[1:2])],
            [add_low(lb[1:2], lm[1:2]), add_low(r[half : half + 1], d[half : half + 1])],
            add_low(r[:1], d[:1]),
            *[add_low(r[k : k + 1], d[k : k + 1]) for k in range(1, mems) if k not in (1, half)],
        ],
        ring, gate_y, linear_y, gate_b, gate_bm, linear_b, linear_bm, grad_down_a[last - 1].reshape(shards),
        limit=60,
    )
    ring_both, gate_bk, linear_bk, message_x, message_y, down_mine, *down_rest = parts
    others = [k for k in range(1, mems) if k not in (1, half)]
    ring_both = to_next(ring_both)
    message_x, message_y = to_mem(message_x, bits[0]), to_mem(message_y, bits[-1])
    down_rest = [to_mem(p, k) for p, k in zip(down_rest, others)]

    def grad_sums(*grads):
        stacked = jnp.stack([g.reshape(seqs, slim, width) for g in grads], axis=1)
        return lax.psum_scatter(stacked.reshape(seqs, len(grads) * slim, width), "seq", scatter_dimension=0)

    cross_first = grad_sums(after(grad_cq, ring), grad_co)
    grad_kc, grad_vc = kv_weights(place, source, kvg, inner)
    sent, ring_both, message_x, message_y, down_rest, grad_kc, kvg[0] = tie(
        sent, ring_both, message_x, message_y, down_rest, grad_kc, kvg[0]
    )

    columns = columns_of(spot, kept, sent, mems)
    columns = [to_mem(p, s) if s else p for s, p in enumerate(columns)]
    ring_both, down_sum = fuse(
        lambda r, g, x, l, y, d, *more: [
            [add_low(r[:1], add_low(g, x[:1])), add_low(r[1:], add_low(l, y[:1]))],
            sum_low([d, x[1:], y[1:], *more]),
        ],
        ring_both, gate_bk, message_x, linear_bk, message_y, down_mine, *down_rest,
    )
    ring_both = to_next(ring_both)
    cross_sum = [grad_sums(grad_kc, grad_vc), cross_first]
    memory_grad = kv_memory(place, source.shape, kc_full, vc_full, kvg)
    score_sum, input_grad, res_more = [after(x, columns[1]) for x in (score_sum, input_grad, res_more)]
    grad_table = lax.dot_general(
        onehot.astype(f32),
        score_sum.reshape(heads, length * length),
        (((0,), (1,)), ((), ())),
        preferred_element_type=f32,
    )
    table_row = jnp.pad(grad_table.reshape(1, buckets * heads), ((0, 0), (0, width - buckets * heads)))
    small = jnp.concatenate([grad_gain_self, grad_gain_cross, grad_gain_feed, table_row], axis=0)

    def to_rows(value):
        high = value.astype(bf16)
        rest = (value - high.astype(f32)).astype(bf16)
        return jnp.concatenate([high, rest, jnp.zeros((16 - 2 * value.shape[0], width), bf16)])

    def from_rows(value):
        return value[:4].astype(f32) + value[4:8].astype(f32)

    small_rows = to_rows(small)
    columns, ring_both, small_rows, memory_grad = tie(columns, ring_both, small_rows, memory_grad)

    share = 4 * slim // mems
    total = sum_low(columns).reshape(chips, share, width)
    pieces = [
        jnp.concatenate([lax.dynamic_index_in_dim(total, (chip + j) % chips, 0, keepdims=False), small_rows])
        for j in range(chips)
    ]
    pieces = [to_step(p, j) if j else p for j, p in enumerate(pieces)]
    both_sum, message_x, message_y = fuse(
        lambda r, g, d: [add_low(r, g), [add_low(r[:1], g[:1]), d], [add_low(r[1:], g[1:]), d]],
        ring_both, both_own, down_sum,
    )
    message_x, message_y = to_mem(message_x, bits[0]), to_mem(message_y, bits[-1])
    down_rest = [to_mem(down_sum, k) for k in range(1, mems) if k not in (1, half)]
    pieces, message_x, message_y, down_rest, cross_sum = tie(pieces, message_x, message_y, down_rest, cross_sum)

    down_g = [down_sum if k == 0 else message_x[1:] if k == 1 else message_y[1:] if k == half else None for k in range(mems)]
    for k in range(mems):
        if down_g[k] is None:
            down_g[k] = down_rest.pop(0)
    down_g = [p[0] for p in down_g]
    self_mine = sum_low([p[:share] for p in pieces])
    small = jnp.stack([from_rows(p[share:]) for p in pieces])
    small = tree_sum(
        [lax.dynamic_index_in_dim(small, (chip - z) % chips, 0, keepdims=False) for z in range(chips)]
    )
    gate_g, gate_order = [both_sum[:1], message_x[:1]], [0, bits[0]]
    linear_g, linear_order = [both_sum[1:], message_y[:1]], [0, bits[-1]]
    gate_g, gate_order = spread_rest(jnp.concatenate(gate_g), gate_order, bits[1:-1])
    linear_g, linear_order = spread_rest(jnp.concatenate(linear_g), linear_order, bits[::-1][1:-1])
    gate_g, linear_g = joined(gate_g), joined(linear_g)
    small_rows = to_rows(small)
    cut = gate_g.shape[0] * part
    cross_parts = list(quarters(jnp.concatenate(cross_sum)))
    messages = fuse(
        lambda g, l, rows_, *ps: [
            [*([l] if k == 1 else [g] if k == half else []), p, rows_] for k, p in enumerate(ps)
        ],
        gate_g.reshape(cut, width), linear_g.reshape(cut, width), small_rows, *cross_parts,
    )
    cross_parts[0] = messages[0]
    moved = {k: to_mem(p, k) for k, p in enumerate(messages) if k}
    moved, small_rows, self_mine, cross_own = tie(moved, small_rows, self_mine, cross_parts[0])
    linear_g = jnp.concatenate([linear_g, moved[1][:cut].reshape(-1, part, width)])
    gate_g = jnp.concatenate([gate_g, moved[half][:cut].reshape(-1, part, width)])
    gate_order = gate_order + [k | half for k in gate_order]
    linear_order = linear_order + [k | 1 for k in linear_order]
    cross_parts = [cross_own] + [moved[k][cut:] if k in (1, half) else moved[k] for k in range(1, mems)]
    small = tree_sum([from_rows(p[share:]) for p in cross_parts])

    mine = jnp.concatenate([self_mine, sum_low([p[:share] for p in cross_parts])])
    mine_g = [mine] + [to_mem(mine, k) for k in range(1, mems)]
    small = small + to_core(small)

    def settle(flat, order):
        return natural([flat[order.index(k)] for k in range(mems)], mem_index).astype(f32)

    gate_out = settle(gate_g, gate_order).reshape(feed, width)
    linear_out = settle(linear_g, linear_order).reshape(feed, width)
    down_out = natural(down_g, mem_index).astype(f32).reshape(feed, width)
    result = second_sum + res_own + res_more.astype(f32)
    mine_g, gate_out, linear_out, down_out = tie(mine_g, gate_out, linear_out, down_out)

    def settled(start, rows_of):
        return natural([p[start : start + rows_of] for p in mine_g], mem_index).astype(f32)

    self_sum = settled(0, share).reshape(4, slim, width)
    cross_sum = settled(share, share).reshape(4, slim, width)
    return (
        result.reshape(inputs.shape),
        input_grad.reshape(inputs.shape),
        memory_grad.swapaxes(2, 3).reshape(memory.shape),
        small[0],
        self_sum[0].T,
        self_sum[1].T,
        self_sum[2].T,
        self_sum[3],
        small[3, : buckets * heads].reshape(buckets, heads),
        small[1],
        cross_sum[2].T,
        cross_sum[0].T,
        cross_sum[1].T,
        cross_sum[3],
        small[2],
        gate_out.T,
        linear_out.T,
        down_out,
    )


def solution(mesh):
    tokens_at = P(None, "seq", "mem", None, None)
    memory_at = P(None, "seq", None, "mem", None)
    columns, row_cut = P(None, "seq"), P("seq", None)
    return jax.shard_map(
        per_device,
        mesh=mesh,
        in_specs=(
            tokens_at,
            memory_at,
            P(None, "seq", None),
            P(None, "seq", None, "mem"),
            P(),
            columns,
            columns,
            columns,
            row_cut,
            P(),
            P(),
            columns,
            columns,
            columns,
            row_cut,
            P(),
            columns,
            columns,
            row_cut,
            tokens_at,
        ),
        out_specs=(
            tokens_at,
            tokens_at,
            memory_at,
            P(),
            columns,
            columns,
            columns,
            row_cut,
            P(),
            P(),
            columns,
            columns,
            columns,
            row_cut,
            P(),
            columns,
            columns,
            row_cut,
        ),
        check_vma=False,
    )
```

```python
import functools
import math

import jax
import jax.numpy as jnp
from jax import lax
from jax.experimental import pallas as pl
from jax.experimental.pallas import tpu as pltpu
from jax.sharding import PartitionSpec as P

norm_eps = 1e-06
masked_score = -1e30
bf16 = jnp.bfloat16
f32 = jnp.float32


def bucket_edges():
    return [math.ceil(16 * 8 ** ((number - 16) / 16)) for number in range(17, 32)]


def position_buckets(length):
    row_index = jnp.arange(length, dtype=jnp.int32)
    offset = jnp.maximum(row_index[:, None] - row_index[None, :], 0)
    bucket = jnp.minimum(offset, 16)
    for threshold in bucket_edges():
        bucket = bucket + (offset >= threshold).astype(jnp.int32)
    return bucket


def matmul(left, right):
    return jnp.dot(left, right, preferred_element_type=f32)


def contract_rows(left, right):
    return lax.dot_general(left, right, (((0,), (0,)), ((), ())), preferred_element_type=f32)


def contract_cols(left, right):
    return lax.dot_general(left, right, (((1,), (1,)), ((), ())), preferred_element_type=f32)


def add_low(left, right):
    return (left.astype(f32) + right.astype(f32)).astype(bf16)


def to_core(value):
    count = lax.axis_size("seq")
    return lax.ppermute(value, "seq", [(i, i ^ 1) for i in range(count)])


def rows_to_core(value):
    return to_core(value.reshape(-1, 64, value.shape[-1])).reshape(value.shape)


def to_next(value):
    count = lax.axis_size("seq")
    return lax.ppermute(value, "seq", [(i, (i + 2) % count) for i in range(count)])


def to_mem(value, mask):
    count = lax.axis_size("mem")
    return lax.ppermute(value, "mem", [(i, i ^ mask) for i in range(count)])


def mem_bits():
    return [1 << b for b in range((lax.axis_size("mem") - 1).bit_length())]


def to_step(value, step):
    count = lax.axis_size("seq")
    return lax.ppermute(value, "seq", [(i, (i + 2 * step) % count) for i in range(count)])


def to_seq(value, mask):
    count = lax.axis_size("seq")
    return lax.ppermute(value, "seq", [(i, i ^ mask) for i in range(count)])


def after(value, *others):
    return lax.optimization_barrier((value, *others))[0]


def ring_gather(value):
    pieces = [value]
    for _ in range(lax.axis_size("seq") // 2 - 1):
        pieces.append(to_next(pieces[-1]))
    return pieces


def ring_sum(pieces):
    total = pieces[1]
    for piece in pieces[2:]:
        total = add_low(to_next(total), piece)
    return add_low(to_next(total), pieces[0])


def spread_gather(value, bits):
    held, order = value[None], [0]
    for bit in bits:
        held = jnp.concatenate([held, to_mem(held, bit)], axis=0)
        order = order + [k | bit for k in order]
    return [held[order.index(k)] for k in range(len(order))]


def fold(held, bits):
    order = list(range(held.shape[0]))
    for bit in bits:
        keep = [i for i, k in enumerate(order) if not k & bit]
        send = [order.index(order[i] | bit) for i in keep]
        moved = to_mem(jnp.stack([held[i] for i in send]), bit)
        held = jnp.stack([add_low(held[i], moved[n]) for n, i in enumerate(keep)])
        order = [order[i] for i in keep]
    return held[0]


def sum_low(pieces):
    total = pieces[0].astype(f32)
    for piece in pieces[1:]:
        total = total + piece.astype(f32)
    return total.astype(bf16)


def direct_fold(pieces):
    return sum_low([to_mem(p, k) if k else p for k, p in enumerate(pieces)])


def natural(pieces, mem_index):
    stacked = jnp.stack(pieces)
    return jnp.stack(
        [
            lax.dynamic_index_in_dim(stacked, mem_index ^ k, 0, keepdims=False)
            for k in range(len(pieces))
        ]
    )


def back_to_mem(value, mem_index):
    pieces = [to_mem(value, k) if k else value for k in range(lax.axis_size("mem"))]
    return natural(pieces, mem_index).astype(f32)


def assemble_kernel(spot, own, other, *outs):
    chips = own.shape[0]
    core, chip = spot[0], spot[1]
    for q, out in enumerate(outs):
        for j in range(chips):
            at = lax.rem(chip - j + chips, chips) * 2
            out[at + core] = own[j, spot[2 + q]]
            out[at + 1 - core] = other[j, spot[2 + q]]


def assemble(spot, own, other):
    chips, mems, share, width = own.shape
    vmem = pl.BlockSpec(memory_space=pltpu.VMEM)
    return pl.pallas_call(
        assemble_kernel,
        in_specs=[pl.BlockSpec(memory_space=pltpu.SMEM), vmem, vmem],
        out_shape=[jax.ShapeDtypeStruct((2 * chips, share, width), bf16)] * mems,
        compiler_params=params(26),
        cost_estimate=cost(3),
        name="assemble",
    )(spot, own, other)


def params(limit_mb=56):
    return pltpu.CompilerParams(vmem_limit_bytes=limit_mb * 1024 * 1024)


def cost(micro_seconds):
    return pl.CostEstimate(
        flops=micro_seconds * 10**9, bytes_accessed=micro_seconds * 3 * 10**6, transcendentals=0
    )


def row_norm(value):
    return lax.rsqrt(jnp.mean(value * value, axis=-1, keepdims=True) + norm_eps)


def norm_back_rows(value, gain, upstream):
    scale = row_norm(value)
    weighted = upstream * gain
    mean_dot = jnp.mean(weighted * value, axis=-1, keepdims=True)
    gain_grad = jnp.sum(upstream * value * scale, axis=0, keepdims=True)
    return weighted * scale - value * (scale * scale * scale * mean_dot), gain_grad


def lane_head(length, depth):
    return lax.broadcasted_iota(jnp.int32, (length, 128), 1) // depth


def self_fwd_kernel(depth, length, tok, g1, qw, kw, vw, ow, bias, g2, cw, tok_o, normed_o, q_o, k_o, v_o, mixed_o, first_o, nc_o, cq_o):
    for m in range(tok.shape[0]):
        tok_o[m * length : (m + 1) * length] = tok[m].astype(f32).T.astype(bf16)
    x = tok_o[...].astype(f32)
    normed = (x * row_norm(x) * g1[...]).astype(bf16)
    normed_o[...] = normed
    q_o[...] = contract_cols(normed, qw[...]).astype(bf16)
    k_o[...] = contract_cols(normed, kw[...]).astype(bf16)
    v_o[...] = contract_cols(normed, vw[...]).astype(bf16)
    inner = qw.shape[0]
    groups, share = inner // 128, 128 // depth
    lanes = lane_head(length, depth)

    def body(step, carry):
        micro, group = step // groups, step % groups
        rows = pl.ds(pl.multiple_of(micro * length, length), length)
        cols = pl.ds(pl.multiple_of(group * 128, 128), 128)
        q, k, v = q_o[rows, cols], k_o[rows, cols], v_o[rows, cols]
        out = jnp.zeros((length, 128), f32)
        for a in range(share):
            s = contract_cols(jnp.where(lanes == a, q, 0), k) + bias[group * share + a]
            e = jnp.exp(s - jnp.max(s, axis=-1, keepdims=True))
            p = (e / jnp.sum(e, axis=-1, keepdims=True)).astype(bf16)
            out = jnp.where(lanes == a, matmul(p, v), out)
        mixed_o[rows, cols] = out.astype(bf16)
        return carry

    lax.fori_loop(0, x.shape[0] // length * groups, body, 0)
    first = tok_o[...].astype(f32) + matmul(mixed_o[...], ow[...])
    first_o[...] = first
    nc = (first * row_norm(first) * g2[...]).astype(bf16)
    nc_o[...] = nc
    cq_o[...] = contract_cols(nc, cw[...]).astype(bf16)


def self_fwd(depth, length, tok, g1, qw, kw, vw, ow, bias, g2, cw):
    rows, width = tok.shape[0] * tok.shape[2], tok.shape[1]
    inner = qw.shape[0]
    low, slim = jax.ShapeDtypeStruct((rows, width), bf16), jax.ShapeDtypeStruct((rows, inner), bf16)
    return pl.pallas_call(
        functools.partial(self_fwd_kernel, depth, length),
        out_shape=(low, low, slim, slim, slim, slim, jax.ShapeDtypeStruct((rows, width), f32), low, slim),
        compiler_params=params(40),
        cost_estimate=cost(16),
        name="self_fwd",
    )(tok, g1, qw, kw, vw, ow, bias, g2, cw)


def cross_fwd_kernel(depth, length, parts, cq, mask, ow, first, g3, *refs):
    kvs, (mixed_o, second_o, nf_o) = refs[:parts], refs[parts:]
    inner = ow.shape[0]
    groups, share = inner // 128, 128 // depth
    lanes = lane_head(length, depth)

    def body(step, carry):
        micro, group = step // groups, step % groups
        rows = pl.ds(pl.multiple_of(micro * length, length), length)
        cols = pl.ds(pl.multiple_of(group * 128, 128), 128)
        vcols = pl.ds(pl.multiple_of(inner + group * 128, 128), 128)
        q = cq[rows, cols]
        k = jnp.concatenate([kv[micro, :, cols] for kv in kvs], axis=0)
        v = jnp.concatenate([kv[micro, :, vcols] for kv in kvs], axis=0)
        out = jnp.zeros((length, 128), f32)
        for a in range(share):
            s = contract_cols(jnp.where(lanes == a, q, 0), k)
            s = jnp.where(mask[micro] > 0, s, masked_score)
            e = jnp.exp(s - jnp.max(s, axis=-1, keepdims=True))
            p = (e / jnp.sum(e, axis=-1, keepdims=True)).astype(bf16)
            out = jnp.where(lanes == a, matmul(p, v), out)
        mixed_o[rows, cols] = out.astype(bf16)
        return carry

    lax.fori_loop(0, cq.shape[0] // length * groups, body, 0)
    second = first[...] + matmul(mixed_o[...], ow[...])
    second_o[...] = second
    nf_o[...] = (second * row_norm(second) * g3[...]).astype(bf16)


def cross_fwd(depth, length, cq, mask, ow, first, g3, kvs):
    rows, width = first.shape
    return pl.pallas_call(
        functools.partial(cross_fwd_kernel, depth, length, len(kvs)),
        out_shape=(
            jax.ShapeDtypeStruct(cq.shape, bf16),
            jax.ShapeDtypeStruct((rows, width), f32),
            jax.ShapeDtypeStruct((rows, width), bf16),
        ),
        compiler_params=params(36),
        cost_estimate=cost(15),
        name="cross_fwd",
    )(cq, mask, ow, first, g3, *kvs)


def cross_bwd_kernel(depth, length, parts, og, nf_own, nf_more, second, g3, mixed, cq, mask, ow, first, g2, nc, qw, *refs):
    kvs = refs[:parts]
    kvg = refs[parts : 2 * parts]
    g3_o, dow_o, dqw_o, firstg_o, g2_o, mixg, dq = refs[2 * parts :]
    inner = ow.shape[0]
    slots = kvs[0].shape[1]
    groups, share = inner // 128, 128 // depth
    lanes = lane_head(length, depth)
    part, gain = norm_back_rows(second[...], g3[...], nf_own[...] + nf_more[...].astype(f32))
    g3_o[...] = gain
    second_grad = og[...].astype(f32) + part
    firstg_o[...] = second_grad
    low = second_grad.astype(bf16)
    dow_o[...] = contract_rows(mixed[...], low).astype(bf16)
    mixg[...] = contract_cols(low, ow[...]).astype(bf16)

    def body(step, carry):
        micro, group = step // groups, step % groups
        rows = pl.ds(pl.multiple_of(micro * length, length), length)
        cols = pl.ds(pl.multiple_of(group * 128, 128), 128)
        vcols = pl.ds(pl.multiple_of(inner + group * 128, 128), 128)
        q, o = cq[rows, cols], mixg[rows, cols]
        k = jnp.concatenate([kv[micro, :, cols] for kv in kvs], axis=0)
        v = jnp.concatenate([kv[micro, :, vcols] for kv in kvs], axis=0)
        q_grad = jnp.zeros((length, 128), f32)
        k_grad = jnp.zeros((parts * slots, 128), f32)
        v_grad = jnp.zeros((parts * slots, 128), f32)
        for a in range(share):
            qa, oa = jnp.where(lanes == a, q, 0), jnp.where(lanes == a, o, 0)
            s = contract_cols(qa, k)
            s = jnp.where(mask[micro] > 0, s, masked_score)
            e = jnp.exp(s - jnp.max(s, axis=-1, keepdims=True))
            p = e / jnp.sum(e, axis=-1, keepdims=True)
            v_grad += contract_rows(p.astype(bf16), oa)
            dp = contract_cols(oa, v)
            ds = (p * (dp - jnp.sum(p * dp, axis=-1, keepdims=True))).astype(bf16)
            q_grad = jnp.where(lanes == a, matmul(ds, k), q_grad)
            k_grad += contract_rows(ds, qa)
        dq[rows, cols] = q_grad.astype(bf16)
        for t in range(parts):
            kvg[t][micro, :, cols] = k_grad[t * slots : (t + 1) * slots].astype(bf16)
            kvg[t][micro, :, vcols] = v_grad[t * slots : (t + 1) * slots].astype(bf16)
        return carry

    lax.fori_loop(0, cq.shape[0] // length * groups, body, 0)
    dqw_o[...] = contract_rows(dq[...], nc[...]).astype(bf16)
    part, gain = norm_back_rows(first[...], g2[...], matmul(dq[...], qw[...]))
    g2_o[...] = gain
    firstg_o[...] = firstg_o[...] + part


def cross_bwd(depth, length, og, nf_own, nf_more, second, g3, mixed, cq, mask, ow, first, g2, nc, qw, kvs):
    rows, width = first.shape
    gain = jax.ShapeDtypeStruct((1, width), f32)
    weight = jax.ShapeDtypeStruct(ow.shape, bf16)
    out = pl.pallas_call(
        functools.partial(cross_bwd_kernel, depth, length, len(kvs)),
        out_shape=(
            *[jax.ShapeDtypeStruct(kv.shape, bf16) for kv in kvs],
            gain,
            weight,
            weight,
            jax.ShapeDtypeStruct((rows, width), f32),
            gain,
        ),
        scratch_shapes=[pltpu.VMEM(cq.shape, bf16), pltpu.VMEM(cq.shape, bf16)],
        compiler_params=params(50),
        cost_estimate=cost(31),
        name="cross_bwd",
    )(og, nf_own, nf_more, second, g3, mixed, cq, mask, ow, first, g2, nc, qw, *kvs)
    return out[: len(kvs)], out[len(kvs) :]


def self_bwd_kernel(depth, length, first_grad, mixed, q, k, v, bias, ow, qw, kw, vw, normed, tok, g1, dow_o, dqw_o, dkw_o, dvw_o, ing_o, g1_o, ds_o, mixg, dq, dk, dv):
    inner = ow.shape[0]
    groups, share = inner // 128, 128 // depth
    lanes = lane_head(length, depth)
    low = first_grad[...].astype(bf16)
    dow_o[...] = contract_rows(mixed[...], low).astype(bf16)
    mixg[...] = contract_cols(low, ow[...]).astype(bf16)

    def body(group, carry):
        cols = pl.ds(pl.multiple_of(group * 128, 128), 128)
        total = [jnp.zeros((length, length), f32) for _ in range(share)]
        for micro in range(tok.shape[0] // length):
            rows = slice(micro * length, (micro + 1) * length)
            qs, ks, vs, o = q[rows, cols], k[rows, cols], v[rows, cols], mixg[rows, cols]
            q_grad = jnp.zeros((length, 128), f32)
            k_grad = jnp.zeros((length, 128), f32)
            v_grad = jnp.zeros((length, 128), f32)
            for a in range(share):
                qa, oa = jnp.where(lanes == a, qs, 0), jnp.where(lanes == a, o, 0)
                s = contract_cols(qa, ks) + bias[group * share + a]
                e = jnp.exp(s - jnp.max(s, axis=-1, keepdims=True))
                p = e / jnp.sum(e, axis=-1, keepdims=True)
                v_grad += contract_rows(p.astype(bf16), oa)
                dp = contract_cols(oa, vs)
                ds = (p * (dp - jnp.sum(p * dp, axis=-1, keepdims=True))).astype(bf16)
                total[a] = total[a] + ds.astype(f32)
                q_grad = jnp.where(lanes == a, matmul(ds, ks), q_grad)
                k_grad += contract_rows(ds, qa)
            dq[rows, cols] = q_grad.astype(bf16)
            dk[rows, cols] = k_grad.astype(bf16)
            dv[rows, cols] = v_grad.astype(bf16)
        for a in range(share):
            ds_o[group * share + a] = total[a]
        return carry

    lax.fori_loop(0, groups, body, 0)
    dqw_o[...] = contract_rows(dq[...], normed[...]).astype(bf16)
    dkw_o[...] = contract_rows(dk[...], normed[...]).astype(bf16)
    dvw_o[...] = contract_rows(dv[...], normed[...]).astype(bf16)
    up = matmul(dq[...], qw[...]) + matmul(dk[...], kw[...]) + matmul(dv[...], vw[...])
    part, gain = norm_back_rows(tok[...].astype(f32), g1[...], up)
    g1_o[...] = gain
    ing_o[...] = first_grad[...] + part


def self_bwd(depth, length, first_grad, mixed, q, k, v, bias, ow, qw, kw, vw, normed, tok, g1):
    rows, width = tok.shape
    weight = jax.ShapeDtypeStruct(ow.shape, bf16)
    return pl.pallas_call(
        functools.partial(self_bwd_kernel, depth, length),
        out_shape=(
            weight,
            weight,
            weight,
            weight,
            jax.ShapeDtypeStruct((rows, width), f32),
            jax.ShapeDtypeStruct((1, width), f32),
            jax.ShapeDtypeStruct(bias.shape, f32),
        ),
        scratch_shapes=[pltpu.VMEM(q.shape, bf16)] * 4,
        compiler_params=params(42),
        cost_estimate=cost(21),
        name="self_bwd",
    )(first_grad, mixed, q, k, v, bias, ow, qw, kw, vw, normed, tok, g1)


def kv_fwd_kernel(place, source, kw, vw, *outs):
    rows = source[0, 0]
    both = [
        lax.dot_general(rows, w[...], (((0,), (1,)), ((), ())), preferred_element_type=f32).astype(bf16)
        for w in (kw, vw)
    ]
    for s, out in enumerate(outs):

        @pl.when(pl.program_id(0) == s)
        def write(out=out):
            out[0] = jnp.concatenate(both, axis=1)


def kv_fwd(place, memory, kw, vw):
    micros, pairs, width, slots = memory.shape
    inner = kw.shape[0]
    whole = pl.BlockSpec((inner, width), lambda s, m, place: (0, 0))
    return pl.pallas_call(
        kv_fwd_kernel,
        grid_spec=pltpu.PrefetchScalarGridSpec(
            num_scalar_prefetch=1,
            grid=(pairs, micros),
            in_specs=[
                pl.BlockSpec((1, 1, width, slots), lambda s, m, place: (m, place[s], 0, 0)),
                whole,
                whole,
            ],
            out_specs=[
                pl.BlockSpec(
                    (1, slots, 2 * inner),
                    lambda s, m, place, t=t: (jnp.where(s < t, 0, jnp.where(s == t, m, micros - 1)), 0, 0),
                )
                for t in range(pairs)
            ],
        ),
        out_shape=[jax.ShapeDtypeStruct((micros, slots, 2 * inner), bf16)] * pairs,
        compiler_params=params(20),
        cost_estimate=cost(9),
        name="kv_fwd",
    )(place, memory, kw, vw)


def kv_weights_kernel(place, source, *refs):
    kvgs, (dkw_o, dvw_o, acc) = refs[:-3], refs[-3:]
    inner = dkw_o.shape[0]
    pair = pl.program_id(0)
    step = pair * pl.num_programs(1) + pl.program_id(1)

    @pl.when(step == 0)
    def clear():
        acc[...] = jnp.zeros_like(acc)

    grads = kvgs[0][0]
    for t in range(1, len(kvgs)):
        grads = jnp.where(pair == t, kvgs[t][0], grads)
    acc[...] += lax.dot_general(
        grads, source[0, 0], (((0,), (1,)), ((), ())), preferred_element_type=f32
    )

    @pl.when(step == pl.num_programs(0) * pl.num_programs(1) - 1)
    def write():
        dkw_o[...] = acc[:inner].astype(bf16)
        dvw_o[...] = acc[inner:].astype(bf16)


def kv_memory_kernel(place, kw, vw, *refs):
    kvgs, out = refs[:-1], refs[-1]
    inner = kw.shape[0]
    pair = pl.program_id(0)
    grads = kvgs[0][0]
    for t in range(1, len(kvgs)):
        grads = jnp.where(pair == t, kvgs[t][0], grads)
    out[0, 0] = lax.dot_general(
        kw[...], grads[:, :inner], (((0,), (1,)), ((), ())), preferred_element_type=f32
    ) + lax.dot_general(
        vw[...], grads[:, inner:], (((0,), (1,)), ((), ())), preferred_element_type=f32
    )


def kv_specs(pairs, micros, slots, inner, width):
    whole = pl.BlockSpec((inner, width), lambda s, m, place: (0, 0))
    block = pl.BlockSpec((1, 1, width, slots), lambda s, m, place: (m, place[s], 0, 0))
    pieces = [
        pl.BlockSpec(
            (1, slots, 2 * inner),
            lambda s, m, place, t=t: (jnp.where(s < t, 0, jnp.where(s == t, m, micros - 1)), 0, 0),
        )
        for t in range(pairs)
    ]
    return whole, block, pieces


def kv_weights(place, memory, kvgs, inner):
    micros, pairs, width, slots = memory.shape
    whole, block, pieces = kv_specs(pairs, micros, slots, inner, width)
    weight = jax.ShapeDtypeStruct((inner, width), bf16)
    return pl.pallas_call(
        kv_weights_kernel,
        grid_spec=pltpu.PrefetchScalarGridSpec(
            num_scalar_prefetch=1,
            grid=(pairs, micros),
            in_specs=[block, *pieces],
            out_specs=(whole, whole),
            scratch_shapes=[pltpu.VMEM((2 * inner, width), f32)],
        ),
        out_shape=(weight, weight),
        compiler_params=params(24),
        cost_estimate=cost(9),
        name="kv_weights",
    )(place, memory, *kvgs)


def kv_memory(place, shape, kw, vw, kvgs):
    micros, pairs, width, slots = shape
    inner = kw.shape[0]
    whole, block, pieces = kv_specs(pairs, micros, slots, inner, width)
    return pl.pallas_call(
        kv_memory_kernel,
        grid_spec=pltpu.PrefetchScalarGridSpec(
            num_scalar_prefetch=1,
            grid=(pairs, micros),
            in_specs=[whole, whole, *pieces],
            out_specs=block,
        ),
        out_shape=jax.ShapeDtypeStruct(shape, f32),
        compiler_params=params(20),
        cost_estimate=cost(10),
        name="kv_memory",
    )(place, kw, vw, *kvgs)


gelu_c = math.sqrt(2 / math.pi)


def plan(steps):
    arrays, out = [], []
    for buffers in steps:
        out.append([])
        for n, sources in enumerate(buffers):
            at = 0
            for array, index, rows in sources:
                found = [i for i, known in enumerate(arrays) if known is array]
                if not found:
                    arrays.append(array)
                out[-1].append((found[0] if found else len(arrays) - 1, index, n, at, rows))
                at += rows
    return arrays, out


def fetch(places, refs, hold, sems, step, slot):
    copies = []
    for i, (which, index, n, at, rows) in enumerate(places[step]):
        src = refs[which].at[index] if index else refs[which]
        copies.append(pltpu.make_async_copy(src, hold.at[slot, n, pl.ds(at, rows)], sems.at[slot, i]))
    return copies


def run_fetch(places, refs, hold, sems):
    step = pl.program_id(0)
    for i in range(len(places)):

        @pl.when(step == i)
        def move(i=i):
            if i == 0:
                for copy in fetch(places, refs, hold, sems, 0, 0):
                    copy.start()
            if i + 1 < len(places):
                for copy in fetch(places, refs, hold, sems, i + 1, (i + 1) % 2):
                    copy.start()
            for copy in fetch(places, refs, hold, sems, i, i % 2):
                copy.wait()


def feed_grad_kernel(places, count, mems, *refs):
    nf_a, nf_b, og_a, og_b = refs[:4]
    weights = refs[4 : 4 + count]
    split = 2 if mems else 1
    dgw_o, dlw_o = refs[4 + count : 4 + count + split], refs[4 + count + split : 4 + count + 2 * split]
    steps = len(places)
    ddw_o = refs[4 + count + 2 * split : 4 + count + 2 * split + steps]
    hid_o, gl_o, ll_o, nf, og, hold, sems, whole_sems = refs[4 + count + 2 * split + steps :]
    rows = nf_a.shape[0]
    step = pl.program_id(0)

    def loads():
        return [
            pltpu.make_async_copy(src, dst.at[pl.ds(at, rows)], whole_sems.at[i])
            for i, (src, dst, at) in enumerate([(nf_a, nf, 0), (nf_b, nf, rows), (og_a, og, 0), (og_b, og, rows)])
        ]

    @pl.when(step == 0)
    def load():
        for copy in loads():
            copy.start()

    run_fetch(places, weights, hold, sems)

    @pl.when(step == 0)
    def loaded():
        for copy in loads():
            copy.wait()

    slot = lax.rem(step, 2)
    x, up = nf[...], og[...]
    g = contract_cols(x, hold[slot, 0])
    lin = contract_cols(x, hold[slot, 1])
    hg = contract_cols(up, hold[slot, 2])
    t = jnp.tanh(gelu_c * (g + 0.044715 * (g * g * g)))
    act = 0.5 * g * (1.0 + t)
    slope = 0.5 * (1.0 + t) + 0.5 * g * (1.0 - t * t) * (gelu_c * (1.0 + 3 * 0.044715 * (g * g)))
    hidden = (act * lin).astype(bf16)
    gl = (hg * lin * slope).astype(bf16)
    ll = (hg * act).astype(bf16)
    hid_o[0] = hidden
    gl_o[0] = gl
    ll_o[0] = ll
    for outs, upstream, bit in ((dgw_o, gl, mems // 2), (dlw_o, ll, 1)):
        grad = contract_rows(upstream, x).astype(bf16)
        if not mems:
            outs[0][0] = grad
            continue
        part = grad.shape[0] // mems
        for k in range(mems):
            at = [i for i in range(mems) if (i & bit) == (k & bit)].index(k)
            outs[1 if k & bit else 0][0, at] = grad[k * part : (k + 1) * part]
    down_grad = contract_rows(hidden, up).astype(bf16)

    for i, out in enumerate(ddw_o):

        @pl.when(step == i)
        def write(out=out):
            out[...] = down_grad


def feed_grad(nf_a, nf_b, og_a, og_b, steps, block, mems, price=13):
    rows, width = nf_a.shape
    weights, places = plan(steps)
    n = len(steps)
    any_spec = pl.BlockSpec(memory_space=pl.ANY)
    tile = pl.BlockSpec((1, block, width), lambda i: (i, 0, 0))
    column = pl.BlockSpec((1, 2 * rows, block), lambda i: (i, 0, 0))
    weight = jax.ShapeDtypeStruct((n, block, width), bf16)
    act = jax.ShapeDtypeStruct((n, 2 * rows, block), bf16)
    half_tile, half = tile, weight
    if mems:
        half_tile = pl.BlockSpec((1, mems // 2, block // mems, width), lambda i: (i, 0, 0, 0))
        half = jax.ShapeDtypeStruct((n, mems // 2, block // mems, width), bf16)
    count = 4 if mems else 2
    return pl.pallas_call(
        functools.partial(feed_grad_kernel, places, len(weights), mems),
        grid=(n,),
        in_specs=[any_spec] * (4 + len(weights)),
        out_specs=(
            *[half_tile] * count,
            *[pl.BlockSpec((block, width), lambda i: (0, 0))] * n,
            column,
            column,
            column,
        ),
        out_shape=(
            *[half] * count,
            *[jax.ShapeDtypeStruct((block, width), bf16)] * n,
            act,
            act,
            act,
        ),
        scratch_shapes=[
            pltpu.VMEM((2 * rows, width), bf16),
            pltpu.VMEM((2 * rows, width), bf16),
            pltpu.VMEM((2, 3, block, width), bf16),
            pltpu.SemaphoreType.DMA((2, max(len(p) for p in places))),
            pltpu.SemaphoreType.DMA((4,)),
        ],
        compiler_params=params(54),
        cost_estimate=cost(price * n),
        name="feed_grad",
    )(nf_a, nf_b, og_a, og_b, *weights)


def feed_sum_kernel(places, act_places, count, act_count, *refs):
    weights, acts = refs[:count], refs[count : count + act_count]
    own_o, other_o, other, hold, acts_hold, sems, act_sems = refs[count + act_count :]
    step = pl.program_id(0)
    rows = own_o.shape[0]
    run_fetch(places, weights, hold, sems)
    run_fetch(act_places, acts, acts_hold, act_sems)
    slot = lax.rem(step, 2)
    total = matmul(acts_hold[slot, 0], hold[slot, 0])
    for m in range(1, hold.shape[1]):
        total = total + matmul(acts_hold[slot, m], hold[slot, m])

    @pl.when(step == 0)
    def first():
        own_o[...] = total[:rows]
        other[...] = total[rows:]

    @pl.when(step > 0)
    def later():
        own_o[...] += total[:rows]
        other[...] += total[rows:]

    @pl.when(step == pl.num_programs(0) - 1)
    def last():
        other_o[...] = other[...].astype(bf16)


def feed_sum(rows, width, steps, act_steps, block):
    weights, places = plan(steps)
    acts, act_places = plan(act_steps)
    count = len(steps[0])
    whole = pl.BlockSpec((rows, width), lambda i: (0, 0))
    return pl.pallas_call(
        functools.partial(feed_sum_kernel, places, act_places, len(weights), len(acts)),
        grid=(len(steps),),
        in_specs=[pl.BlockSpec(memory_space=pl.ANY)] * (len(weights) + len(acts)),
        out_specs=(whole, whole),
        out_shape=(jax.ShapeDtypeStruct((rows, width), f32), jax.ShapeDtypeStruct((rows, width), bf16)),
        scratch_shapes=[
            pltpu.VMEM((rows, width), f32),
            pltpu.VMEM((2, count, block, width), bf16),
            pltpu.VMEM((2, count, 2 * rows, block), bf16),
            pltpu.SemaphoreType.DMA((2, max(len(p) for p in places))),
            pltpu.SemaphoreType.DMA((2, max(len(p) for p in act_places))),
        ],
        compiler_params=params(48),
        cost_estimate=cost(1 if count == 1 else 23),
        name="feed_sum",
    )(*weights, *acts)


def joined(value):
    return jnp.concatenate(value) if isinstance(value, list) else value


def fuse(fn, *arrays, limit=0):
    shapes = jax.eval_shape(lambda *a: [joined(o) for o in fn(*a)], *arrays)
    if any(a.shape[-2] % 16 for a in (*arrays, *shapes)):
        return [joined(o) for o in fn(*arrays)]

    limit = limit or 6 + sum(math.prod(a.shape) for a in (*arrays, *shapes)) * 4 // 2**20

    def kernel(*refs):
        for out, value in zip(refs[len(arrays) :], fn(*[ref[...] for ref in refs[: len(arrays)]])):
            at = 0
            for piece in value if isinstance(value, list) else [value]:
                out[at : at + piece.shape[0]] = piece
                at += piece.shape[0]

    return pl.pallas_call(
        kernel, out_shape=shapes, compiler_params=params(limit), cost_estimate=cost(3), name="fuse"
    )(*arrays)


def core_split_kernel(spot, *refs):
    grads, (kept, sent) = refs[:-2], refs[-2:]
    core = spot[0]
    for i, grad in enumerate(grads):
        for z in range(grad.shape[0]):
            kept[z, i] = grad[z, core]
            sent[z, i] = grad[z, 1 - core]


def core_split(spot, grads):
    chips, _, slim, width = grads[0].shape
    shape = jax.ShapeDtypeStruct((chips, len(grads), slim, width), bf16)
    return pl.pallas_call(
        core_split_kernel,
        in_specs=[pl.BlockSpec(memory_space=pltpu.SMEM)] + [pl.BlockSpec(memory_space=pltpu.VMEM)] * len(grads),
        out_shape=(shape, shape),
        compiler_params=params(60),
        cost_estimate=cost(4),
        name="core_split",
    )(spot, *grads)


def columns_kernel(spot, kept, moved, *outs):
    chips = kept.shape[0]
    for k, out in enumerate(outs):
        for z in range(chips):
            out[z] = add_low(kept[z, spot[2 + k]], moved[z, spot[2 + k]])


def columns_of(spot, kept, moved, mems):
    chips, count, slim, width = kept.shape
    if count != mems:
        total = add_low(kept, moved).reshape(chips, mems, -1, width)
        return [lax.dynamic_index_in_dim(total, spot[2 + k], 1, keepdims=False) for k in range(mems)]
    vmem = pl.BlockSpec(memory_space=pltpu.VMEM)
    return pl.pallas_call(
        columns_kernel,
        in_specs=[pl.BlockSpec(memory_space=pltpu.SMEM), vmem, vmem],
        out_shape=[jax.ShapeDtypeStruct((chips, slim, width), bf16)] * mems,
        compiler_params=params(18),
        cost_estimate=cost(4),
        name="columns",
    )(spot, kept, moved)


def tree_sum(values):
    while len(values) > 1:
        values = [left + right for left, right in zip(values[::2], values[1::2])]
    return values[0]


def tie(*values):
    return lax.optimization_barrier(values)


def fold_parts(held, order, bit):
    keep = [i for i, k in enumerate(order) if not k & bit]
    send = [order.index(order[i] | bit) for i in keep]
    return [jnp.stack([held[:, i] for i in at], axis=1) for at in (keep, send)]


def fold_step(held, order, bit):
    kept, sent = fold_parts(held, order, bit)
    return kept, to_mem(sent, bit), [k for k in order if not k & bit]


def per_device(
    inputs,
    memory,
    memory_lengths,
    keep_mask,
    norm_self,
    query_self,
    key_self,
    value_self,
    output_self,
    bias_table,
    norm_cross,
    query_cross,
    key_cross,
    value_cross,
    output_cross,
    norm_feed,
    gate_feed,
    linear_feed,
    down_feed,
    output_grad,
):
    micros = inputs.shape[0]
    length = inputs.shape[3]
    width = inputs.shape[4]
    pairs = memory.shape[2]
    slots = memory.shape[3]
    heads = bias_table.shape[1]
    buckets = bias_table.shape[0]
    seqs = lax.axis_size("seq")
    mems = lax.axis_size("mem")
    chips = seqs // 2
    slim = query_self.shape[1]
    inner = slim * seqs
    depth = inner // heads
    feed = gate_feed.shape[1]
    part = feed // mems
    rows = micros * length
    seq_index = lax.axis_index("seq")
    core = seq_index % 2
    chip = seq_index // 2
    mem_index = lax.axis_index("mem")
    gain_self = norm_self.astype(f32)
    gain_cross = norm_cross.astype(f32)
    gain_feed = norm_feed.astype(f32)


    bits = mem_bits()
    spot = jnp.stack([core, chip] + [mem_index ^ q for q in range(mems)]).astype(jnp.int32)

    def quarters(shard):
        shard = shard.reshape(mems, shard.shape[0] // mems, width)
        return jnp.stack(
            [lax.dynamic_index_in_dim(shard, mem_index ^ k, 0, keepdims=False) for k in range(mems)]
        )

    last = chips - 1
    early = list(range(1, last))

    def matrices(held, other):
        full = assemble(spot, held, other)
        if mems == 4:
            return [full[i].reshape(inner, width) for i in range(4)]
        full = jnp.stack(full).reshape(4, mems // 4, seqs, -1, width).transpose(0, 2, 1, 3, 4)
        return list(full.reshape(4, inner, width))

    def hold_plane(pack, moved):
        return jnp.concatenate([pack[None], jnp.stack(moved, axis=1)], axis=0)

    first_pack = quarters(jnp.concatenate([key_cross.T, value_cross.T, query_self.T, key_self.T], axis=0))
    second_pack = quarters(
        jnp.concatenate([value_self.T, output_self, query_cross.T, output_cross], axis=0)
    )
    gate_own, linear_own, down_own = quarters(gate_feed.T), quarters(linear_feed.T), quarters(down_feed)
    both = [jnp.stack([gate_own[0], linear_own[0]])]
    halved = mems // 2
    down_a, down_b = [down_own[:halved]], [down_own[halved:]]

    onehot = (
        position_buckets(length).reshape(length * length, 1)
        == jnp.arange(buckets, dtype=jnp.int32)[None, :]
    ).astype(bf16)
    position_bias = (
        jnp.dot(onehot, bias_table, preferred_element_type=f32)
        .reshape(length, length, heads)
        .transpose(2, 0, 1)
    )
    row_index = jnp.arange(length, dtype=jnp.int32)
    causal = row_index[:, None] >= row_index[None, :]
    position_bias = jnp.where(causal[None], position_bias, masked_score)
    og_low = output_grad.reshape(rows, width)
    gain_self, gain_cross, gain_feed = [g.reshape(1, width) for g in (gain_self, gain_cross, gain_feed)]
    spots = jnp.stack(
        [(mem_index ^ s) * slots + jnp.arange(slots, dtype=jnp.int32) for s in range(mems)], 0
    )
    len_own = lax.dynamic_index_in_dim(memory_lengths[:, 0], mem_index, 1, keepdims=False)
    place = spot[2:]
    source = memory.reshape(micros, pairs, slots, width).swapaxes(2, 3)
    both_packs = jnp.stack([first_pack[0], second_pack[0]])
    moved = [to_step(both_packs, j) for j in range(1, chips)]
    og_other = rows_to_core(og_low)
    keep_all = lax.all_gather(keep_mask[:, 0], "mem", axis=0)
    moved, both[0], og_other, keep_all = tie(moved, both[0], og_other, keep_all)
    keep_own = lax.dynamic_index_in_dim(keep_all, mem_index, 2, keepdims=False)
    keep_own = jnp.stack(
        [lax.dynamic_index_in_dim(keep_own, mem_index ^ s, 0, keepdims=False) for s in range(mems)], 1
    )
    valid = (spots[None] < len_own[:, None, None]) & ((keep_own == 1) | (spots[None] == 0))
    valid = valid.reshape(micros, 1, mems * slots).astype(f32)


    first_parts, second_parts = fuse(
        lambda *m: [[p[:1] for p in m], [p[1:] for p in m]], *moved
    )
    first_parts, second_parts = first_parts[None], second_parts[None]
    first_order, second_order = [0], [0]
    for first_bit, second_bit in zip(bits, bits[::-1]):
        first_more, second_more = to_mem(first_parts, first_bit), to_mem(second_parts, second_bit)
        first_order = first_order + [k | first_bit for k in first_order]
        second_order = second_order + [k | second_bit for k in second_order]
        if len(both) < last:
            both.append(to_next(both[-1]))
        first_more, second_more, both[-1] = tie(first_more, second_more, both[-1])
        first_parts = jnp.concatenate([first_parts, first_more])
        second_parts = jnp.concatenate([second_parts, second_more])
    while len(both) < last:
        both.append(to_next(both[-1]))

    def hold_parts(pack, parts, order):
        spread = jnp.stack([parts[order.index(k)] for k in range(mems)], axis=1)
        return jnp.concatenate([pack[None], spread], axis=0)

    first_held = hold_parts(first_pack, first_parts, first_order)
    first_more = to_core(first_held)
    gate_early = jnp.stack([both[j][0] for j in early])[None]
    linear_early = jnp.stack([both[j][1] for j in early])[None]
    gate_a1 = to_mem(gate_early, bits[0])
    linear_a1 = to_mem(linear_early, bits[-1])
    both.append(to_next(both[-1]))
    second_held = hold_parts(second_pack, second_parts, second_order)
    first_more, gate_a1, linear_a1, both[last], second_held, down_a[0] = tie(
        first_more, gate_a1, linear_a1, both[last], second_held, down_a[0]
    )

    second_more = to_core(second_held)
    gate_late, linear_late = both[last][:1], both[last][1:]
    gate_late_a1 = to_mem(gate_late, bits[0])
    linear_late_a1 = to_mem(linear_late, bits[-1])
    first_mats = matrices(first_held, first_more)
    kc_full, vc_full, qs_full, ks_full = first_mats
    kv_local = kv_fwd(place, source, kc_full, vc_full)
    gate_early = jnp.concatenate([gate_early, gate_a1])
    linear_early = jnp.concatenate([linear_early, linear_a1])
    down_a.append(to_next(down_a[0]))
    kv_local, second_more, gate_late_a1, linear_late_a1, down_a[1], down_b[0], gate_early, linear_early = tie(
        kv_local, second_more, gate_late_a1, linear_late_a1, down_a[1], down_b[0], gate_early, linear_early
    )

    kvs = [to_mem(kv_local[s], s) if s else kv_local[s] for s in range(mems)]
    down_b.append(to_next(down_b[0]))
    down_a.append(to_next(down_a[1]))
    second_mats = matrices(second_held, second_more)
    vs_full, os_full, qc_full, oc_full = second_mats
    tokens, normed, q, k, v, mixed, first_sum, normed_cross, cq = self_fwd(
        depth, length, inputs.reshape(micros, length, width).swapaxes(1, 2), gain_self, qs_full, ks_full, vs_full, os_full, position_bias, gain_cross, qc_full
    )
    kvs, down_a[2], down_b[1], cq, gate_early, linear_early = tie(
        kvs, down_a[2], down_b[1], cq, gate_early, linear_early
    )

    def spread_rest(held, order, over):
        parts = [held]
        for bit in over:
            parts.append(to_mem(jnp.concatenate(parts) if len(parts) > 1 else parts[0], bit))
            order = order + [k | bit for k in order]
        return parts, order

    def sources(parts, order, n):
        places = {}
        at = 0
        for piece in parts:
            for i in range(piece.shape[0]):
                places[order[at]] = (piece, (i, n) if piece.ndim == 4 else (i,), part)
                at += 1
        return [places[k] for k in range(mems)]

    def whole_source(array, listed):
        if part % 16 == 0:
            return listed
        pieces = []
        for piece, index, _ in listed:
            for i in index:
                piece = piece[i]
            pieces.append(piece)
        return [(jnp.concatenate(pieces), (), feed)]

    natural_order = list(range(mems))
    gate_ord = [k for k in natural_order if not k & bits[-1]]
    linear_ord = [k for k in natural_order if not k & bits[0]]
    whole_bits = mems if mems == 4 and part % 16 == 0 else 0

    def halves(grads):
        if whole_bits:
            return (grads[0:2], grads[2:4], grads[4:-3], *grads[-3:])
        shape = (-1, mems, part, width)
        return (
            fold_parts(grads[0].reshape(shape), natural_order, bits[-1]),
            fold_parts(grads[1].reshape(shape), natural_order, bits[0]),
            grads[2:-3],
            *grads[-3:],
        )

    middle = (len(early) + 1) // 2
    starts = [0, middle] if middle < len(early) else [0]
    cuts = [slice(0, middle), slice(middle, len(early))][: len(starts)]
    gate_cuts, linear_cuts = [gate_early[:, c] for c in cuts], [linear_early[:, c] for c in cuts]
    gate_parts, linear_parts = [None] * len(cuts), [None] * len(cuts)
    gate_parts[0], gate_order = spread_rest(gate_cuts[0], [0, bits[0]], bits[1:])
    linear_parts[0], linear_order = spread_rest(linear_cuts[0], [0, bits[-1]], bits[::-1][1:])
    gate_late = jnp.concatenate([gate_late, gate_late_a1])
    linear_late = jnp.concatenate([linear_late, linear_late_a1])
    down_b.append(to_next(down_b[1]))
    cmixed, second_sum, normed_feed = cross_fwd(depth, length, cq, valid, oc_full, first_sum, gain_feed, kvs)
    gate_parts[0], linear_parts[0], gate_late, linear_late, normed_feed, gate_cuts, linear_cuts, down_b[2] = tie(
        gate_parts[0], linear_parts[0], gate_late, linear_late, normed_feed, gate_cuts, linear_cuts, down_b[2]
    )

    nf_other = rows_to_core(normed_feed)
    for n in range(1, len(cuts)):
        gate_parts[n], gate_order = spread_rest(gate_cuts[n], [0, bits[0]], bits[1:])
        linear_parts[n], linear_order = spread_rest(linear_cuts[n], [0, bits[-1]], bits[::-1][1:])
    own_steps = [[[(g.reshape(feed, width), (), feed)] for g in (gate_own, linear_own, down_own)]]
    grads_o = feed_grad(normed_feed, nf_other, og_low, og_other, own_steps, feed, whole_bits, 1)
    while len(down_b) < last:
        down_a.append(to_next(down_a[-1]))
        down_b.append(to_next(down_b[-1]))
    down_a.append(to_next(down_a[-1]))
    gate_parts, linear_parts, down_a[last], down_b[1:], grads_o, nf_other = tie(
        gate_parts, linear_parts, down_a[last], down_b[1:], grads_o, nf_other
    )

    (gate_keep_o, gate_send_o), (linear_keep_o, linear_send_o), (grad_down_o,), *acts_o = halves(grads_o)
    gate_moved_o = to_mem(gate_send_o, bits[-1])
    linear_moved_o = to_mem(linear_send_o, bits[0])
    early_steps = [
        [
            whole_source(None, sources(gate_parts[c], gate_order, n - starts[c])),
            whole_source(None, sources(linear_parts[c], linear_order, n - starts[c])),
            [(p[j].reshape(feed // 2, width), (), feed // 2) for p in (down_a, down_b)],
        ]
        for n, j in enumerate(early)
        for c in [len([1 for at in starts if at <= n]) - 1]
    ]
    gate_late_parts, gate_order = spread_rest(gate_late, [0, bits[0]], bits[1:])
    linear_late_parts, linear_order = spread_rest(linear_late, [0, bits[-1]], bits[::-1][1:])
    down_b.append(to_next(down_b[-1]))
    grads_a = feed_grad(normed_feed, nf_other, og_low, og_other, early_steps, feed, whole_bits)
    grads_a, gate_late_parts, linear_late_parts, down_b[last], nf_more, gate_moved_o, linear_moved_o = tie(
        grads_a, gate_late_parts, linear_late_parts, down_b[last], nf_other, gate_moved_o, linear_moved_o
    )

    (gate_keep, gate_send), (linear_keep, linear_send), grad_down_a, *acts_a = halves(grads_a)
    grad_down_a = [*grad_down_a, grad_down_o]
    down_total = to_next(grad_down_a[0])
    gate_moved = to_mem(gate_send, bits[-1])
    linear_moved = to_mem(linear_send, bits[0])
    late_steps = [
        [
            whole_source(None, sources(gate_late_parts, gate_order, 0)),
            whole_source(None, sources(linear_late_parts, linear_order, 0)),
            [(p[last].reshape(feed // 2, width), (), feed // 2) for p in (down_a, down_b)],
        ]
    ]
    grads_b = feed_grad(normed_feed, nf_more, og_low, og_other, late_steps, feed, whole_bits)
    (gate_b, gate_bs), (linear_b, linear_bs), (grad_down_b,), *acts_b = halves(grads_b)
    all_steps = early_steps + own_steps + late_steps
    all_acts = [(a, n) for a, count in ((acts_a, len(early)), (acts_o, 1), (acts_b, 1)) for n in range(count)]
    nfg_own, nfg_send = feed_sum(
        rows,
        width,
        [step[:2] for step in all_steps],
        [[[(acts[i], (n,), 2 * rows)] for i in (1, 2)] for acts, n in all_acts],
        feed,
    )
    gate_moved, linear_moved, down_total, nfg_send, gate_bs, linear_bs = tie(
        gate_moved, linear_moved, down_total, nfg_send, gate_bs, linear_bs
    )

    def fold_to_last(held, order, over):
        for bit in over[:-1]:
            kept, moved, order = fold_step(held, order, bit)
            held = add_low(kept, moved)
        return held

    nfg_more = rows_to_core(nfg_send)
    half = mems // 2
    if len(bits) == 2:
        both_y = fuse(
            lambda gk, gm, lk, lm, gko, gmo, lko, lmo: [
                [add_low(gk[:, 0], gm[:, 0]), add_low(gko[:, 0], gmo[:, 0])],
                [add_low(gk[:, 1], gm[:, 1]), add_low(gko[:, 1], gmo[:, 1])],
                [add_low(lk[:, 0], lm[:, 0]), add_low(lko[:, 0], lmo[:, 0])],
                [add_low(lk[:, 1], lm[:, 1]), add_low(lko[:, 1], lmo[:, 1])],
            ],
            gate_keep, gate_moved, linear_keep, linear_moved,
            gate_keep_o, gate_moved_o, linear_keep_o, linear_moved_o,
        )
    else:
        gate_keep, gate_moved, linear_keep, linear_moved = [
            jnp.concatenate(pair)
            for pair in (
                (gate_keep, gate_keep_o),
                (gate_moved, gate_moved_o),
                (linear_keep, linear_keep_o),
                (linear_moved, linear_moved_o),
            )
        ]
        gate_y = fold_to_last(add_low(gate_keep, gate_moved), gate_ord, bits[::-1][1:])
        linear_y = fold_to_last(add_low(linear_keep, linear_moved), linear_ord, bits[1:])
        both_y = [gate_y[:, 0], gate_y[:, 1], linear_y[:, 0], linear_y[:, 1]]
    message_y, message_x = fuse(
        lambda gs, ly, ls, gy: [[gs[0], ly], [ls[0], gy]], gate_bs, both_y[3], linear_bs, both_y[1]
    )
    down_next = after(down_total, message_y, message_x)
    for j in early[1:]:
        down_next = to_next(add_low(down_next, grad_down_a[j - 1]))
    message_y, message_x = to_mem(message_y, bits[-1]), to_mem(message_x, bits[0])
    kvg, (grad_gain_feed, grad_co, grad_cq, first_grad, grad_gain_cross) = cross_bwd(
        depth, length, og_low, nfg_own, nfg_more, second_sum, gain_feed, cmixed, cq, valid, oc_full,
        first_sum, gain_cross, normed_cross, qc_full, kvs,
    )
    message_y, message_x, down_next, kvg, grad_gain_cross, hid_b = tie(
        message_y, message_x, down_next, kvg, grad_gain_cross, acts_b[0]
    )

    kvg = [to_mem(kvg[s], s) if s else kvg[s] for s in range(mems)]
    shards = (mems, part, width)
    own = last - 1
    gate_y, linear_y, both_own, ring = fuse(
        lambda g, x, l, y, d, b: [
            add_low(g[:own], x[half:-1]),
            add_low(l[:own], y[half:-1]),
            [add_low(g[own:], x[-1:]), add_low(l[own:], y[-1:])],
            [add_low(d, b), add_low(g[:1], x[half : half + 1]), add_low(l[:1], y[half : half + 1])],
        ],
        both_y[0], message_x, both_y[2], message_y, down_next.reshape(shards), grad_down_b.reshape(shards),
    )
    ring = to_next(ring)
    hid_acts = [(hid_b if a is acts_b else a[0], n) for a, n in all_acts]
    res_own, res_send = feed_sum(
        rows,
        width,
        [step[2:] for step in all_steps],
        [[[(hid, (n,), 2 * rows)]] for hid, n in hid_acts],
        feed,
    )
    grad_os, grad_qs, grad_ks, grad_vs, input_grad, grad_gain_self, score_sum = self_bwd(
        depth, length, first_grad, mixed, q, k, v, position_bias, os_full, qs_full, ks_full, vs_full,
        normed, tokens, gain_self,
    )
    kvg, ring, grad_qs, res_send = tie(kvg, ring, grad_qs, res_send)

    at = early[-1] - 1
    if len(early) == 2:
        (ring_both,) = fuse(
            lambda r, g, l: [[add_low(r[:1], g[at : at + 1]), add_low(r[1:], l[at : at + 1])]],
            ring[mems:], gate_y, linear_y,
        )
        ring_both = to_next(ring_both)
        grad_qs = after(grad_qs, gate_y)
    kept, sent = core_split(
        spot, [g.reshape(chips, 2, slim, width) for g in (grad_qs, grad_ks, grad_vs, grad_os)]
    )
    sent = to_core(sent)
    for j in early[1:-1]:
        ring_both = to_next(add_low(ring[mems:], jnp.stack([gate_y[j - 1], linear_y[j - 1]])))
        ring = jnp.concatenate([ring[:mems], ring_both])
    gate_b, linear_b = gate_b[0], linear_b[0]
    gate_bm, linear_bm = message_y, message_x
    if len(bits) > 2:
        gate_bm, linear_bm = message_y[:half], message_x[:half]
        gate_b = fold_to_last(add_low(gate_b, gate_bm)[None], gate_ord, bits[::-1][1:])[0]
        linear_b = fold_to_last(add_low(linear_b, linear_bm)[None], linear_ord, bits[1:])[0]
        gate_bm, linear_bm = jnp.zeros_like(gate_b), jnp.zeros_like(linear_b)
    if len(early) != 2:
        ring_both = to_next(add_low(ring[mems:], jnp.stack([gate_y[at], linear_y[at]])))
    parts = fuse(
        lambda r, gb, gm, lb, lm, d: [
            add_low(gb[:1], gm[:1]),
            add_low(lb[:1], lm[:1]),
            [add_low(gb[1:2], gm[1:2]), add_low(r[1:2], d[1:2])],
            [add_low(lb[1:2], lm[1:2]), add_low(r[half : half + 1], d[half : half + 1])],
            add_low(r[:1], d[:1]),
            *[add_low(r[k : k + 1], d[k : k + 1]) for k in range(1, mems) if k not in (1, half)],
        ],
        ring[:mems], gate_b, gate_bm, linear_b, linear_bm, grad_down_a[last - 1].reshape(shards),
        limit=60,
    )
    gate_bk, linear_bk, message_x, message_y, down_mine, *down_rest = parts
    others = [k for k in range(1, mems) if k not in (1, half)]
    message_x, message_y = to_mem(message_x, bits[0]), to_mem(message_y, bits[-1])
    down_rest = [to_mem(p, k) for p, k in zip(down_rest, others)]

    def grad_sums(*grads):
        stacked = jnp.stack([g.reshape(seqs, slim, width) for g in grads], axis=1)
        return lax.psum_scatter(stacked.reshape(seqs, len(grads) * slim, width), "seq", scatter_dimension=0)

    cross_first = grad_sums(after(grad_cq, ring), grad_co)
    grad_kc, grad_vc = kv_weights(place, source, kvg, inner)
    sent, ring_both, message_x, message_y, down_rest, grad_kc, kvg[0] = tie(
        sent, ring_both, message_x, message_y, down_rest, grad_kc, kvg[0]
    )

    columns = columns_of(spot, kept, sent, mems)
    columns = [to_mem(p, s) if s else p for s, p in enumerate(columns)]
    ring_both, down_sum = fuse(
        lambda r, g, x, l, y, d, *more: [
            [add_low(r[:1], add_low(g, x[:1])), add_low(r[1:], add_low(l, y[:1]))],
            sum_low([d, x[1:], y[1:], *more]),
        ],
        ring_both, gate_bk, message_x, linear_bk, message_y, down_mine, *down_rest,
    )
    ring_both = to_next(ring_both)
    cross_sum = [grad_sums(grad_kc, grad_vc), cross_first]
    memory_grad = kv_memory(place, source.shape, kc_full, vc_full, kvg)
    score_sum, input_grad = [after(x, columns[1]) for x in (score_sum, input_grad)]
    grad_table = lax.dot_general(
        onehot.astype(f32),
        score_sum.reshape(heads, length * length),
        (((0,), (1,)), ((), ())),
        preferred_element_type=f32,
    )
    table_row = jnp.pad(grad_table.reshape(1, buckets * heads), ((0, 0), (0, width - buckets * heads)))
    small = jnp.concatenate([grad_gain_self, grad_gain_cross, grad_gain_feed, table_row], axis=0)

    def to_rows(value):
        high = value.astype(bf16)
        rest = (value - high.astype(f32)).astype(bf16)
        return jnp.concatenate([high, rest, jnp.zeros((16 - 2 * value.shape[0], width), bf16)])

    def from_rows(value):
        return value[:4].astype(f32) + value[4:8].astype(f32)

    small_rows = to_rows(small)
    columns, ring_both, small_rows, memory_grad = tie(columns, ring_both, small_rows, memory_grad)

    share = 4 * slim // mems
    total = sum_low(columns).reshape(chips, share, width)
    pieces = [
        jnp.concatenate([lax.dynamic_index_in_dim(total, (chip + j) % chips, 0, keepdims=False), small_rows])
        for j in range(chips)
    ]
    pieces = [to_step(p, j) if j else p for j, p in enumerate(pieces)]
    both_sum, message_x, message_y = fuse(
        lambda r, g, d: [add_low(r, g), [add_low(r[:1], g[:1]), d], [add_low(r[1:], g[1:]), d]],
        ring_both, both_own, down_sum,
    )
    message_x, message_y = to_mem(message_x, bits[0]), to_mem(message_y, bits[-1])
    down_rest = [to_mem(down_sum, k) for k in range(1, mems) if k not in (1, half)]
    pieces, message_x, message_y, down_rest, cross_sum, res_send = tie(
        pieces, message_x, message_y, down_rest, cross_sum, res_send
    )

    down_g = [down_sum if k == 0 else message_x[1:] if k == 1 else message_y[1:] if k == half else None for k in range(mems)]
    for k in range(mems):
        if down_g[k] is None:
            down_g[k] = down_rest.pop(0)
    down_g = [p[0] for p in down_g]
    self_mine = sum_low([p[:share] for p in pieces])
    small = jnp.stack([from_rows(p[share:]) for p in pieces])
    small = tree_sum(
        [lax.dynamic_index_in_dim(small, (chip - z) % chips, 0, keepdims=False) for z in range(chips)]
    )
    gate_g, gate_order = [both_sum[:1], message_x[:1]], [0, bits[0]]
    linear_g, linear_order = [both_sum[1:], message_y[:1]], [0, bits[-1]]
    gate_g, gate_order = spread_rest(jnp.concatenate(gate_g), gate_order, bits[1:-1])
    linear_g, linear_order = spread_rest(jnp.concatenate(linear_g), linear_order, bits[::-1][1:-1])
    gate_g, linear_g = joined(gate_g), joined(linear_g)
    small_rows = to_rows(small)
    cut = gate_g.shape[0] * part
    cross_parts = list(quarters(jnp.concatenate(cross_sum)))
    messages = fuse(
        lambda g, l, rows_, *ps: [
            [*([l] if k == 1 else [g] if k == half else []), p, rows_] for k, p in enumerate(ps)
        ],
        gate_g.reshape(cut, width), linear_g.reshape(cut, width), small_rows, *cross_parts,
    )
    cross_parts[0] = messages[0]
    moved = {k: to_mem(p, k) for k, p in enumerate(messages) if k}
    res_more = rows_to_core(res_send)
    moved, small_rows, self_mine, cross_own = tie(moved, small_rows, self_mine, cross_parts[0])
    linear_g = jnp.concatenate([linear_g, moved[1][:cut].reshape(-1, part, width)])
    gate_g = jnp.concatenate([gate_g, moved[half][:cut].reshape(-1, part, width)])
    gate_order = gate_order + [k | half for k in gate_order]
    linear_order = linear_order + [k | 1 for k in linear_order]
    cross_parts = [cross_own] + [moved[k][cut:] if k in (1, half) else moved[k] for k in range(1, mems)]
    small = tree_sum([from_rows(p[share:]) for p in cross_parts])

    mine = jnp.concatenate([self_mine, sum_low([p[:share] for p in cross_parts])])
    mine_g = [mine] + [to_mem(mine, k) for k in range(1, mems)]
    small = small + to_core(small)

    def settle(flat, order):
        return natural([flat[order.index(k)] for k in range(mems)], mem_index).astype(f32)

    gate_out = settle(gate_g, gate_order).reshape(feed, width)
    linear_out = settle(linear_g, linear_order).reshape(feed, width)
    down_out = natural(down_g, mem_index).astype(f32).reshape(feed, width)
    result = second_sum + res_own + res_more.astype(f32)
    mine_g, gate_out, linear_out, down_out = tie(mine_g, gate_out, linear_out, down_out)

    def settled(start, rows_of):
        return natural([p[start : start + rows_of] for p in mine_g], mem_index).astype(f32)

    self_sum = settled(0, share).reshape(4, slim, width)
    cross_sum = settled(share, share).reshape(4, slim, width)
    return (
        result.reshape(inputs.shape),
        input_grad.reshape(inputs.shape),
        memory_grad.swapaxes(2, 3).reshape(memory.shape),
        small[0],
        self_sum[0].T,
        self_sum[1].T,
        self_sum[2].T,
        self_sum[3],
        small[3, : buckets * heads].reshape(buckets, heads),
        small[1],
        cross_sum[2].T,
        cross_sum[0].T,
        cross_sum[1].T,
        cross_sum[3],
        small[2],
        gate_out.T,
        linear_out.T,
        down_out,
    )


def solution(mesh):
    tokens_at = P(None, "seq", "mem", None, None)
    memory_at = P(None, "seq", None, "mem", None)
    columns, row_cut = P(None, "seq"), P("seq", None)
    return jax.shard_map(
        per_device,
        mesh=mesh,
        in_specs=(
            tokens_at,
            memory_at,
            P(None, "seq", None),
            P(None, "seq", None, "mem"),
            P(),
            columns,
            columns,
            columns,
            row_cut,
            P(),
            P(),
            columns,
            columns,
            columns,
            row_cut,
            P(),
            columns,
            columns,
            row_cut,
            tokens_at,
        ),
        out_specs=(
            tokens_at,
            tokens_at,
            memory_at,
            P(),
            columns,
            columns,
            columns,
            row_cut,
            P(),
            P(),
            columns,
            columns,
            columns,
            row_cut,
            P(),
            columns,
            columns,
            row_cut,
        ),
        check_vma=False,
    )
```

```python
import functools
import math

import jax
import jax.numpy as jnp
from jax import lax
from jax.experimental import pallas as pl
from jax.experimental.pallas import tpu as pltpu
from jax.sharding import PartitionSpec as P

norm_eps = 1e-06
masked_score = -1e30
bf16 = jnp.bfloat16
f32 = jnp.float32


def bucket_edges():
    return [math.ceil(16 * 8 ** ((number - 16) / 16)) for number in range(17, 32)]


def position_buckets(length):
    row_index = jnp.arange(length, dtype=jnp.int32)
    offset = jnp.maximum(row_index[:, None] - row_index[None, :], 0)
    bucket = jnp.minimum(offset, 16)
    for threshold in bucket_edges():
        bucket = bucket + (offset >= threshold).astype(jnp.int32)
    return bucket


def matmul(left, right):
    return jnp.dot(left, right, preferred_element_type=f32)


def contract_rows(left, right):
    return lax.dot_general(left, right, (((0,), (0,)), ((), ())), preferred_element_type=f32)


def contract_cols(left, right):
    return lax.dot_general(left, right, (((1,), (1,)), ((), ())), preferred_element_type=f32)


def add_low(left, right):
    return (left.astype(f32) + right.astype(f32)).astype(bf16)


def to_core(value):
    count = lax.axis_size("seq")
    return lax.ppermute(value, "seq", [(i, i ^ 1) for i in range(count)])


def rows_to_core(value):
    return to_core(value.reshape(-1, 64, value.shape[-1])).reshape(value.shape)


def to_next(value):
    count = lax.axis_size("seq")
    return lax.ppermute(value, "seq", [(i, (i + 2) % count) for i in range(count)])


def to_mem(value, mask):
    count = lax.axis_size("mem")
    return lax.ppermute(value, "mem", [(i, i ^ mask) for i in range(count)])


def mem_bits():
    return [1 << b for b in range((lax.axis_size("mem") - 1).bit_length())]


def to_step(value, step):
    count = lax.axis_size("seq")
    return lax.ppermute(value, "seq", [(i, (i + 2 * step) % count) for i in range(count)])


def to_seq(value, mask):
    count = lax.axis_size("seq")
    return lax.ppermute(value, "seq", [(i, i ^ mask) for i in range(count)])


def after(value, *others):
    return lax.optimization_barrier((value, *others))[0]


def ring_gather(value):
    pieces = [value]
    for _ in range(lax.axis_size("seq") // 2 - 1):
        pieces.append(to_next(pieces[-1]))
    return pieces


def ring_sum(pieces):
    total = pieces[1]
    for piece in pieces[2:]:
        total = add_low(to_next(total), piece)
    return add_low(to_next(total), pieces[0])


def spread_gather(value, bits):
    held, order = value[None], [0]
    for bit in bits:
        held = jnp.concatenate([held, to_mem(held, bit)], axis=0)
        order = order + [k | bit for k in order]
    return [held[order.index(k)] for k in range(len(order))]


def fold(held, bits):
    order = list(range(held.shape[0]))
    for bit in bits:
        keep = [i for i, k in enumerate(order) if not k & bit]
        send = [order.index(order[i] | bit) for i in keep]
        moved = to_mem(jnp.stack([held[i] for i in send]), bit)
        held = jnp.stack([add_low(held[i], moved[n]) for n, i in enumerate(keep)])
        order = [order[i] for i in keep]
    return held[0]


def sum_low(pieces):
    total = pieces[0].astype(f32)
    for piece in pieces[1:]:
        total = total + piece.astype(f32)
    return total.astype(bf16)


def direct_fold(pieces):
    return sum_low([to_mem(p, k) if k else p for k, p in enumerate(pieces)])


def natural(pieces, mem_index):
    stacked = jnp.stack(pieces)
    return jnp.stack(
        [
            lax.dynamic_index_in_dim(stacked, mem_index ^ k, 0, keepdims=False)
            for k in range(len(pieces))
        ]
    )


def back_to_mem(value, mem_index):
    pieces = [to_mem(value, k) if k else value for k in range(lax.axis_size("mem"))]
    return natural(pieces, mem_index).astype(f32)


def assemble_kernel(spot, own, other, *outs):
    chips = own.shape[0]
    core, chip = spot[0], spot[1]
    for q, out in enumerate(outs):
        for j in range(chips):
            at = lax.rem(chip - j + chips, chips) * 2
            out[at + core] = own[j, spot[2 + q]]
            out[at + 1 - core] = other[j, spot[2 + q]]


def assemble(spot, own, other):
    chips, mems, share, width = own.shape
    vmem = pl.BlockSpec(memory_space=pltpu.VMEM)
    return pl.pallas_call(
        assemble_kernel,
        in_specs=[pl.BlockSpec(memory_space=pltpu.SMEM), vmem, vmem],
        out_shape=[jax.ShapeDtypeStruct((2 * chips, share, width), bf16)] * mems,
        compiler_params=params(26),
        cost_estimate=cost(3),
        name="assemble",
    )(spot, own, other)


def params(limit_mb=56):
    return pltpu.CompilerParams(vmem_limit_bytes=limit_mb * 1024 * 1024)


def cost(micro_seconds):
    return pl.CostEstimate(
        flops=micro_seconds * 10**9, bytes_accessed=micro_seconds * 3 * 10**6, transcendentals=0
    )


def row_norm(value):
    return lax.rsqrt(jnp.mean(value * value, axis=-1, keepdims=True) + norm_eps)


def norm_back_rows(value, gain, upstream):
    scale = row_norm(value)
    weighted = upstream * gain
    mean_dot = jnp.mean(weighted * value, axis=-1, keepdims=True)
    gain_grad = jnp.sum(upstream * value * scale, axis=0, keepdims=True)
    return weighted * scale - value * (scale * scale * scale * mean_dot), gain_grad


def lane_head(length, depth):
    return lax.broadcasted_iota(jnp.int32, (length, 128), 1) // depth


def self_fwd_kernel(depth, length, tok, g1, qw, kw, vw, ow, bias, g2, cw, tok_o, normed_o, q_o, k_o, v_o, mixed_o, first_o, nc_o, cq_o):
    for m in range(tok.shape[0]):
        tok_o[m * length : (m + 1) * length] = tok[m].astype(f32).T.astype(bf16)
    x = tok_o[...].astype(f32)
    normed = (x * row_norm(x) * g1[...]).astype(bf16)
    normed_o[...] = normed
    q_o[...] = contract_cols(normed, qw[...]).astype(bf16)
    k_o[...] = contract_cols(normed, kw[...]).astype(bf16)
    v_o[...] = contract_cols(normed, vw[...]).astype(bf16)
    inner = qw.shape[0]
    groups, share = inner // 128, 128 // depth
    lanes = lane_head(length, depth)

    def body(step, carry):
        micro, group = step // groups, step % groups
        rows = pl.ds(pl.multiple_of(micro * length, length), length)
        cols = pl.ds(pl.multiple_of(group * 128, 128), 128)
        q, k, v = q_o[rows, cols], k_o[rows, cols], v_o[rows, cols]
        out = jnp.zeros((length, 128), f32)
        for a in range(share):
            s = contract_cols(jnp.where(lanes == a, q, 0), k) + bias[group * share + a]
            e = jnp.exp(s - jnp.max(s, axis=-1, keepdims=True))
            p = (e / jnp.sum(e, axis=-1, keepdims=True)).astype(bf16)
            out = jnp.where(lanes == a, matmul(p, v), out)
        mixed_o[rows, cols] = out.astype(bf16)
        return carry

    lax.fori_loop(0, x.shape[0] // length * groups, body, 0)
    first = tok_o[...].astype(f32) + matmul(mixed_o[...], ow[...])
    first_o[...] = first
    nc = (first * row_norm(first) * g2[...]).astype(bf16)
    nc_o[...] = nc
    cq_o[...] = contract_cols(nc, cw[...]).astype(bf16)


def self_fwd(depth, length, tok, g1, qw, kw, vw, ow, bias, g2, cw):
    rows, width = tok.shape[0] * tok.shape[2], tok.shape[1]
    inner = qw.shape[0]
    low, slim = jax.ShapeDtypeStruct((rows, width), bf16), jax.ShapeDtypeStruct((rows, inner), bf16)
    return pl.pallas_call(
        functools.partial(self_fwd_kernel, depth, length),
        out_shape=(low, low, slim, slim, slim, slim, jax.ShapeDtypeStruct((rows, width), f32), low, slim),
        compiler_params=params(40),
        cost_estimate=cost(16),
        name="self_fwd",
    )(tok, g1, qw, kw, vw, ow, bias, g2, cw)


def cross_fwd_kernel(depth, length, parts, cq, mask, ow, first, g3, *refs):
    kvs, (mixed_o, second_o, nf_o) = refs[:parts], refs[parts:]
    inner = ow.shape[0]
    groups, share = inner // 128, 128 // depth
    lanes = lane_head(length, depth)

    def body(step, carry):
        micro, group = step // groups, step % groups
        rows = pl.ds(pl.multiple_of(micro * length, length), length)
        cols = pl.ds(pl.multiple_of(group * 128, 128), 128)
        vcols = pl.ds(pl.multiple_of(inner + group * 128, 128), 128)
        q = cq[rows, cols]
        k = jnp.concatenate([kv[micro, :, cols] for kv in kvs], axis=0)
        v = jnp.concatenate([kv[micro, :, vcols] for kv in kvs], axis=0)
        out = jnp.zeros((length, 128), f32)
        for a in range(share):
            s = contract_cols(jnp.where(lanes == a, q, 0), k)
            s = jnp.where(mask[micro] > 0, s, masked_score)
            e = jnp.exp(s - jnp.max(s, axis=-1, keepdims=True))
            p = (e / jnp.sum(e, axis=-1, keepdims=True)).astype(bf16)
            out = jnp.where(lanes == a, matmul(p, v), out)
        mixed_o[rows, cols] = out.astype(bf16)
        return carry

    lax.fori_loop(0, cq.shape[0] // length * groups, body, 0)
    second = first[...] + matmul(mixed_o[...], ow[...])
    second_o[...] = second
    nf_o[...] = (second * row_norm(second) * g3[...]).astype(bf16)


def cross_fwd(depth, length, cq, mask, ow, first, g3, kvs):
    rows, width = first.shape
    return pl.pallas_call(
        functools.partial(cross_fwd_kernel, depth, length, len(kvs)),
        out_shape=(
            jax.ShapeDtypeStruct(cq.shape, bf16),
            jax.ShapeDtypeStruct((rows, width), f32),
            jax.ShapeDtypeStruct((rows, width), bf16),
        ),
        compiler_params=params(36),
        cost_estimate=cost(15),
        name="cross_fwd",
    )(cq, mask, ow, first, g3, *kvs)


def cross_bwd_kernel(depth, length, parts, og, nf_own, nf_more, second, g3, mixed, cq, mask, ow, first, g2, nc, qw, *refs):
    kvs = refs[:parts]
    kvg = refs[parts : 2 * parts]
    g3_o, dow_o, dqw_o, firstg_o, g2_o, mixg, dq = refs[2 * parts :]
    inner = ow.shape[0]
    slots = kvs[0].shape[1]
    groups, share = inner // 128, 128 // depth
    lanes = lane_head(length, depth)
    part, gain = norm_back_rows(second[...], g3[...], nf_own[...] + nf_more[...].astype(f32))
    g3_o[...] = gain
    second_grad = og[...].astype(f32) + part
    firstg_o[...] = second_grad
    low = second_grad.astype(bf16)
    dow_o[...] = contract_rows(mixed[...], low).astype(bf16)
    mixg[...] = contract_cols(low, ow[...]).astype(bf16)

    def body(step, carry):
        micro, group = step // groups, step % groups
        rows = pl.ds(pl.multiple_of(micro * length, length), length)
        cols = pl.ds(pl.multiple_of(group * 128, 128), 128)
        vcols = pl.ds(pl.multiple_of(inner + group * 128, 128), 128)
        q, o = cq[rows, cols], mixg[rows, cols]
        k = jnp.concatenate([kv[micro, :, cols] for kv in kvs], axis=0)
        v = jnp.concatenate([kv[micro, :, vcols] for kv in kvs], axis=0)
        q_grad = jnp.zeros((length, 128), f32)
        k_grad = jnp.zeros((parts * slots, 128), f32)
        v_grad = jnp.zeros((parts * slots, 128), f32)
        for a in range(share):
            qa, oa = jnp.where(lanes == a, q, 0), jnp.where(lanes == a, o, 0)
            s = contract_cols(qa, k)
            s = jnp.where(mask[micro] > 0, s, masked_score)
            e = jnp.exp(s - jnp.max(s, axis=-1, keepdims=True))
            p = e / jnp.sum(e, axis=-1, keepdims=True)
            v_grad += contract_rows(p.astype(bf16), oa)
            dp = contract_cols(oa, v)
            ds = (p * (dp - jnp.sum(p * dp, axis=-1, keepdims=True))).astype(bf16)
            q_grad = jnp.where(lanes == a, matmul(ds, k), q_grad)
            k_grad += contract_rows(ds, qa)
        dq[rows, cols] = q_grad.astype(bf16)
        for t in range(parts):
            kvg[t][micro, :, cols] = k_grad[t * slots : (t + 1) * slots].astype(bf16)
            kvg[t][micro, :, vcols] = v_grad[t * slots : (t + 1) * slots].astype(bf16)
        return carry

    lax.fori_loop(0, cq.shape[0] // length * groups, body, 0)
    dqw_o[...] = contract_rows(dq[...], nc[...]).astype(bf16)
    part, gain = norm_back_rows(first[...], g2[...], matmul(dq[...], qw[...]))
    g2_o[...] = gain
    firstg_o[...] = firstg_o[...] + part


def cross_bwd(depth, length, og, nf_own, nf_more, second, g3, mixed, cq, mask, ow, first, g2, nc, qw, kvs):
    rows, width = first.shape
    gain = jax.ShapeDtypeStruct((1, width), f32)
    weight = jax.ShapeDtypeStruct(ow.shape, bf16)
    out = pl.pallas_call(
        functools.partial(cross_bwd_kernel, depth, length, len(kvs)),
        out_shape=(
            *[jax.ShapeDtypeStruct(kv.shape, bf16) for kv in kvs],
            gain,
            weight,
            weight,
            jax.ShapeDtypeStruct((rows, width), f32),
            gain,
        ),
        scratch_shapes=[pltpu.VMEM(cq.shape, bf16), pltpu.VMEM(cq.shape, bf16)],
        compiler_params=params(50),
        cost_estimate=cost(31),
        name="cross_bwd",
    )(og, nf_own, nf_more, second, g3, mixed, cq, mask, ow, first, g2, nc, qw, *kvs)
    return out[: len(kvs)], out[len(kvs) :]


def self_bwd_kernel(depth, length, first_grad, mixed, q, k, v, bias, ow, qw, kw, vw, normed, tok, g1, dow_o, dqw_o, dkw_o, dvw_o, ing_o, g1_o, ds_o, mixg, dq, dk, dv):
    inner = ow.shape[0]
    groups, share = inner // 128, 128 // depth
    lanes = lane_head(length, depth)
    low = first_grad[...].astype(bf16)
    dow_o[...] = contract_rows(mixed[...], low).astype(bf16)
    mixg[...] = contract_cols(low, ow[...]).astype(bf16)

    def body(group, carry):
        cols = pl.ds(pl.multiple_of(group * 128, 128), 128)
        total = [jnp.zeros((length, length), f32) for _ in range(share)]
        for micro in range(tok.shape[0] // length):
            rows = slice(micro * length, (micro + 1) * length)
            qs, ks, vs, o = q[rows, cols], k[rows, cols], v[rows, cols], mixg[rows, cols]
            q_grad = jnp.zeros((length, 128), f32)
            k_grad = jnp.zeros((length, 128), f32)
            v_grad = jnp.zeros((length, 128), f32)
            for a in range(share):
                qa, oa = jnp.where(lanes == a, qs, 0), jnp.where(lanes == a, o, 0)
                s = contract_cols(qa, ks) + bias[group * share + a]
                e = jnp.exp(s - jnp.max(s, axis=-1, keepdims=True))
                p = e / jnp.sum(e, axis=-1, keepdims=True)
                v_grad += contract_rows(p.astype(bf16), oa)
                dp = contract_cols(oa, vs)
                ds = (p * (dp - jnp.sum(p * dp, axis=-1, keepdims=True))).astype(bf16)
                total[a] = total[a] + ds.astype(f32)
                q_grad = jnp.where(lanes == a, matmul(ds, ks), q_grad)
                k_grad += contract_rows(ds, qa)
            dq[rows, cols] = q_grad.astype(bf16)
            dk[rows, cols] = k_grad.astype(bf16)
            dv[rows, cols] = v_grad.astype(bf16)
        for a in range(share):
            ds_o[group * share + a] = total[a]
        return carry

    lax.fori_loop(0, groups, body, 0)
    dqw_o[...] = contract_rows(dq[...], normed[...]).astype(bf16)
    dkw_o[...] = contract_rows(dk[...], normed[...]).astype(bf16)
    dvw_o[...] = contract_rows(dv[...], normed[...]).astype(bf16)
    up = matmul(dq[...], qw[...]) + matmul(dk[...], kw[...]) + matmul(dv[...], vw[...])
    part, gain = norm_back_rows(tok[...].astype(f32), g1[...], up)
    g1_o[...] = gain
    ing_o[...] = first_grad[...] + part


def self_bwd(depth, length, first_grad, mixed, q, k, v, bias, ow, qw, kw, vw, normed, tok, g1):
    rows, width = tok.shape
    weight = jax.ShapeDtypeStruct(ow.shape, bf16)
    return pl.pallas_call(
        functools.partial(self_bwd_kernel, depth, length),
        out_shape=(
            weight,
            weight,
            weight,
            weight,
            jax.ShapeDtypeStruct((rows, width), f32),
            jax.ShapeDtypeStruct((1, width), f32),
            jax.ShapeDtypeStruct(bias.shape, f32),
        ),
        scratch_shapes=[pltpu.VMEM(q.shape, bf16)] * 4,
        compiler_params=params(42),
        cost_estimate=cost(21),
        name="self_bwd",
    )(first_grad, mixed, q, k, v, bias, ow, qw, kw, vw, normed, tok, g1)


def kv_fwd_kernel(place, source, kw, vw, *outs):
    rows = source[0, 0]
    both = [
        lax.dot_general(rows, w[...], (((0,), (1,)), ((), ())), preferred_element_type=f32).astype(bf16)
        for w in (kw, vw)
    ]
    for s, out in enumerate(outs):

        @pl.when(pl.program_id(0) == s)
        def write(out=out):
            out[0] = jnp.concatenate(both, axis=1)


def kv_fwd(place, memory, kw, vw):
    micros, pairs, width, slots = memory.shape
    inner = kw.shape[0]
    whole = pl.BlockSpec((inner, width), lambda s, m, place: (0, 0))
    return pl.pallas_call(
        kv_fwd_kernel,
        grid_spec=pltpu.PrefetchScalarGridSpec(
            num_scalar_prefetch=1,
            grid=(pairs, micros),
            in_specs=[
                pl.BlockSpec((1, 1, width, slots), lambda s, m, place: (m, place[s], 0, 0)),
                whole,
                whole,
            ],
            out_specs=[
                pl.BlockSpec(
                    (1, slots, 2 * inner),
                    lambda s, m, place, t=t: (jnp.where(s < t, 0, jnp.where(s == t, m, micros - 1)), 0, 0),
                )
                for t in range(pairs)
            ],
        ),
        out_shape=[jax.ShapeDtypeStruct((micros, slots, 2 * inner), bf16)] * pairs,
        compiler_params=params(20),
        cost_estimate=cost(9),
        name="kv_fwd",
    )(place, memory, kw, vw)


def kv_weights_kernel(place, source, *refs):
    kvgs, (dkw_o, dvw_o, acc) = refs[:-3], refs[-3:]
    inner = dkw_o.shape[0]
    pair = pl.program_id(0)
    step = pair * pl.num_programs(1) + pl.program_id(1)

    @pl.when(step == 0)
    def clear():
        acc[...] = jnp.zeros_like(acc)

    grads = kvgs[0][0]
    for t in range(1, len(kvgs)):
        grads = jnp.where(pair == t, kvgs[t][0], grads)
    acc[...] += lax.dot_general(
        grads, source[0, 0], (((0,), (1,)), ((), ())), preferred_element_type=f32
    )

    @pl.when(step == pl.num_programs(0) * pl.num_programs(1) - 1)
    def write():
        dkw_o[...] = acc[:inner].astype(bf16)
        dvw_o[...] = acc[inner:].astype(bf16)


def kv_memory_kernel(place, kw, vw, *refs):
    kvgs, out = refs[:-1], refs[-1]
    inner = kw.shape[0]
    pair = pl.program_id(0)
    grads = kvgs[0][0]
    for t in range(1, len(kvgs)):
        grads = jnp.where(pair == t, kvgs[t][0], grads)
    out[0, 0] = lax.dot_general(
        kw[...], grads[:, :inner], (((0,), (1,)), ((), ())), preferred_element_type=f32
    ) + lax.dot_general(
        vw[...], grads[:, inner:], (((0,), (1,)), ((), ())), preferred_element_type=f32
    )


def kv_specs(pairs, micros, slots, inner, width):
    whole = pl.BlockSpec((inner, width), lambda s, m, place: (0, 0))
    block = pl.BlockSpec((1, 1, width, slots), lambda s, m, place: (m, place[s], 0, 0))
    pieces = [
        pl.BlockSpec(
            (1, slots, 2 * inner),
            lambda s, m, place, t=t: (jnp.where(s < t, 0, jnp.where(s == t, m, micros - 1)), 0, 0),
        )
        for t in range(pairs)
    ]
    return whole, block, pieces


def kv_weights(place, memory, kvgs, inner):
    micros, pairs, width, slots = memory.shape
    whole, block, pieces = kv_specs(pairs, micros, slots, inner, width)
    weight = jax.ShapeDtypeStruct((inner, width), bf16)
    return pl.pallas_call(
        kv_weights_kernel,
        grid_spec=pltpu.PrefetchScalarGridSpec(
            num_scalar_prefetch=1,
            grid=(pairs, micros),
            in_specs=[block, *pieces],
            out_specs=(whole, whole),
            scratch_shapes=[pltpu.VMEM((2 * inner, width), f32)],
        ),
        out_shape=(weight, weight),
        compiler_params=params(24),
        cost_estimate=cost(9),
        name="kv_weights",
    )(place, memory, *kvgs)


def kv_memory(place, shape, kw, vw, kvgs):
    micros, pairs, width, slots = shape
    inner = kw.shape[0]
    whole, block, pieces = kv_specs(pairs, micros, slots, inner, width)
    return pl.pallas_call(
        kv_memory_kernel,
        grid_spec=pltpu.PrefetchScalarGridSpec(
            num_scalar_prefetch=1,
            grid=(pairs, micros),
            in_specs=[whole, whole, *pieces],
            out_specs=block,
        ),
        out_shape=jax.ShapeDtypeStruct(shape, f32),
        compiler_params=params(20),
        cost_estimate=cost(10),
        name="kv_memory",
    )(place, kw, vw, *kvgs)


gelu_c = math.sqrt(2 / math.pi)


def plan(steps):
    arrays, out = [], []
    for buffers in steps:
        out.append([])
        for n, sources in enumerate(buffers):
            at = 0
            for array, index, rows in sources:
                found = [i for i, known in enumerate(arrays) if known is array]
                if not found:
                    arrays.append(array)
                out[-1].append((found[0] if found else len(arrays) - 1, index, n, at, rows))
                at += rows
    return arrays, out


def fetch(places, refs, hold, sems, step, slot):
    copies = []
    for i, (which, index, n, at, rows) in enumerate(places[step]):
        src = refs[which].at[index] if index else refs[which]
        copies.append(pltpu.make_async_copy(src, hold.at[slot, n, pl.ds(at, rows)], sems.at[slot, i]))
    return copies


def run_fetch(places, refs, hold, sems):
    step = pl.program_id(0)
    for i in range(len(places)):

        @pl.when(step == i)
        def move(i=i):
            if i == 0:
                for copy in fetch(places, refs, hold, sems, 0, 0):
                    copy.start()
            if i + 1 < len(places):
                for copy in fetch(places, refs, hold, sems, i + 1, (i + 1) % 2):
                    copy.start()
            for copy in fetch(places, refs, hold, sems, i, i % 2):
                copy.wait()


def feed_grad_kernel(places, count, mems, *refs):
    nf_a, nf_b, og_a, og_b = refs[:4]
    weights = refs[4 : 4 + count]
    split = 2 if mems else 1
    dgw_o, dlw_o = refs[4 + count : 4 + count + split], refs[4 + count + split : 4 + count + 2 * split]
    steps = len(places)
    ddw_o = refs[4 + count + 2 * split : 4 + count + 2 * split + steps]
    hid_o, gl_o, ll_o, nf, og, hold, sems, whole_sems = refs[4 + count + 2 * split + steps :]
    rows = nf_a.shape[0]
    step = pl.program_id(0)

    def loads():
        return [
            pltpu.make_async_copy(src, dst.at[pl.ds(at, rows)], whole_sems.at[i])
            for i, (src, dst, at) in enumerate([(nf_a, nf, 0), (nf_b, nf, rows), (og_a, og, 0), (og_b, og, rows)])
        ]

    @pl.when(step == 0)
    def load():
        for copy in loads():
            copy.start()

    run_fetch(places, weights, hold, sems)

    @pl.when(step == 0)
    def loaded():
        for copy in loads():
            copy.wait()

    slot = lax.rem(step, 2)
    x, up = nf[...], og[...]
    g = contract_cols(x, hold[slot, 0])
    lin = contract_cols(x, hold[slot, 1])
    hg = contract_cols(up, hold[slot, 2])
    t = jnp.tanh(gelu_c * (g + 0.044715 * (g * g * g)))
    act = 0.5 * g * (1.0 + t)
    slope = 0.5 * (1.0 + t) + 0.5 * g * (1.0 - t * t) * (gelu_c * (1.0 + 3 * 0.044715 * (g * g)))
    hidden = (act * lin).astype(bf16)
    gl = (hg * lin * slope).astype(bf16)
    ll = (hg * act).astype(bf16)
    hid_o[0] = hidden
    gl_o[0] = gl
    ll_o[0] = ll
    for outs, upstream, bit in ((dgw_o, gl, mems // 2), (dlw_o, ll, 1)):
        grad = contract_rows(upstream, x).astype(bf16)
        if not mems:
            outs[0][0] = grad
            continue
        part = grad.shape[0] // mems
        for k in range(mems):
            at = [i for i in range(mems) if (i & bit) == (k & bit)].index(k)
            outs[1 if k & bit else 0][0, at] = grad[k * part : (k + 1) * part]
    down_grad = contract_rows(hidden, up).astype(bf16)

    for i, out in enumerate(ddw_o):

        @pl.when(step == i)
        def write(out=out):
            out[...] = down_grad


def feed_grad(nf_a, nf_b, og_a, og_b, steps, block, mems, price=13):
    rows, width = nf_a.shape
    weights, places = plan(steps)
    n = len(steps)
    any_spec = pl.BlockSpec(memory_space=pl.ANY)
    tile = pl.BlockSpec((1, block, width), lambda i: (i, 0, 0))
    column = pl.BlockSpec((1, 2 * rows, block), lambda i: (i, 0, 0))
    weight = jax.ShapeDtypeStruct((n, block, width), bf16)
    act = jax.ShapeDtypeStruct((n, 2 * rows, block), bf16)
    half_tile, half = tile, weight
    if mems:
        half_tile = pl.BlockSpec((1, mems // 2, block // mems, width), lambda i: (i, 0, 0, 0))
        half = jax.ShapeDtypeStruct((n, mems // 2, block // mems, width), bf16)
    count = 4 if mems else 2
    return pl.pallas_call(
        functools.partial(feed_grad_kernel, places, len(weights), mems),
        grid=(n,),
        in_specs=[any_spec] * (4 + len(weights)),
        out_specs=(
            *[half_tile] * count,
            *[pl.BlockSpec((block, width), lambda i: (0, 0))] * n,
            column,
            column,
            column,
        ),
        out_shape=(
            *[half] * count,
            *[jax.ShapeDtypeStruct((block, width), bf16)] * n,
            act,
            act,
            act,
        ),
        scratch_shapes=[
            pltpu.VMEM((2 * rows, width), bf16),
            pltpu.VMEM((2 * rows, width), bf16),
            pltpu.VMEM((2, 3, block, width), bf16),
            pltpu.SemaphoreType.DMA((2, max(len(p) for p in places))),
            pltpu.SemaphoreType.DMA((4,)),
        ],
        compiler_params=params(54),
        cost_estimate=cost(price * n),
        name="feed_grad",
    )(nf_a, nf_b, og_a, og_b, *weights)


def feed_sum_kernel(places, act_places, count, act_count, *refs):
    weights, acts = refs[:count], refs[count : count + act_count]
    own_o, other_o, other, hold, acts_hold, sems, act_sems = refs[count + act_count :]
    step = pl.program_id(0)
    rows = own_o.shape[0]
    run_fetch(places, weights, hold, sems)
    run_fetch(act_places, acts, acts_hold, act_sems)
    slot = lax.rem(step, 2)
    total = matmul(acts_hold[slot, 0], hold[slot, 0])
    for m in range(1, hold.shape[1]):
        total = total + matmul(acts_hold[slot, m], hold[slot, m])

    @pl.when(step == 0)
    def first():
        own_o[...] = total[:rows]
        other[...] = total[rows:]

    @pl.when(step > 0)
    def later():
        own_o[...] += total[:rows]
        other[...] += total[rows:]

    @pl.when(step == pl.num_programs(0) - 1)
    def last():
        other_o[...] = other[...].astype(bf16)


def feed_sum(rows, width, steps, act_steps, block):
    weights, places = plan(steps)
    acts, act_places = plan(act_steps)
    count = len(steps[0])
    whole = pl.BlockSpec((rows, width), lambda i: (0, 0))
    return pl.pallas_call(
        functools.partial(feed_sum_kernel, places, act_places, len(weights), len(acts)),
        grid=(len(steps),),
        in_specs=[pl.BlockSpec(memory_space=pl.ANY)] * (len(weights) + len(acts)),
        out_specs=(whole, whole),
        out_shape=(jax.ShapeDtypeStruct((rows, width), f32), jax.ShapeDtypeStruct((rows, width), bf16)),
        scratch_shapes=[
            pltpu.VMEM((rows, width), f32),
            pltpu.VMEM((2, count, block, width), bf16),
            pltpu.VMEM((2, count, 2 * rows, block), bf16),
            pltpu.SemaphoreType.DMA((2, max(len(p) for p in places))),
            pltpu.SemaphoreType.DMA((2, max(len(p) for p in act_places))),
        ],
        compiler_params=params(48),
        cost_estimate=cost(1 if count == 1 else 23),
        name="feed_sum",
    )(*weights, *acts)


def joined(value):
    return jnp.concatenate(value) if isinstance(value, list) else value


def fuse(fn, *arrays, limit=0):
    shapes = jax.eval_shape(lambda *a: [joined(o) for o in fn(*a)], *arrays)
    if any(a.shape[-2] % 16 for a in (*arrays, *shapes)):
        return [joined(o) for o in fn(*arrays)]

    limit = limit or 6 + sum(math.prod(a.shape) for a in (*arrays, *shapes)) * 4 // 2**20

    def kernel(*refs):
        for out, value in zip(refs[len(arrays) :], fn(*[ref[...] for ref in refs[: len(arrays)]])):
            at = 0
            for piece in value if isinstance(value, list) else [value]:
                out[at : at + piece.shape[0]] = piece
                at += piece.shape[0]

    return pl.pallas_call(
        kernel, out_shape=shapes, compiler_params=params(limit), cost_estimate=cost(3), name="fuse"
    )(*arrays)


def core_split_kernel(spot, *refs):
    grads, (kept, sent) = refs[:-2], refs[-2:]
    core = spot[0]
    for i, grad in enumerate(grads):
        for z in range(grad.shape[0]):
            kept[z, i] = grad[z, core]
            sent[z, i] = grad[z, 1 - core]


def core_split(spot, grads):
    chips, _, slim, width = grads[0].shape
    shape = jax.ShapeDtypeStruct((chips, len(grads), slim, width), bf16)
    return pl.pallas_call(
        core_split_kernel,
        in_specs=[pl.BlockSpec(memory_space=pltpu.SMEM)] + [pl.BlockSpec(memory_space=pltpu.VMEM)] * len(grads),
        out_shape=(shape, shape),
        compiler_params=params(60),
        cost_estimate=cost(4),
        name="core_split",
    )(spot, *grads)


def columns_kernel(spot, kept, moved, *outs):
    chips = kept.shape[0]
    for k, out in enumerate(outs):
        for z in range(chips):
            out[z] = add_low(kept[z, spot[2 + k]], moved[z, spot[2 + k]])


def columns_of(spot, kept, moved, mems):
    chips, count, slim, width = kept.shape
    if count != mems:
        total = add_low(kept, moved).reshape(chips, mems, -1, width)
        return [lax.dynamic_index_in_dim(total, spot[2 + k], 1, keepdims=False) for k in range(mems)]
    vmem = pl.BlockSpec(memory_space=pltpu.VMEM)
    return pl.pallas_call(
        columns_kernel,
        in_specs=[pl.BlockSpec(memory_space=pltpu.SMEM), vmem, vmem],
        out_shape=[jax.ShapeDtypeStruct((chips, slim, width), bf16)] * mems,
        compiler_params=params(18),
        cost_estimate=cost(4),
        name="columns",
    )(spot, kept, moved)


def tree_sum(values):
    while len(values) > 1:
        values = [left + right for left, right in zip(values[::2], values[1::2])]
    return values[0]


def tie(*values):
    return lax.optimization_barrier(values)


def fold_parts(held, order, bit):
    keep = [i for i, k in enumerate(order) if not k & bit]
    send = [order.index(order[i] | bit) for i in keep]
    return [jnp.stack([held[:, i] for i in at], axis=1) for at in (keep, send)]


def fold_step(held, order, bit):
    kept, sent = fold_parts(held, order, bit)
    return kept, to_mem(sent, bit), [k for k in order if not k & bit]


def per_device(
    inputs,
    memory,
    memory_lengths,
    keep_mask,
    norm_self,
    query_self,
    key_self,
    value_self,
    output_self,
    bias_table,
    norm_cross,
    query_cross,
    key_cross,
    value_cross,
    output_cross,
    norm_feed,
    gate_feed,
    linear_feed,
    down_feed,
    output_grad,
):
    micros = inputs.shape[0]
    length = inputs.shape[3]
    width = inputs.shape[4]
    pairs = memory.shape[2]
    slots = memory.shape[3]
    heads = bias_table.shape[1]
    buckets = bias_table.shape[0]
    seqs = lax.axis_size("seq")
    mems = lax.axis_size("mem")
    chips = seqs // 2
    slim = query_self.shape[1]
    inner = slim * seqs
    depth = inner // heads
    feed = gate_feed.shape[1]
    part = feed // mems
    rows = micros * length
    seq_index = lax.axis_index("seq")
    core = seq_index % 2
    chip = seq_index // 2
    mem_index = lax.axis_index("mem")
    gain_self = norm_self.astype(f32)
    gain_cross = norm_cross.astype(f32)
    gain_feed = norm_feed.astype(f32)


    bits = mem_bits()
    spot = jnp.stack([core, chip] + [mem_index ^ q for q in range(mems)]).astype(jnp.int32)

    def quarters(shard):
        shard = shard.reshape(mems, shard.shape[0] // mems, width)
        return jnp.stack(
            [lax.dynamic_index_in_dim(shard, mem_index ^ k, 0, keepdims=False) for k in range(mems)]
        )

    last = chips - 1
    early = list(range(1, last))

    def matrices(held, other):
        full = assemble(spot, held, other)
        if mems == 4:
            return [full[i].reshape(inner, width) for i in range(4)]
        full = jnp.stack(full).reshape(4, mems // 4, seqs, -1, width).transpose(0, 2, 1, 3, 4)
        return list(full.reshape(4, inner, width))

    def hold_plane(pack, moved):
        return jnp.concatenate([pack[None], jnp.stack(moved, axis=1)], axis=0)

    first_pack = quarters(jnp.concatenate([key_cross.T, value_cross.T, query_self.T, key_self.T], axis=0))
    second_pack = quarters(
        jnp.concatenate([value_self.T, output_self, query_cross.T, output_cross], axis=0)
    )
    gate_own, linear_own, down_own = quarters(gate_feed.T), quarters(linear_feed.T), quarters(down_feed)
    both = [jnp.stack([gate_own[0], linear_own[0]])]
    halved = mems // 2
    down_a, down_b = [down_own[:halved]], [down_own[halved:]]

    onehot = (
        position_buckets(length).reshape(length * length, 1)
        == jnp.arange(buckets, dtype=jnp.int32)[None, :]
    ).astype(bf16)
    position_bias = (
        jnp.dot(onehot, bias_table, preferred_element_type=f32)
        .reshape(length, length, heads)
        .transpose(2, 0, 1)
    )
    row_index = jnp.arange(length, dtype=jnp.int32)
    causal = row_index[:, None] >= row_index[None, :]
    position_bias = jnp.where(causal[None], position_bias, masked_score)
    og_low = output_grad.reshape(rows, width)
    gain_self, gain_cross, gain_feed = [g.reshape(1, width) for g in (gain_self, gain_cross, gain_feed)]
    spots = jnp.stack(
        [(mem_index ^ s) * slots + jnp.arange(slots, dtype=jnp.int32) for s in range(mems)], 0
    )
    len_own = lax.dynamic_index_in_dim(memory_lengths[:, 0], mem_index, 1, keepdims=False)
    place = spot[2:]
    source = memory.reshape(micros, pairs, slots, width).swapaxes(2, 3)
    both_packs = jnp.stack([first_pack[0], second_pack[0]])
    moved = [to_step(both_packs, j) for j in range(1, chips)]
    og_other = rows_to_core(og_low)
    keep_all = lax.all_gather(keep_mask[:, 0], "mem", axis=0)
    moved, both[0], og_other, keep_all = tie(moved, both[0], og_other, keep_all)
    keep_own = lax.dynamic_index_in_dim(keep_all, mem_index, 2, keepdims=False)
    keep_own = jnp.stack(
        [lax.dynamic_index_in_dim(keep_own, mem_index ^ s, 0, keepdims=False) for s in range(mems)], 1
    )
    valid = (spots[None] < len_own[:, None, None]) & ((keep_own == 1) | (spots[None] == 0))
    valid = valid.reshape(micros, 1, mems * slots).astype(f32)


    first_parts, second_parts = fuse(
        lambda *m: [[p[:1] for p in m], [p[1:] for p in m]], *moved
    )
    first_parts, second_parts = first_parts[None], second_parts[None]
    first_order, second_order = [0], [0]
    for first_bit, second_bit in zip(bits, bits[::-1]):
        first_more, second_more = to_mem(first_parts, first_bit), to_mem(second_parts, second_bit)
        first_order = first_order + [k | first_bit for k in first_order]
        second_order = second_order + [k | second_bit for k in second_order]
        if len(both) < last:
            both.append(to_next(both[-1]))
        first_more, second_more, both[-1] = tie(first_more, second_more, both[-1])
        first_parts = jnp.concatenate([first_parts, first_more])
        second_parts = jnp.concatenate([second_parts, second_more])
    while len(both) < last:
        both.append(to_next(both[-1]))

    def hold_parts(pack, parts, order):
        spread = jnp.stack([parts[order.index(k)] for k in range(mems)], axis=1)
        return jnp.concatenate([pack[None], spread], axis=0)

    first_held = hold_parts(first_pack, first_parts, first_order)
    first_more = to_core(first_held)
    gate_early = jnp.stack([both[j][0] for j in early])[None]
    linear_early = jnp.stack([both[j][1] for j in early])[None]
    gate_a1 = to_mem(gate_early, bits[0])
    linear_a1 = to_mem(linear_early, bits[-1])
    both.append(to_next(both[-1]))
    second_held = hold_parts(second_pack, second_parts, second_order)
    first_more, gate_a1, linear_a1, both[last], second_held, down_a[0] = tie(
        first_more, gate_a1, linear_a1, both[last], second_held, down_a[0]
    )

    second_more = to_core(second_held)
    gate_late, linear_late = both[last][:1], both[last][1:]
    gate_late_a1 = to_mem(gate_late, bits[0])
    linear_late_a1 = to_mem(linear_late, bits[-1])
    first_mats = matrices(first_held, first_more)
    kc_full, vc_full, qs_full, ks_full = first_mats
    kv_local = kv_fwd(place, source, kc_full, vc_full)
    gate_early = jnp.concatenate([gate_early, gate_a1])
    linear_early = jnp.concatenate([linear_early, linear_a1])
    down_a.append(to_next(down_a[0]))
    kv_local, second_more, gate_late_a1, linear_late_a1, down_a[1], down_b[0], gate_early, linear_early = tie(
        kv_local, second_more, gate_late_a1, linear_late_a1, down_a[1], down_b[0], gate_early, linear_early
    )

    kvs = [to_mem(kv_local[s], s) if s else kv_local[s] for s in range(mems)]
    down_b.append(to_next(down_b[0]))
    down_a.append(to_next(down_a[1]))
    second_mats = matrices(second_held, second_more)
    vs_full, os_full, qc_full, oc_full = second_mats
    tokens, normed, q, k, v, mixed, first_sum, normed_cross, cq = self_fwd(
        depth, length, inputs.reshape(micros, length, width).swapaxes(1, 2), gain_self, qs_full, ks_full, vs_full, os_full, position_bias, gain_cross, qc_full
    )
    kvs, down_a[2], down_b[1], cq, gate_early, linear_early = tie(
        kvs, down_a[2], down_b[1], cq, gate_early, linear_early
    )

    def spread_rest(held, order, over):
        parts = [held]
        for bit in over:
            parts.append(to_mem(jnp.concatenate(parts) if len(parts) > 1 else parts[0], bit))
            order = order + [k | bit for k in order]
        return parts, order

    def sources(parts, order, n):
        places = {}
        at = 0
        for piece in parts:
            for i in range(piece.shape[0]):
                places[order[at]] = (piece, (i, n) if piece.ndim == 4 else (i,), part)
                at += 1
        return [places[k] for k in range(mems)]

    def whole_source(array, listed):
        if part % 16 == 0:
            return listed
        pieces = []
        for piece, index, _ in listed:
            for i in index:
                piece = piece[i]
            pieces.append(piece)
        return [(jnp.concatenate(pieces), (), feed)]

    natural_order = list(range(mems))
    gate_ord = [k for k in natural_order if not k & bits[-1]]
    linear_ord = [k for k in natural_order if not k & bits[0]]
    whole_bits = mems if mems == 4 and part % 16 == 0 else 0

    def halves(grads):
        if whole_bits:
            return (grads[0:2], grads[2:4], grads[4:-3], *grads[-3:])
        shape = (-1, mems, part, width)
        return (
            fold_parts(grads[0].reshape(shape), natural_order, bits[-1]),
            fold_parts(grads[1].reshape(shape), natural_order, bits[0]),
            grads[2:-3],
            *grads[-3:],
        )

    middle = (len(early) + 1) // 2
    starts = [0, middle] if middle < len(early) else [0]
    cuts = [slice(0, middle), slice(middle, len(early))][: len(starts)]
    gate_cuts, linear_cuts = [gate_early[:, c] for c in cuts], [linear_early[:, c] for c in cuts]
    gate_parts, linear_parts = [None] * len(cuts), [None] * len(cuts)
    gate_parts[0], gate_order = spread_rest(gate_cuts[0], [0, bits[0]], bits[1:])
    linear_parts[0], linear_order = spread_rest(linear_cuts[0], [0, bits[-1]], bits[::-1][1:])
    gate_late = jnp.concatenate([gate_late, gate_late_a1])
    linear_late = jnp.concatenate([linear_late, linear_late_a1])
    down_b.append(to_next(down_b[1]))
    cmixed, second_sum, normed_feed = cross_fwd(depth, length, cq, valid, oc_full, first_sum, gain_feed, kvs)
    gate_parts[0], linear_parts[0], gate_late, linear_late, normed_feed, gate_cuts, linear_cuts, down_b[2] = tie(
        gate_parts[0], linear_parts[0], gate_late, linear_late, normed_feed, gate_cuts, linear_cuts, down_b[2]
    )

    nf_other = rows_to_core(normed_feed)
    for n in range(1, len(cuts)):
        gate_parts[n], gate_order = spread_rest(gate_cuts[n], [0, bits[0]], bits[1:])
        linear_parts[n], linear_order = spread_rest(linear_cuts[n], [0, bits[-1]], bits[::-1][1:])
    own_steps = [[[(g.reshape(feed, width), (), feed)] for g in (gate_own, linear_own, down_own)]]
    grads_o = feed_grad(normed_feed, nf_other, og_low, og_other, own_steps, feed, whole_bits, 1)
    while len(down_b) < last:
        down_a.append(to_next(down_a[-1]))
        down_b.append(to_next(down_b[-1]))
    down_a.append(to_next(down_a[-1]))
    gate_parts, linear_parts, down_a[last], down_b[1:], grads_o, nf_other = tie(
        gate_parts, linear_parts, down_a[last], down_b[1:], grads_o, nf_other
    )

    (gate_keep_o, gate_send_o), (linear_keep_o, linear_send_o), (grad_down_o,), *acts_o = halves(grads_o)
    gate_moved_o = to_mem(gate_send_o, bits[-1])
    linear_moved_o = to_mem(linear_send_o, bits[0])
    early_steps = [
        [
            whole_source(None, sources(gate_parts[c], gate_order, n - starts[c])),
            whole_source(None, sources(linear_parts[c], linear_order, n - starts[c])),
            [(p[j].reshape(feed // 2, width), (), feed // 2) for p in (down_a, down_b)],
        ]
        for n, j in enumerate(early)
        for c in [len([1 for at in starts if at <= n]) - 1]
    ]
    gate_late_parts, gate_order = spread_rest(gate_late, [0, bits[0]], bits[1:])
    linear_late_parts, linear_order = spread_rest(linear_late, [0, bits[-1]], bits[::-1][1:])
    down_b.append(to_next(down_b[-1]))
    grads_a = feed_grad(normed_feed, nf_other, og_low, og_other, early_steps, feed, whole_bits)
    grads_a, gate_late_parts, linear_late_parts, down_b[last], nf_more, gate_moved_o, linear_moved_o = tie(
        grads_a, gate_late_parts, linear_late_parts, down_b[last], nf_other, gate_moved_o, linear_moved_o
    )

    (gate_keep, gate_send), (linear_keep, linear_send), grad_down_a, *acts_a = halves(grads_a)
    grad_down_a = [*grad_down_a, grad_down_o]
    down_total = to_next(grad_down_a[0])
    gate_moved = to_mem(gate_send, bits[-1])
    linear_moved = to_mem(linear_send, bits[0])
    late_steps = [
        [
            whole_source(None, sources(gate_late_parts, gate_order, 0)),
            whole_source(None, sources(linear_late_parts, linear_order, 0)),
            [(p[last].reshape(feed // 2, width), (), feed // 2) for p in (down_a, down_b)],
        ]
    ]
    grads_b = feed_grad(normed_feed, nf_more, og_low, og_other, late_steps, feed, whole_bits)
    (gate_b, gate_bs), (linear_b, linear_bs), (grad_down_b,), *acts_b = halves(grads_b)
    all_steps = early_steps + own_steps + late_steps
    all_acts = [(a, n) for a, count in ((acts_a, len(early)), (acts_o, 1), (acts_b, 1)) for n in range(count)]
    nfg_own, nfg_send = feed_sum(
        rows,
        width,
        [step[:2] for step in all_steps],
        [[[(acts[i], (n,), 2 * rows)] for i in (1, 2)] for acts, n in all_acts],
        feed,
    )
    gate_moved, linear_moved, down_total, nfg_send, gate_bs, linear_bs = tie(
        gate_moved, linear_moved, down_total, nfg_send, gate_bs, linear_bs
    )

    def fold_to_last(held, order, over):
        for bit in over[:-1]:
            kept, moved, order = fold_step(held, order, bit)
            held = add_low(kept, moved)
        return held

    nfg_more = rows_to_core(nfg_send)
    half = mems // 2
    if len(bits) == 2:
        both_y = fuse(
            lambda gk, gm, lk, lm, gko, gmo, lko, lmo: [
                [add_low(gk[:, 0], gm[:, 0]), add_low(gko[:, 0], gmo[:, 0])],
                [add_low(gk[:, 1], gm[:, 1]), add_low(gko[:, 1], gmo[:, 1])],
                [add_low(lk[:, 0], lm[:, 0]), add_low(lko[:, 0], lmo[:, 0])],
                [add_low(lk[:, 1], lm[:, 1]), add_low(lko[:, 1], lmo[:, 1])],
            ],
            gate_keep, gate_moved, linear_keep, linear_moved,
            gate_keep_o, gate_moved_o, linear_keep_o, linear_moved_o,
        )
    else:
        gate_keep, gate_moved, linear_keep, linear_moved = [
            jnp.concatenate(pair)
            for pair in (
                (gate_keep, gate_keep_o),
                (gate_moved, gate_moved_o),
                (linear_keep, linear_keep_o),
                (linear_moved, linear_moved_o),
            )
        ]
        gate_y = fold_to_last(add_low(gate_keep, gate_moved), gate_ord, bits[::-1][1:])
        linear_y = fold_to_last(add_low(linear_keep, linear_moved), linear_ord, bits[1:])
        both_y = [gate_y[:, 0], gate_y[:, 1], linear_y[:, 0], linear_y[:, 1]]
    message_y, message_x = fuse(
        lambda gs, ly, ls, gy: [[gs[0], ly], [ls[0], gy]], gate_bs, both_y[3], linear_bs, both_y[1]
    )
    down_next = after(down_total, message_y, message_x)
    for j in early[1:]:
        down_next = to_next(add_low(down_next, grad_down_a[j - 1]))
    message_y, message_x = to_mem(message_y, bits[-1]), to_mem(message_x, bits[0])
    kvg, (grad_gain_feed, grad_co, grad_cq, first_grad, grad_gain_cross) = cross_bwd(
        depth, length, og_low, nfg_own, nfg_more, second_sum, gain_feed, cmixed, cq, valid, oc_full,
        first_sum, gain_cross, normed_cross, qc_full, kvs,
    )
    message_y, message_x, down_next, kvg, grad_gain_cross, hid_b = tie(
        message_y, message_x, down_next, kvg, grad_gain_cross, acts_b[0]
    )

    kvg = [to_mem(kvg[s], s) if s else kvg[s] for s in range(mems)]
    shards = (mems, part, width)
    own = last - 1
    gate_y, linear_y, both_own, ring = fuse(
        lambda g, x, l, y, d, b: [
            add_low(g[:own], x[half:-1]),
            add_low(l[:own], y[half:-1]),
            [add_low(g[own:], x[-1:]), add_low(l[own:], y[-1:])],
            [add_low(d, b), add_low(g[:1], x[half : half + 1]), add_low(l[:1], y[half : half + 1])],
        ],
        both_y[0], message_x, both_y[2], message_y, down_next.reshape(shards), grad_down_b.reshape(shards),
    )
    ring = to_next(ring)
    hid_acts = [(hid_b if a is acts_b else a[0], n) for a, n in all_acts]
    res_own, res_send = feed_sum(
        rows,
        width,
        [step[2:] for step in all_steps],
        [[[(hid, (n,), 2 * rows)]] for hid, n in hid_acts],
        feed,
    )
    grad_os, grad_qs, grad_ks, grad_vs, input_grad, grad_gain_self, score_sum = self_bwd(
        depth, length, first_grad, mixed, q, k, v, position_bias, os_full, qs_full, ks_full, vs_full,
        normed, tokens, gain_self,
    )
    kvg, ring, grad_qs, res_send = tie(kvg, ring, grad_qs, res_send)

    at = early[-1] - 1
    if len(early) == 2:
        (ring_both,) = fuse(
            lambda r, g, l: [[add_low(r[:1], g[at : at + 1]), add_low(r[1:], l[at : at + 1])]],
            ring[mems:], gate_y, linear_y,
        )
        ring_both = to_next(ring_both)
        grad_qs = after(grad_qs, gate_y)
    kept, sent = core_split(
        spot, [g.reshape(chips, 2, slim, width) for g in (grad_qs, grad_ks, grad_vs, grad_os)]
    )
    sent = to_core(sent)
    for j in early[1:-1]:
        ring_both = to_next(add_low(ring[mems:], jnp.stack([gate_y[j - 1], linear_y[j - 1]])))
        ring = jnp.concatenate([ring[:mems], ring_both])
    gate_b, linear_b = gate_b[0], linear_b[0]
    gate_bm, linear_bm = message_y, message_x
    if len(bits) > 2:
        gate_bm, linear_bm = message_y[:half], message_x[:half]
        gate_b = fold_to_last(add_low(gate_b, gate_bm)[None], gate_ord, bits[::-1][1:])[0]
        linear_b = fold_to_last(add_low(linear_b, linear_bm)[None], linear_ord, bits[1:])[0]
        gate_bm, linear_bm = jnp.zeros_like(gate_b), jnp.zeros_like(linear_b)
    if len(early) != 2:
        ring_both = to_next(add_low(ring[mems:], jnp.stack([gate_y[at], linear_y[at]])))
    parts = fuse(
        lambda r, gb, gm, lb, lm, d: [
            add_low(gb[:1], gm[:1]),
            add_low(lb[:1], lm[:1]),
            [add_low(gb[1:2], gm[1:2]), add_low(r[1:2], d[1:2])],
            [add_low(lb[1:2], lm[1:2]), add_low(r[half : half + 1], d[half : half + 1])],
            add_low(r[:1], d[:1]),
            *[add_low(r[k : k + 1], d[k : k + 1]) for k in range(1, mems) if k not in (1, half)],
        ],
        ring[:mems], gate_b, gate_bm, linear_b, linear_bm, grad_down_a[last - 1].reshape(shards),
        limit=60,
    )
    gate_bk, linear_bk, message_x, message_y, down_mine, *down_rest = parts
    others = [k for k in range(1, mems) if k not in (1, half)]
    message_x, message_y = to_mem(message_x, bits[0]), to_mem(message_y, bits[-1])
    down_rest = [to_mem(p, k) for p, k in zip(down_rest, others)]

    def grad_sums(*grads):
        stacked = jnp.stack([g.reshape(seqs, slim, width) for g in grads], axis=1)
        return lax.psum_scatter(stacked.reshape(seqs, len(grads) * slim, width), "seq", scatter_dimension=0)

    cross_first = grad_sums(after(grad_cq, ring), grad_co)
    grad_kc, grad_vc = kv_weights(place, source, kvg, inner)
    sent, ring_both, message_x, message_y, down_rest, grad_kc, kvg[0] = tie(
        sent, ring_both, message_x, message_y, down_rest, grad_kc, kvg[0]
    )

    columns = columns_of(spot, kept, sent, mems)
    columns = [to_mem(p, s) if s else p for s, p in enumerate(columns)]
    ring_both, down_sum = fuse(
        lambda r, g, x, l, y, d, *more: [
            [add_low(r[:1], add_low(g, x[:1])), add_low(r[1:], add_low(l, y[:1]))],
            sum_low([d, x[1:], y[1:], *more]),
        ],
        ring_both, gate_bk, message_x, linear_bk, message_y, down_mine, *down_rest,
    )
    ring_both = to_next(ring_both)
    cross_sum = [grad_sums(grad_kc, grad_vc), cross_first]
    memory_grad = kv_memory(place, source.shape, kc_full, vc_full, kvg)
    score_sum, input_grad = [after(x, columns[1]) for x in (score_sum, input_grad)]
    grad_table = lax.dot_general(
        onehot.astype(f32),
        score_sum.reshape(heads, length * length),
        (((0,), (1,)), ((), ())),
        preferred_element_type=f32,
    )
    table_row = jnp.pad(grad_table.reshape(1, buckets * heads), ((0, 0), (0, width - buckets * heads)))
    small = jnp.concatenate([grad_gain_self, grad_gain_cross, grad_gain_feed, table_row], axis=0)

    def to_rows(value):
        high = value.astype(bf16)
        rest = (value - high.astype(f32)).astype(bf16)
        return jnp.concatenate([high, rest, jnp.zeros((16 - 2 * value.shape[0], width), bf16)])

    def from_rows(value):
        return value[:4].astype(f32) + value[4:8].astype(f32)

    small_rows = to_rows(small)
    columns, ring_both, small_rows, memory_grad = tie(columns, ring_both, small_rows, memory_grad)

    share = 4 * slim // mems
    total = sum_low(columns).reshape(chips, share, width)
    pieces = [
        jnp.concatenate([lax.dynamic_index_in_dim(total, (chip + j) % chips, 0, keepdims=False), small_rows])
        for j in range(chips)
    ]
    pieces = [to_step(p, j) if j else p for j, p in enumerate(pieces)]
    both_sum, message_x, message_y = fuse(
        lambda r, g, d: [add_low(r, g), [add_low(r[:1], g[:1]), d], [add_low(r[1:], g[1:]), d]],
        ring_both, both_own, down_sum,
    )
    message_x, message_y = to_mem(message_x, bits[0]), to_mem(message_y, bits[-1])
    down_rest = [to_mem(down_sum, k) for k in range(1, mems) if k not in (1, half)]
    pieces, message_x, message_y, down_rest, cross_sum, res_send = tie(
        pieces, message_x, message_y, down_rest, cross_sum, res_send
    )

    down_g = [down_sum if k == 0 else message_x[1:] if k == 1 else message_y[1:] if k == half else None for k in range(mems)]
    for k in range(mems):
        if down_g[k] is None:
            down_g[k] = down_rest.pop(0)
    down_g = [p[0] for p in down_g]
    self_mine = sum_low([p[:share] for p in pieces])
    small = jnp.stack([from_rows(p[share:]) for p in pieces])
    small = tree_sum(
        [lax.dynamic_index_in_dim(small, (chip - z) % chips, 0, keepdims=False) for z in range(chips)]
    )
    gate_g, gate_order = [both_sum[:1], message_x[:1]], [0, bits[0]]
    linear_g, linear_order = [both_sum[1:], message_y[:1]], [0, bits[-1]]
    gate_g, gate_order = spread_rest(jnp.concatenate(gate_g), gate_order, bits[1:-1])
    linear_g, linear_order = spread_rest(jnp.concatenate(linear_g), linear_order, bits[::-1][1:-1])
    gate_g, linear_g = joined(gate_g), joined(linear_g)
    small_rows = to_rows(small)
    cut = gate_g.shape[0] * part
    cross_parts = list(quarters(jnp.concatenate(cross_sum)))
    messages = fuse(
        lambda g, l, rows_, *ps: [
            [*([l] if k == 1 else [g] if k == half else []), p, rows_] for k, p in enumerate(ps)
        ],
        gate_g.reshape(cut, width), linear_g.reshape(cut, width), small_rows, *cross_parts,
    )
    cross_parts[0] = messages[0]
    moved = {k: to_mem(p, k) for k, p in enumerate(messages) if k}
    res_more = rows_to_core(res_send)
    result = (second_sum + res_own + res_more.astype(f32)).reshape(micros, length, width).swapaxes(1, 2)
    moved, small_rows, self_mine, cross_own, result = tie(
        moved, small_rows, self_mine, cross_parts[0], result
    )
    result = result.swapaxes(1, 2)
    linear_g = jnp.concatenate([linear_g, moved[1][:cut].reshape(-1, part, width)])
    gate_g = jnp.concatenate([gate_g, moved[half][:cut].reshape(-1, part, width)])
    gate_order = gate_order + [k | half for k in gate_order]
    linear_order = linear_order + [k | 1 for k in linear_order]
    cross_parts = [cross_own] + [moved[k][cut:] if k in (1, half) else moved[k] for k in range(1, mems)]
    small = tree_sum([from_rows(p[share:]) for p in cross_parts])

    mine = jnp.concatenate([self_mine, sum_low([p[:share] for p in cross_parts])])
    mine_g = [mine] + [to_mem(mine, k) for k in range(1, mems)]
    small = small + to_core(small)

    def settle(flat, order):
        return natural([flat[order.index(k)] for k in range(mems)], mem_index).astype(f32)

    gate_out = settle(gate_g, gate_order).reshape(feed, width)
    linear_out = settle(linear_g, linear_order).reshape(feed, width)
    down_out = natural(down_g, mem_index).astype(f32).reshape(feed, width)
    mine_g, gate_out, linear_out, down_out = tie(mine_g, gate_out, linear_out, down_out)

    def settled(start, rows_of):
        return natural([p[start : start + rows_of] for p in mine_g], mem_index).astype(f32)

    self_sum = settled(0, share).reshape(4, slim, width)
    cross_sum = settled(share, share).reshape(4, slim, width)
    return (
        result.reshape(inputs.shape),
        input_grad.reshape(inputs.shape),
        memory_grad.swapaxes(2, 3).reshape(memory.shape),
        small[0],
        self_sum[0].T,
        self_sum[1].T,
        self_sum[2].T,
        self_sum[3],
        small[3, : buckets * heads].reshape(buckets, heads),
        small[1],
        cross_sum[2].T,
        cross_sum[0].T,
        cross_sum[1].T,
        cross_sum[3],
        small[2],
        gate_out.T,
        linear_out.T,
        down_out,
    )


def solution(mesh):
    tokens_at = P(None, "seq", "mem", None, None)
    memory_at = P(None, "seq", None, "mem", None)
    columns, row_cut = P(None, "seq"), P("seq", None)
    return jax.shard_map(
        per_device,
        mesh=mesh,
        in_specs=(
            tokens_at,
            memory_at,
            P(None, "seq", None),
            P(None, "seq", None, "mem"),
            P(),
            columns,
            columns,
            columns,
            row_cut,
            P(),
            P(),
            columns,
            columns,
            columns,
            row_cut,
            P(),
            columns,
            columns,
            row_cut,
            tokens_at,
        ),
        out_specs=(
            tokens_at,
            tokens_at,
            memory_at,
            P(),
            columns,
            columns,
            columns,
            row_cut,
            P(),
            P(),
            columns,
            columns,
            columns,
            row_cut,
            P(),
            columns,
            columns,
            row_cut,
        ),
        check_vma=False,
    )
```
